128 devices in a mesh: fsdp: 8 (over z, core), expert: 16 (over y, x).
Axes of the slice: x: 4, y: 4, z: 4, core: 2. Of those that a mesh axis runs over, the one named last changes fastest.
Arguments:
- layer_input: bfloat16 [16, 1024, 2048], P('expert', 'fsdp'), may hold values from -6 to 6
- routes: int32 [16, 1024, 8], P('expert', 'fsdp'), may hold values from 0 to 31, all different within a row; in each aligned block of 128 rows (0 to 127, 128 to 255, ..., all dimensions but the last counted through in order) at most 40 rows name the same one
- cotangent: bfloat16 [16, 1024, 2048], P('expert', 'fsdp'), may hold values from -6 to 6
- attn_gain: float32 [2048], replicated, may hold values from 0.5 to 1.5
- query_gain: float32 [128], replicated, may hold values from 0.1 to 1.9
- key_gain: float32 [128], replicated, may hold values from 0.1 to 1.9
- mlp_gain: float32 [2048], replicated, may hold values from 0.5 to 1.5
- w_query: bfloat16 [2048, 4096], P('fsdp'), may hold values from -0.125 to 0.125
- key_weight: bfloat16 [2048, 512], P('fsdp'), may hold values from -0.125 to 0.125
- value_weight: bfloat16 [2048, 512], P('fsdp'), may hold values from -0.125 to 0.125
- w_out: bfloat16 [4096, 2048], P('fsdp'), may hold values from -0.75 to 0.75
- w_router: bfloat16 [2048, 32], P('fsdp'), may hold values from -0.0625 to 0.0625
- w_gate: bfloat16 [32, 2048, 768], P('expert', 'fsdp'), may hold values from -0.125 to 0.125
- w_up: bfloat16 [32, 2048, 768], P('expert', 'fsdp'), may hold values from -0.125 to 0.125
- w_down: bfloat16 [32, 768, 2048], P('expert', 'fsdp'), may hold values from -0.875 to 0.875
Outputs:
- output: bfloat16 [16, 1024, 2048], P('expert', 'fsdp')
- grad_input: bfloat16 [16, 1024, 2048], P('expert', 'fsdp')
- grad_attn_gain: float32 [2048], replicated
- grad_query_gain: float32 [128], replicated
- grad_key_gain: float32 [128], replicated
- grad_mlp_gain: float32 [2048], replicated
- grad_w_query: float32 [2048, 4096], P('fsdp')
- grad_w_key: float32 [2048, 512], P('fsdp')
- grad_w_value: float32 [2048, 512], P('fsdp')
- grad_w_out: float32 [4096, 2048], P('fsdp')
- grad_w_router: float32 [2048, 32], P('fsdp')
- grad_w_gate: float32 [32, 2048, 768], P('expert', 'fsdp')
- grad_w_up: float32 [32, 2048, 768], P('expert', 'fsdp')
- grad_w_down: float32 [32, 768, 2048], P('expert', 'fsdp')
The draws below stay inside these ranges and needn't reach their ends.
Inputs may be any that keep to these rules, and one draw needn't show every extreme that they name: `routes`: each token names 8 different experts. Among the rows of one device no expert is named more than 40 times, and in some device's rows an expert is named exactly 40 times.
All inputs are finite; a program needn't handle non-finite values.
Results may differ from the reference program's by a relative error of at most 0.025.
Values may be sent and summed in bfloat16 or wider, within the bound.
No kernel may reach another device: no remote copies, remote signals or barrier semaphores. Data moves between devices by JAX's collectives and lax.ppermute only.
A program may use at most 256 MiB of HBM per device.

```python
import math
import jax
import jax.numpy as jnp
import numpy as np
from jax import lax

MODEL_WIDTH = 2048
QUERY_HEADS = 32
KEY_VALUE_HEADS = 4
HEAD_SIZE = 128
FF = 768
TOPK = 8
EXPERTS = 32
SEQ_LEN = 1024
TOK_DEV = 128
SEQS = 16
CAP = 40
N_FSDP = 8


def block_scale(own_key, extent, pieces, low, largest):
    level = 1.0
    for position, shards_of in pieces:
        draws = jax.random.uniform(jax.random.fold_in(jax.random.fold_in(own_key, 6), position), (shards_of,), jnp.float32, low / len(pieces), largest / len(pieces))
        level = level * jnp.repeat(jnp.exp(draws), extent[position] // shards_of).reshape((-1,) + (1,) * (len(extent) - 1 - position))
    return level


def deal_out(own_key, own, number, rows, amount, top, reach, slope):
    ranking = jax.random.permutation(own_key, amount)
    packed, usual = portions_of(amount, rows * top, reach, slope, True), portions_of(amount, rows * top, reach, slope, False)
    places = jnp.arange(amount)

    def named(tallies, turn):
        used = int((tallies > 0).sum())
        fixed = max(1, used // 4)
        passed = fixed + (places - fixed + turn * (used - fixed)) % max(1, amount - fixed)
        return jnp.zeros((amount,), jnp.int32).at[ranking[jnp.where(places < fixed, places, passed)]].set(jnp.asarray(tallies, jnp.int32))

    tallies = jnp.where(number % 4 == 0, named(packed, number // 4), named(usual, number - number // 4 - 1))
    mixed = jax.random.permutation(jax.random.fold_in(own, 3), amount)
    source_of, receiver = mixed[0:amount // 2 * 2:2], mixed[1:amount // 2 * 2:2]
    slack = jnp.minimum(tallies[source_of] - 1, reach - tallies[receiver]) // 2
    slack = jnp.where((source_of == ranking[0]) | (receiver == ranking[0]) | (tallies[receiver] == 0), 0, jnp.maximum(slack, 0))
    passed = jax.random.randint(jax.random.fold_in(own, 4), (amount // 2,), 0, 1 << 20) % (slack + 1)
    tallies = tallies.at[source_of].add(-passed).at[receiver].add(passed)
    labels = jnp.searchsorted(jnp.cumsum(tallies), jnp.arange(rows * top), side="right").astype(jnp.int32)
    table = labels.reshape(top, rows).T
    table = table[jax.random.permutation(jax.random.fold_in(own, 1), rows)]
    turn = jax.random.randint(jax.random.fold_in(own, 2), (rows, 1), 0, top)
    return jnp.take_along_axis(table, (jnp.arange(top)[None, :] + turn) % top, axis=1)


def portions_of(count, total, limit, skew, full):
    portions = [(1 << 20) // math.isqrt(rank ** skew) + 1 for rank in range(1, count + 1)]
    largest = limit if full else min(limit, max(-(-total // count), total * portions[0] // sum(portions)))
    least = 1 if total - largest >= count - 1 else 0
    holding, surplus = [largest] + [least] * (count - 1), total - largest - least * (count - 1)
    while surplus > 0:
        movable = [i for i in range(1, count) if holding[i] < largest] or [i for i in range(1, count) if holding[i] < limit]
        whole, budget = sum([portions[i] for i in movable]), surplus
        for i in movable:
            more = min(limit - holding[i], max(1, budget * portions[i] // whole), surplus)
            holding[i] = holding[i] + more
            surplus = surplus - more
    return np.array(holding)


def normal_values(own_key, dims, scale, bound, pieces=(), held_as=jnp.bfloat16):
    level = block_scale(own_key, dims, pieces, -0.22, 0.18) if pieces else 1.0
    values = jax.random.normal(own_key, dims, jnp.float32) * scale * level
    return jnp.minimum(jnp.maximum(values, -bound), bound).astype(held_as)


def setup_inputs(seed: int = 0) -> dict:
    splits = jax.random.split(jax.random.key(seed), 16)
    layer_input = normal_values(splits[0], (SEQS, SEQ_LEN, MODEL_WIDTH), 1.0, 6.0, ((0, 16), (1, 8)))
    routes_keys = jax.random.split(jax.random.fold_in(splits[1], 1), SEQS * SEQ_LEN // TOK_DEV)
    routes_turns = jax.random.permutation(jax.random.fold_in(splits[1], 3), SEQS * SEQ_LEN // TOK_DEV)
    routes = jax.vmap(lambda own, number: deal_out(jax.random.fold_in(splits[1], 2), own, number, TOK_DEV, EXPERTS, TOPK, CAP, 2))(routes_keys, routes_turns).reshape((SEQS, SEQ_LEN, TOPK))
    cotangent = normal_values(splits[2], (SEQS, SEQ_LEN, MODEL_WIDTH), 1.0, 6.0, ((0, 16), (1, 8)))
    attn_gain = jnp.clip(1.0 + 0.1 * jax.random.normal(splits[3], (MODEL_WIDTH,), jnp.float32), 0.5, 1.5)
    query_gain = jnp.clip(1.0 + 0.18 * jax.random.normal(splits[4], (HEAD_SIZE,), jnp.float32), 0.1, 1.9)
    key_gain = jnp.clip(1.0 + 0.18 * jax.random.normal(splits[5], (HEAD_SIZE,), jnp.float32), 0.1, 1.9)
    mlp_gain = jnp.clip(1.0 + 0.1 * jax.random.normal(splits[6], (MODEL_WIDTH,), jnp.float32), 0.5, 1.5)
    w_query = normal_values(splits[7], (MODEL_WIDTH, QUERY_HEADS * HEAD_SIZE), MODEL_WIDTH ** -0.5, 0.125, ((0, 8),))
    key_weight = normal_values(splits[8], (MODEL_WIDTH, KEY_VALUE_HEADS * HEAD_SIZE), MODEL_WIDTH ** -0.5, 0.125, ((0, 8),))
    value_weight = normal_values(splits[9], (MODEL_WIDTH, KEY_VALUE_HEADS * HEAD_SIZE), MODEL_WIDTH ** -0.5, 0.125, ((0, 8),))
    w_out = normal_values(splits[10], (QUERY_HEADS * HEAD_SIZE, MODEL_WIDTH), (QUERY_HEADS * HEAD_SIZE // 64) ** -0.5, 0.75, ((0, 8),))
    w_router = normal_values(splits[11], (MODEL_WIDTH, EXPERTS), (4 * MODEL_WIDTH) ** -0.5, 0.0625, ((0, 8),))
    w_gate = normal_values(splits[12], (EXPERTS, MODEL_WIDTH, FF), MODEL_WIDTH ** -0.5, 0.125, ((0, 16), (1, 8)))
    w_up = normal_values(splits[13], (EXPERTS, MODEL_WIDTH, FF), MODEL_WIDTH ** -0.5, 0.125, ((0, 16), (1, 8)))
    w_down = normal_values(splits[14], (EXPERTS, FF, MODEL_WIDTH), (FF // 16) ** -0.5, 0.875, ((0, 16), (1, 8)))
    return dict(layer_input=layer_input, routes=routes, cotangent=cotangent, attn_gain=attn_gain, query_gain=query_gain, key_gain=key_gain, mlp_gain=mlp_gain, w_query=w_query, key_weight=key_weight, value_weight=value_weight, w_out=w_out, w_router=w_router, w_gate=w_gate, w_up=w_up, w_down=w_down)


@jax.custom_vjp
def reduced_precision(v):
    return lax.optimization_barrier(v.astype(jnp.bfloat16)).astype(jnp.float32)

@jax.custom_vjp
def reduced_backward(v):
    return v

def low_keep(v):
    return (reduced_precision(v), None)

def low_pass(kept, grad):
    return (grad,)

def back_keep(v):
    return (v, None)

def back_low(kept, grad):
    return (reduced_precision(grad),)
reduced_precision.defvjp(low_keep, low_pass)
reduced_backward.defvjp(back_keep, back_low)
epsilon = 1e-06
rope_base = 1000000.0
highest_precision = lax.Precision.HIGHEST

def inv_rms(values):
    return lax.rsqrt(lax.optimization_barrier(jnp.mean(values * values, axis=-1, keepdims=True)) + epsilon)

def rotate(values, cosine, sine_table):
    middle = values.shape[-1] // 2
    turned = jnp.concatenate([-values[..., middle:], values[..., :middle]], axis=-1)
    return values * cosine + turned * sine_table

def layer_forward(params, inputs, route_ids, cosine, sine_table):
    attn_gain, query_gain, key_gain, mlp_gain, w_query, key_weight, value_weight, w_out, w_router, w_gate, w_up, w_down = params
    sequence_length = inputs.shape[0]
    first_hidden = reduced_precision(inputs * inv_rms(inputs) * attn_gain)
    query_raw = reduced_backward(jnp.dot(first_hidden, w_query, precision=highest_precision)).reshape(sequence_length, QUERY_HEADS, HEAD_SIZE)
    key_unrotated = reduced_backward(jnp.dot(first_hidden, key_weight, precision=highest_precision)).reshape(sequence_length, KEY_VALUE_HEADS, HEAD_SIZE)
    value_reduced = reduced_precision(reduced_backward(jnp.dot(first_hidden, value_weight, precision=highest_precision))).reshape(sequence_length, KEY_VALUE_HEADS, HEAD_SIZE)
    query_reduced = reduced_precision(reduced_backward(rotate(query_raw * inv_rms(query_raw) * query_gain, cosine, sine_table)))
    key_reduced = reduced_precision(reduced_backward(rotate(key_unrotated * inv_rms(key_unrotated) * key_gain, cosine, sine_table)))
    query_grouped = query_reduced.reshape(sequence_length, KEY_VALUE_HEADS, QUERY_HEADS // KEY_VALUE_HEADS, HEAD_SIZE)
    attention_scores = reduced_backward(jnp.einsum('nvum,wvm->vunw', query_grouped, key_reduced, precision=highest_precision) * HEAD_SIZE ** (-0.5))
    places = jnp.arange(sequence_length)
    causal = places[:, None] >= places[None, :]
    attention_scores = jnp.where(causal, attention_scores, -1e+30)
    attention_probs = reduced_precision(jax.nn.softmax(attention_scores, axis=-1))
    attention_output = jnp.einsum('zjbi,izn->bzjn', attention_probs, value_reduced, precision=highest_precision).reshape(sequence_length, QUERY_HEADS * HEAD_SIZE)
    attention_output = reduced_precision(reduced_backward(attention_output))
    resid_two = inputs + reduced_backward(jnp.dot(attention_output, w_out, precision=highest_precision))
    hidden_two = reduced_precision(resid_two * inv_rms(resid_two) * mlp_gain)
    logits = reduced_backward(jnp.dot(hidden_two, w_router, precision=highest_precision))
    expert_ids = jnp.arange(EXPERTS).astype(jnp.int32)
    picked_table = (route_ids[:, :, None] == expert_ids[None, None, :]).astype(jnp.float32)
    chosen = lax.optimization_barrier(jnp.sum(picked_table * logits[:, None, :], axis=-1))
    gate_probs = jax.nn.softmax(chosen, axis=-1)
    flat_ids = route_ids.reshape(-1).astype(jnp.int32)
    member = (flat_ids[:, None] == expert_ids[None, :]).astype(jnp.int32)
    rank_within = lax.optimization_barrier(jnp.sum((jnp.cumsum(member, axis=0) - 1) * member, axis=1)).astype(jnp.int32)
    slot_room = N_FSDP * CAP
    slot_index = flat_ids * slot_room + rank_within
    count_slots = EXPERTS * slot_room
    source_row = jnp.zeros((count_slots,), jnp.int32).at[slot_index].set((jnp.arange(flat_ids.shape[0]) // TOPK).astype(jnp.int32))
    occupied = jnp.zeros((count_slots, 1), jnp.float32).at[slot_index].set(1.0)
    arrived = reduced_backward(hidden_two[source_row] * occupied).reshape(EXPERTS, slot_room, MODEL_WIDTH)
    gate_pre = reduced_backward(jnp.einsum('ecd,edf->ecf', arrived, w_gate, precision=highest_precision))
    up_pre = reduced_backward(jnp.einsum('ecd,edf->ecf', arrived, w_up, precision=highest_precision))
    inner_act = reduced_precision(jax.nn.silu(gate_pre) * up_pre)
    expert_out = reduced_precision(reduced_backward(jnp.einsum('ecf,efd->ecd', inner_act, w_down, precision=highest_precision))).reshape(count_slots, MODEL_WIDTH)
    route_out = expert_out[slot_index].reshape(sequence_length, TOPK, MODEL_WIDTH)
    return resid_two + lax.optimization_barrier(jnp.sum(gate_probs[:, :, None] * route_out, axis=1))

def reference(layer_input, routes, cotangent, attn_gain, query_gain, key_gain, mlp_gain, w_query, key_weight, value_weight, w_out, w_router, w_gate, w_up, w_down):
    params = tuple((argument.astype(jnp.float32) for argument in (attn_gain, query_gain, key_gain, mlp_gain, w_query, key_weight, value_weight, w_out, w_router, w_gate, w_up, w_down)))
    positions = jnp.arange(SEQ_LEN).astype(jnp.float32)
    frequency = rope_base ** (-(jnp.arange(HEAD_SIZE // 2).astype(jnp.float32) * 2.0 / HEAD_SIZE))
    frequency = jnp.concatenate([frequency, frequency])
    angles = positions[:, None] * frequency[None, :]
    cosine = jnp.cos(angles)[:, None, :]
    sine_table = jnp.sin(angles)[:, None, :]

    def per_sequence(totals, inputs):
        seq_input, seq_routes, seq_cotangent = inputs

        def forward(weights, values):
            return layer_forward(weights, values, seq_routes, cosine, sine_table)
        result, pullback = jax.vjp(forward, params, seq_input.astype(jnp.float32))
        grad_params, grad_values = pullback(seq_cotangent.astype(jnp.float32))
        totals = jax.tree.map(jnp.add, totals, grad_params)
        return (totals, (result.astype(jnp.bfloat16), grad_values.astype(jnp.bfloat16)))
    start_totals = jax.tree.map(jnp.zeros_like, params)
    totals, (output, grad_input) = lax.scan(per_sequence, start_totals, (layer_input, routes, cotangent))
    return (output, grad_input, totals[0], totals[1], totals[2], totals[3], totals[4], totals[5], totals[6], totals[7], totals[8], totals[9], totals[10], totals[11])
```

```python
import functools

import jax
import jax.numpy as jnp
from jax import lax
from jax.experimental import pallas as pl
from jax.experimental.pallas import tpu as pltpu
from jax.sharding import Mesh
from jax.sharding import PartitionSpec as P

MODEL_WIDTH = 2048
QUERY_HEADS = 32
KEY_VALUE_HEADS = 4
HEAD_SIZE = 128
TOPK = 8
EXPERTS = 32
CAP = 40
Z, C, Y, X = "z", "c", "y", "x"
FSDP = (Z, C)
EXPERT = (Y, X)
ALL = (Z, C, Y, X)

bf16 = jnp.bfloat16
f32 = jnp.float32
epsilon = 1e-06
rope_base = 1000000.0


def dot(a, b):
    return jnp.dot(a, b, preferred_element_type=f32)


def es(spec, a, b):
    return jnp.einsum(spec, a, b, preferred_element_type=f32)


def shift(v, axis, by):
    n = 2 if axis == C else 4
    return lax.ppermute(v, axis, [(i, (i + by) % n) for i in range(n)])


def gather_fsdp(p):
    half = p.shape[0] // 2
    up, down, other = shift(p, Z, -1), shift(p, Z, 1), shift(p, C, 1)
    far_low, far_high = shift(down[:half], Z, 1), shift(up[half:], Z, -1)
    far = [(up, 1, 0), (down, 3, 0), (far_low, 2, 0), (far_high, 2, half)]
    return (
        [(p, 0, 0, 0), (other, 0, 1, 0)]
        + [(a, dz, 0, r) for a, dz, r in far]
        + [(shift(a, C, 1), dz, 1, r) for a, dz, r in far]
    )


def scatter_fsdp(keep, send):
    got = shift(send, C, 1)
    half = keep.shape[1] // 2

    def both(d, rows=slice(None)):
        return (keep[d, rows].astype(f32) + got[d, rows].astype(f32)).astype(bf16)

    low, high = slice(None, half), slice(half, None)
    far_low, far_high = both(2, low), both(2, high)
    from_down, from_up = shift(far_low, Z, 1), shift(far_high, Z, -1)
    one, three = both(1), both(3)
    one = jnp.concatenate([(one[low].astype(f32) + from_down.astype(f32)).astype(bf16), one[high]])
    three = jnp.concatenate([three[low], (three[high].astype(f32) + from_up.astype(f32)).astype(bf16)])
    from_down, from_up = shift(one, Z, 1), shift(three, Z, -1)
    own = keep[0].astype(f32) + got[0].astype(f32)
    return own + from_down.astype(f32) + from_up.astype(f32)


def gather_ring(v, axis):
    half = v.shape[0] // 2
    up, down = shift(v, axis, -1), shift(v, axis, 1)
    return v, up, shift(down[:half], axis, 1), shift(up[half:], axis, -1), down


def gather_plane(left, right):
    def stacked(parts):
        a, b, low, high, d = parts
        return jnp.stack([a, b, jnp.concatenate([low, high]), d])

    left, right = gather_ring(left, X), gather_ring(right, Y)
    return gather_ring(stacked(left), Y), gather_ring(stacked(right), X)


def scatter_ring(parts, axis):
    own, one, low, high, three = parts
    k = low.shape[0]
    down, up = shift(low, axis, 1), shift(high, axis, -1)

    def plus(a, b):
        return (a.astype(f32) + b.astype(f32)).astype(bf16)

    one = jnp.concatenate([plus(one[:k], down), one[k:]])
    three = jnp.concatenate([three[:k], plus(three[k:], up)])
    down, up = shift(one, axis, 1), shift(three, axis, -1)
    return own.astype(f32) + down.astype(f32) + up.astype(f32)


def scatter_plane(left, right):
    def halves(v):
        v = v.astype(bf16)
        k = v.shape[1] // 2
        return v[0], v[1], v[2, :k], v[2, k:], v[3]

    left = scatter_ring(halves(scatter_ring(left, Y)), X)
    right = scatter_ring(halves(scatter_ring(right, X)), Y)
    return left, right


def sum_all(v):
    v = v + shift(v, C, 1)
    for axis in (Z, Y, X):
        v = (v + shift(v, axis, 1)) + (shift(v, axis, 2) + shift(v, axis, 3))
    return v


def inv_rms(values):
    return lax.rsqrt(jnp.mean(values * values, axis=-1, keepdims=True) + epsilon)


def norm_back(grad_norm, normed, scale_part):
    return scale_part * (grad_norm - normed * jnp.mean(grad_norm * normed, axis=-1, keepdims=True))


def turned(values):
    middle = values.shape[-1] // 2
    return jnp.concatenate([-values[..., middle:], values[..., :middle]], axis=-1)


def turned_back(values):
    middle = values.shape[-1] // 2
    return jnp.concatenate([values[..., middle:], -values[..., :middle]], axis=-1)


def rope_tables(positions):
    frequency = rope_base ** (-(jnp.arange(HEAD_SIZE // 2).astype(f32) * 2.0 / HEAD_SIZE))
    frequency = jnp.concatenate([frequency, frequency])
    angles = positions[:, None] * frequency[None, :]
    return jnp.cos(angles), jnp.sin(angles)


def mm(a, b, dims=((1,), (0,))):
    return lax.dot_general(a, b, (dims, ((), ())), preferred_element_type=f32)


NT = ((1,), (1,))
TN = ((0,), (0,))
ANY = pl.BlockSpec(memory_space=pl.ANY)
VM = pl.BlockSpec(memory_space=pltpu.VMEM)
SM = pl.BlockSpec(memory_space=pltpu.SMEM)
MIB = 1 << 20


def part_of(outer, inner):
    return {0: (0, inner), 1: (1, inner), 2: (2 + inner // 2, inner % 2), 3: (4, inner)}[outer]


def load_pieces(place, spec, pieces, whole, sems):
    copies = []
    for k, (dz, dc, first, rows) in enumerate(spec):
        at = lax.rem(place[0] + dz, 4) * 256 + lax.rem(place[1] + dc, 2) * 128 + first
        at = pl.multiple_of(at, 64)
        copies.append(pltpu.make_async_copy(pieces[k], whole.at[pl.ds(at, rows)], sems.at[k]))
    for copy in copies:
        copy.start()
    return copies


def attention_kernel(spec, place, w_own, w_other, w_out, q_gain, k_gain, cosine, sine, *rest):
    n = len(spec)
    pieces, rest = rest[:n], rest[n:]
    h1, q_raw, k_raw, v_b, q_b, k_b, a_b, lse, keep, send, sems = rest
    z, c = place[0], place[1]
    for copy in load_pieces(place, spec, pieces, h1, sems):
        copy.wait()

    @pl.loop(0, 4)
    def _(i):
        rows = pl.ds(pl.multiple_of(i * 256, 256), 256)
        t = mm(h1[rows], w_own[...])
        other = mm(h1[rows], w_other[...])
        key = jnp.where(c == 0, t[:, 512:], other)
        q_raw[rows] = t[:, :512]
        k_raw[rows] = key
        v_b[rows] = jnp.where(c == 0, other, t[:, 512:]).astype(bf16)
        co, si = cosine[rows], sine[rows]

        def rotated(u, gain):
            u = u * lax.rsqrt(jnp.mean(u * u, axis=-1, keepdims=True) + epsilon) * gain
            return (u * co + pltpu.roll(u, 64, 1) * si).astype(bf16)

        for h in range(4):
            q_b[h, rows] = rotated(t[:, 128 * h : 128 * h + 128], q_gain[...])
        k_b[rows] = rotated(key, k_gain[...])

    lane = lax.broadcasted_iota(jnp.int32, (256, 128), 1)
    below = lax.broadcasted_iota(jnp.int32, (256, 256), 0) >= lax.broadcasted_iota(
        jnp.int32, (256, 256), 1
    )
    for i in range(4):
        n_keys = 256 * (i + 1)
        rows = slice(256 * i, n_keys)
        logs = jnp.zeros((256, 128), f32)
        for h in range(4):
            s = mm(q_b[h, rows], k_b[:n_keys], NT) * (HEAD_SIZE**-0.5)
            e = jnp.exp(s)
            tail = jnp.where(below, e[:, n_keys - 256 :], 0.0)
            e = tail if i == 0 else jnp.concatenate([e[:, : n_keys - 256], tail], axis=1)
            total = jnp.sum(e, axis=1, keepdims=True)
            a = mm(e.astype(bf16), v_b[:n_keys]) / total
            a_b[rows, 128 * h : 128 * h + 128] = a.astype(bf16)
            logs = jnp.where(lane == h, jnp.log(total), logs)
        lse[rows] = logs
        part = mm(a_b[rows], w_out[...]).astype(bf16)
        dz = lax.rem(i - z + 4, 4)
        first, second = part[:128], part[128:]
        keep[dz] = jnp.where(c == 0, first, second)
        send[dz] = jnp.where(c == 0, second, first)


def attention_forward(pieces, place, w_own, w_other, w_out, q_gain, k_gain, cosine, sine):
    spec = [(dz, dc, first, a.shape[0]) for a, dz, dc, first in pieces]
    seq = 1024
    shapes = [
        ((seq, MODEL_WIDTH), bf16),
        ((seq, 512), f32),
        ((seq, 128), f32),
        ((seq, 128), bf16),
        ((4, seq, 128), bf16),
        ((seq, 128), bf16),
        ((seq, 512), bf16),
        ((seq, 128), f32),
        ((4, 128, MODEL_WIDTH), bf16),
        ((4, 128, MODEL_WIDTH), bf16),
    ]
    return pl.pallas_call(
        functools.partial(attention_kernel, spec),
        out_shape=[jax.ShapeDtypeStruct(*s) for s in shapes],
        in_specs=[SM] + [VM] * 7 + [ANY] * len(spec),
        out_specs=[VM] * len(shapes),
        scratch_shapes=[pltpu.SemaphoreType.DMA((len(spec),))],
        compiler_params=pltpu.CompilerParams(vmem_limit_bytes=56 * MIB),
        cost_estimate=pl.CostEstimate(flops=9 << 30, bytes_accessed=28 << 20, transcendentals=3 << 20),
        name="attention_forward",
    )(place, w_own, w_other, w_out, q_gain, k_gain, cosine, sine, *[p[0] for p in pieces])


def rows_kernel(n_pieces, idx, target, *rest):
    pieces, (out, whole, sems) = rest[:n_pieces], rest[n_pieces:]
    waits = [[] for _ in range(8)]
    k = 0

    def start(r0, source, into):
        nonlocal k
        copy = pltpu.make_async_copy(source, into, sems.at[k])
        copy.start()
        waits[r0 // 2].append(copy)
        k += 1

    width = MODEL_WIDTH // 2
    for r in range(16):
        dy, dx = divmod(r, 4)
        if n_pieces == 1:
            start(r, pieces[0].at[idx[r], :, pl.ds(0, MODEL_WIDTH)], whole.at[r])
            continue
        a, ai = part_of(dy, dx)
        b, bi = part_of(dx, dy)
        start(r, pieces[a].at[ai], whole.at[r, :, pl.ds(0, width)])
        start(r, pieces[5 + b].at[bi], whole.at[r, :, pl.ds(width, width)])
    slots = lax.broadcasted_iota(jnp.int32, (80, 256), 0)
    for p in range(8):
        for copy in waits[p]:
            copy.wait()
        h = whole[2 * p : 2 * p + 2].reshape(256, MODEL_WIDTH)
        both = jnp.concatenate(
            [jnp.where(slots == target[p, e : e + 1], 1.0, 0.0) for e in range(2)], axis=0
        )
        rows = mm(both.astype(bf16), h).astype(bf16)
        out[0, 80 * p : 80 * p + 80] = rows[:80]
        out[1, 80 * p : 80 * p + 80] = rows[80:]


def slot_rows(pieces, idx, target):
    n = len(pieces)
    return pl.pallas_call(
        functools.partial(rows_kernel, n),
        out_shape=jax.ShapeDtypeStruct((2, 640, MODEL_WIDTH), bf16),
        in_specs=[SM, VM] + [ANY] * n,
        out_specs=VM,
        scratch_shapes=[pltpu.VMEM((16, 128, MODEL_WIDTH), bf16), pltpu.SemaphoreType.DMA((32,))],
        compiler_params=pltpu.CompilerParams(vmem_limit_bytes=40 * MIB),
        cost_estimate=pl.CostEstimate(flops=3 << 30, bytes_accessed=14 << 20, transcendentals=0),
        name="slot_rows",
    )(idx, target, *pieces)


def expert_kernel(xs, dys, gate, w_gate, w_up, w_down, dhr, hidden, dgate, dg, du, g_s, u_s, d_s):
    g_s[...] = mm(xs[0], w_gate[0])
    u_s[...] = mm(xs[0], w_up[0])
    d_s[...] = mm(dys[0], w_down[0], NT)

    @pl.loop(0, 10)
    def _(i):
        rows = pl.ds(pl.multiple_of(i * 64, 64), 64)
        g, u, d, s = g_s[rows], u_s[rows], d_s[rows], gate[0, rows][:, 0:1]
        sig = 1.0 / (1.0 + jnp.exp(-g))
        act = g * sig
        hid = act * u
        dgate[0, rows] = jnp.broadcast_to(jnp.sum(d * hid, axis=1, keepdims=True), (64, 128))
        hidden[0, rows] = (hid * s).astype(bf16)
        d = d * s
        du[0, rows] = (d * act).astype(bf16)
        dg[0, rows] = (d * u * sig * (1.0 + g * (1.0 - sig))).astype(bf16)

    dhr[0] = (mm(dg[0], w_gate[0], NT) + mm(du[0], w_up[0], NT)).astype(bf16)


def expert_rows(xs, dys, gate, w_gate, w_up, w_down):
    def one(*dims):
        return pl.BlockSpec((1, *dims), lambda e: (e, 0, 0))

    ff = w_down.shape[1]
    outs = [(MODEL_WIDTH, bf16), (ff, bf16), (128, f32), (ff, bf16), (ff, bf16)]
    return pl.pallas_call(
        expert_kernel,
        grid=(2,),
        out_shape=[jax.ShapeDtypeStruct((2, 640, n), t) for n, t in outs],
        in_specs=[one(640, MODEL_WIDTH)] * 2 + [one(640, 128)] + [one(MODEL_WIDTH, ff)] * 2 + [one(ff, MODEL_WIDTH)],
        out_specs=[one(640, n) for n, _ in outs],
        scratch_shapes=[pltpu.VMEM((640, ff), f32)] * 3,
        compiler_params=pltpu.CompilerParams(vmem_limit_bytes=60 * MIB),
        cost_estimate=pl.CostEstimate(flops=20 << 30, bytes_accessed=44 << 20, transcendentals=1 << 20),
        name="expert_rows",
    )(xs, dys, gate, w_gate, w_up, w_down)


def combine_kernel(target, rows, *outs):
    left, right = outs[:5], outs[5:]
    lane = lax.broadcasted_iota(jnp.int32, (256, 160), 1)
    width = MODEL_WIDTH // 2
    for p in range(8):
        t = target[p]
        pick = (lane == t[:, 0:1]) | (lane == t[:, 1:2])
        part = jnp.concatenate([rows[0, 80 * p : 80 * p + 80], rows[1, 80 * p : 80 * p + 80]], axis=0)
        whole = mm(jnp.where(pick, 1.0, 0.0).astype(bf16), part).astype(bf16)
        dy, dx0 = divmod(2 * p, 4)
        for b in range(2):
            dx = dx0 + b
            one = whole[128 * b : 128 * b + 128]
            a, ai = part_of(dy, dx)
            c, ci = part_of(dx, dy)
            left[a][ai] = one[:, :width]
            right[c][ci] = one[:, width:]


def combine(target, rows):
    width = MODEL_WIDTH // 2
    sizes = [4, 4, 2, 2, 4] * 2
    outs = pl.pallas_call(
        combine_kernel,
        out_shape=[jax.ShapeDtypeStruct((n, 128, width), bf16) for n in sizes],
        in_specs=[VM, VM],
        out_specs=[VM] * 10,
        compiler_params=pltpu.CompilerParams(vmem_limit_bytes=40 * MIB),
        cost_estimate=pl.CostEstimate(flops=2 << 30, bytes_accessed=14 << 20, transcendentals=0),
        name="combine",
    )(target, rows)
    return outs[:5], outs[5:]


def attention_back_kernel(spec, place, w_out, a_b, q_b, k_b, v_b, lse, q_raw, q_gain, cosine, sine, *rest):
    n = len(spec)
    pieces, rest = rest[:n], rest[n:]
    da, dq_raw, dkv, gain, dob, sems = rest
    for copy in load_pieces(place, spec, pieces, da, sems):
        copy.wait()

    @pl.loop(0, 4)
    def _(i):
        rows = pl.ds(pl.multiple_of(i * 256, 256), 256)
        dob[rows] = mm(da[rows], w_out[...], NT).astype(bf16)

    root = HEAD_SIZE**-0.5
    below = lax.broadcasted_iota(jnp.int32, (256, 256), 0) >= lax.broadcasted_iota(
        jnp.int32, (256, 256), 1
    )
    dkv[...] = jnp.zeros(dkv.shape, f32)
    total = jnp.zeros((1, HEAD_SIZE), f32)
    for i in range(4):
        keys = 256 * (i + 1)
        rows = slice(256 * i, keys)
        co, si = cosine[rows], sine[rows]
        for h in range(4):
            cols = slice(128 * h, 128 * h + 128)
            q, do = q_b[h, rows], dob[rows, cols]
            p = jnp.exp(mm(q, k_b[:keys], NT) * root - lse[rows, h : h + 1])
            tail = jnp.where(below, p[:, keys - 256 :], 0.0)
            p = tail if i == 0 else jnp.concatenate([p[:, : keys - 256], tail], axis=1)
            dp = mm(do, v_b[:keys], NT)
            mean = jnp.sum(do.astype(f32) * a_b[rows, cols].astype(f32), axis=1, keepdims=True)
            ds = (p * (dp - mean)).astype(bf16)
            dkv[:keys, :128] += mm(ds, q, TN) * root
            dkv[:keys, 128:] += mm(p.astype(bf16), do, TN)
            dq = (mm(ds, k_b[:keys]) * root).astype(bf16).astype(f32)
            dq_in = dq * co + pltpu.roll(dq * si, 64, 1)
            raw = q_raw[rows, cols]
            scale = lax.rsqrt(jnp.mean(raw * raw, axis=-1, keepdims=True) + epsilon)
            hat = raw * scale
            total = total + jnp.sum(dq_in * hat, axis=0, keepdims=True)
            t = dq_in * q_gain[...]
            back = scale * (t - hat * jnp.mean(t * hat, axis=-1, keepdims=True))
            dq_raw[rows, cols] = back.astype(bf16)
    gain[...] = total


def attention_backward(pieces, place, w_out, a_b, q_b, k_b, v_b, lse, q_raw, q_gain, cosine, sine):
    spec = [(dz, dc, first, a.shape[0]) for a, dz, dc, first in pieces]
    shapes = [((1024, MODEL_WIDTH), bf16), ((1024, 512), bf16), ((1024, 256), f32), ((1, HEAD_SIZE), f32)]
    return pl.pallas_call(
        functools.partial(attention_back_kernel, spec),
        out_shape=[jax.ShapeDtypeStruct(*s) for s in shapes],
        in_specs=[SM] + [VM] * 10 + [ANY] * len(spec),
        out_specs=[VM] * 4,
        scratch_shapes=[pltpu.VMEM((1024, 512), bf16), pltpu.SemaphoreType.DMA((len(spec),))],
        compiler_params=pltpu.CompilerParams(vmem_limit_bytes=56 * MIB),
        cost_estimate=pl.CostEstimate(flops=12 << 30, bytes_accessed=20 << 20, transcendentals=3 << 20),
        name="attention_backward",
    )(place, w_out, a_b, q_b, k_b, v_b, lse, q_raw, q_gain, cosine, sine, *[p[0] for p in pieces])


def grads_kernel(place, idx, dq_raw, own, other, k_raw, k_gain, cosine, sine, h1, low, high, dqkv, gain):
    c = place[1]
    dqkv[:, :512] = dq_raw[...]
    total = jnp.zeros((1, HEAD_SIZE), f32)
    for i in range(4):
        rows = slice(256 * i, 256 * i + 256)
        both = (own[rows] + other[rows]).astype(bf16)
        dk = both[:, :128].astype(f32)
        dk_in = dk * cosine[rows] + pltpu.roll(dk * sine[rows], 64, 1)
        raw = k_raw[rows]
        scale = lax.rsqrt(jnp.mean(raw * raw, axis=-1, keepdims=True) + epsilon)
        hat = raw * scale
        total = total + jnp.sum(dk_in * hat, axis=0, keepdims=True)
        t = dk_in * k_gain[...]
        back = scale * (t - hat * jnp.mean(t * hat, axis=-1, keepdims=True))
        dqkv[rows, 512:] = jnp.where(c == 0, back, both[:, 128:].astype(f32)).astype(bf16)
    gain[...] = total
    for f in range(8):
        out = low if f < 4 else high
        part = mm(h1[:, 256 * f : 256 * f + 256], dqkv[...], TN).astype(bf16)
        for r in range(16):
            dy, dx = idx[r] // 4, lax.rem(idx[r], 4)
            at = (dy, dx) if f < 4 else (dx, dy)
            out[at[0], at[1], f % 4] = part[16 * r : 16 * r + 16]


def projection_grads(place, back, dq_raw, own, other, k_raw, k_gain, cosine, sine, h1):
    half = ((4, 4, 4, 16, 640), bf16)
    shapes = [half, half, ((1024, 640), bf16), ((1, HEAD_SIZE), f32)]
    return pl.pallas_call(
        grads_kernel,
        out_shape=[jax.ShapeDtypeStruct(*s) for s in shapes],
        in_specs=[SM, SM] + [VM] * 8,
        out_specs=[VM] * 4,
        compiler_params=pltpu.CompilerParams(vmem_limit_bytes=48 * MIB),
        cost_estimate=pl.CostEstimate(flops=3 << 30, bytes_accessed=12 << 20, transcendentals=0),
        name="projection_grads",
    )(place, back, dq_raw, own, other, k_raw, k_gain, cosine, sine, h1)


def input_grad_kernel(place, dqkv, w_own, keep, send):
    z, c = place[0], place[1]

    @pl.loop(0, 4)
    def _(i):
        rows = pl.ds(pl.multiple_of(i * 256, 256), 256)
        part = mm(dqkv[rows], w_own[...], NT).astype(bf16)
        dz = lax.rem(i - z + 4, 4)
        first, second = part[:128], part[128:]
        keep[dz] = jnp.where(c == 0, first, second)
        send[dz] = jnp.where(c == 0, second, first)


def input_grad(place, dqkv, w_own):
    return pl.pallas_call(
        input_grad_kernel,
        out_shape=[jax.ShapeDtypeStruct((4, 128, MODEL_WIDTH), bf16)] * 2,
        in_specs=[SM, VM, VM],
        out_specs=[VM] * 2,
        compiler_params=pltpu.CompilerParams(vmem_limit_bytes=40 * MIB),
        cost_estimate=pl.CostEstimate(flops=3 << 30, bytes_accessed=8 << 20, transcendentals=0),
        name="input_grad",
    )(place, dqkv, w_own)


def place_kernel(idx, *refs):
    left, right, (query, key, value) = refs[:5], refs[5:10], refs[10:]
    for r in range(16):
        dy, dx = divmod(r, 4)
        rows = pl.ds(pl.multiple_of(idx[r] * 16, 16), 16)
        a, ai = part_of(dy, dx)
        b, bi = part_of(dx, dy)
        for f in range(8):
            block = (left[a][ai, f] if f < 4 else right[b][bi, f - 4]).astype(f32)
            query[rows, 512 * f : 512 * f + 512] = block[:, :512]
            out = key if f % 2 == 0 else value
            out[rows, 128 * (f // 2) : 128 * (f // 2) + 128] = block[:, 512:]


def place_rows(idx, left, right):
    return pl.pallas_call(
        place_kernel,
        out_shape=[jax.ShapeDtypeStruct((256, n), f32) for n in (4096, 512, 512)],
        in_specs=[SM] + [VM] * 10,
        out_specs=[VM] * 3,
        compiler_params=pltpu.CompilerParams(vmem_limit_bytes=32 * MIB),
        cost_estimate=pl.CostEstimate(flops=0, bytes_accessed=8 << 20, transcendentals=0),
        name="place_rows",
    )(idx, *left, *right)


def place_out_kernel(idx, *refs):
    left, right, out = refs[:5], refs[5:10], refs[10]
    width = MODEL_WIDTH // 2
    for r in range(16):
        dy, dx = divmod(r, 4)
        rows = pl.ds(pl.multiple_of(idx[r] * 32, 32), 32)
        a, ai = part_of(dy, dx)
        b, bi = part_of(dx, dy)
        out[rows, :width] = left[a][ai].astype(f32)
        out[rows, width:] = right[b][bi].astype(f32)


def place_out(idx, left, right):
    return pl.pallas_call(
        place_out_kernel,
        out_shape=jax.ShapeDtypeStruct((512, MODEL_WIDTH), f32),
        in_specs=[SM] + [VM] * 10,
        out_specs=VM,
        compiler_params=pltpu.CompilerParams(vmem_limit_bytes=32 * MIB),
        cost_estimate=pl.CostEstimate(flops=0, bytes_accessed=6 << 20, transcendentals=0),
        name="place_out",
    )(idx, *left, *right)


def out_grads_kernel(idx, a_b, da, low, high):
    width = MODEL_WIDTH // 2
    for f in range(2):
        part = mm(a_b[:, 256 * f : 256 * f + 256], da[...], TN).astype(bf16)
        for r in range(8):
            dy, dx = idx[8 * f + r] // 4, lax.rem(idx[8 * f + r], 4)
            block = part[32 * r : 32 * r + 32]
            low[dy, dx] = block[:, :width]
            high[dx, dy] = block[:, width:]


def out_grads(back, a_b, da):
    return pl.pallas_call(
        out_grads_kernel,
        out_shape=[jax.ShapeDtypeStruct((4, 4, 32, MODEL_WIDTH // 2), bf16)] * 2,
        in_specs=[SM, VM, VM],
        out_specs=[VM] * 2,
        compiler_params=pltpu.CompilerParams(vmem_limit_bytes=40 * MIB),
        cost_estimate=pl.CostEstimate(flops=2 << 30, bytes_accessed=8 << 20, transcendentals=0),
        name="out_grads",
    )(back, a_b, da)


def tied(*values):
    return lax.optimization_barrier(values)


def local(
    layer_input, routes, cotangent, attn_gain, query_gain, key_gain, mlp_gain,
    w_query, key_weight, value_weight, w_out, w_router, w_gate, w_up, w_down,
):
    core = lax.axis_index(C)
    place = lax.axis_index(EXPERT)
    py, px = lax.axis_index(Y), lax.axis_index(X)
    zc = jnp.stack([lax.axis_index(Z), core]).astype(jnp.int32)
    ahead = jnp.arange(16, dtype=jnp.int32)
    idx = (py + ahead // 4) % 4 * 4 + (px + ahead % 4) % 4
    back = (ahead // 4 - py) % 4 * 4 + (ahead % 4 - px) % 4
    residual = layer_input[0].astype(f32)
    dy_low = cotangent[0]
    upstream = dy_low.astype(f32)
    scale_one = inv_rms(residual)
    normed_one = residual * scale_one
    h1 = (normed_one * attn_gain).astype(bf16)
    h1_pieces = gather_fsdp(h1)
    rows = w_query.shape[0]
    key_value = jnp.stack([key_weight.reshape(rows, 4, 128), value_weight.reshape(rows, 4, 128)], axis=2)
    blocks = jnp.concatenate(
        [w_query.reshape(rows, 8, 512), key_value.reshape(rows, 8, 128)], axis=2
    ).transpose(1, 0, 2)
    w_own = lax.all_to_all(blocks, FSDP, 0, 0, tiled=True).reshape(8 * rows, 640)
    w_other = shift(w_own[:, 512:], C, 1)
    seq = 1024
    cosine, sine = rope_tables(jnp.arange(seq).astype(f32))
    sign = jnp.where(jnp.arange(HEAD_SIZE) < HEAD_SIZE // 2, -1.0, 1.0).astype(f32)
    signed = sine * sign
    h1_all, q_raw, k_raw, v_b, q_b, k_b, a_b, lse, keep, send = attention_forward(
        h1_pieces, zc, w_own, w_other, w_out, query_gain[None], key_gain[None], cosine, signed
    )
    beside = jnp.pad(routes[0], ((0, 0), (0, 120))).astype(bf16)
    dy_all = lax.all_gather(jnp.concatenate([dy_low, beside], axis=1), EXPERT, axis=0, tiled=False)
    router_own = jnp.pad(w_router, ((0, 0), (0, 96)))
    gate_all = lax.all_gather(
        jnp.concatenate([w_gate, jnp.stack([router_own, router_own])], axis=2), FSDP, axis=1, tiled=True
    )
    up_all = lax.all_gather(w_up, FSDP, axis=1, tiled=True)
    down_all = lax.all_gather(w_down, FSDP, axis=1, tiled=True)
    router = gate_all[0, :, 768 : 768 + EXPERTS]
    routes_all = dy_all[:, :, MODEL_WIDTH : MODEL_WIDTH + TOPK].astype(jnp.int32)
    routes_rel = routes_all[idx]
    own_ids = 2 * place + jnp.arange(2, dtype=jnp.int32)
    member = jnp.any(routes_rel[:, None, :, :] == own_ids[None, :, None, None], axis=-1)
    rank = jnp.cumsum(member.astype(jnp.int32), axis=2) - 1
    slot = jnp.where(member, rank, -1)
    by_pair = slot.reshape(8, 2, 2, 128)
    shifted = jnp.where(by_pair >= 0, by_pair + CAP * jnp.arange(2, dtype=jnp.int32)[:, None, None], -1)
    target = shifted.transpose(0, 2, 1, 3).reshape(8, 2, 256)
    target_t = jnp.where(
        target >= 0, target + 2 * CAP * jnp.arange(2, dtype=jnp.int32)[:, None], -1
    ).transpose(0, 2, 1)
    pick = slot[:, :, None, :] == jnp.arange(CAP)[None, None, :, None]
    dys = slot_rows([dy_all], idx, target)
    attn = scatter_fsdp(keep, send)
    attn, dys, target_t = tied(attn, dys, target_t)
    resid_two = residual + attn
    scale_two = inv_rms(resid_two)
    normed_two = resid_two * scale_two
    h2 = (normed_two * mlp_gain).astype(bf16)
    half = MODEL_WIDTH // 2
    left, right = gather_plane(h2[:, :half], h2[:, half:])
    ids = jnp.arange(EXPERTS, dtype=jnp.int32)
    logits = dot(h2, router)
    chosen = jnp.any(routes[0][:, :, None] == ids, axis=1)
    logits = jnp.where(chosen, logits, -1e30)
    powers = jnp.where(chosen, jnp.exp(logits - jnp.max(logits, axis=-1, keepdims=True)), 0.0)
    gates_own = powers / jnp.sum(powers, axis=-1, keepdims=True)
    gates_part = gates_own.reshape(128, 16, 2).transpose(1, 2, 0)
    gates_all = lax.all_to_all(gates_part, EXPERT, 0, 0, tiled=True)[idx]
    slot_gate = jnp.sum(jnp.where(pick, gates_all[:, :, None, :], 0.0), axis=-1)
    slot_gate = slot_gate.transpose(1, 0, 2).reshape(2, 640, 1)
    slot_gate = jnp.broadcast_to(slot_gate, (2, 640, 128))
    xs = slot_rows([*left, *right], idx, target)
    dhr, hidden, dgate_slot, dg, du = expert_rows(xs, dys, slot_gate, gate_all, up_all, down_all)
    dh_left, dh_right = scatter_plane(*combine(target_t, dhr))
    dh_sum = jnp.concatenate([dh_left, dh_right], axis=1)
    dgate_slot = dgate_slot[:, :, 0].reshape(2, 16, CAP).transpose(1, 0, 2)
    dgate_part = jnp.sum(jnp.where(pick, dgate_slot[..., None], 0.0), axis=2)[back]
    dgate_all = lax.all_to_all(dgate_part, EXPERT, 0, 0, tiled=True)
    dgate = dgate_all.transpose(2, 0, 1).reshape(128, EXPERTS)
    grad_gate = es("erd,erf->edf", xs, dg).astype(bf16)
    grad_up = es("erd,erf->edf", xs, du).astype(bf16)
    grad_down = es("erf,erd->efd", hidden, dys).astype(bf16)
    ys = es("erf,efd->erd", hidden, down_all).astype(bf16)
    y_left, y_right = combine(target_t, ys)
    dh_sum, grad_gate, grad_up, grad_down, y_left, y_right = tied(
        dh_sum, grad_gate, grad_up, grad_down, y_left, y_right
    )
    expert_grads = [
        lax.psum_scatter(v, FSDP, scatter_dimension=1, tiled=True).astype(f32)
        for v in (grad_gate, grad_up, grad_down)
    ]
    dl = (gates_own * (dgate - jnp.sum(gates_own * dgate, axis=-1, keepdims=True))).astype(bf16)
    dh2 = es("te,de->td", dl, router) + dh_sum
    dx2 = upstream + norm_back(dh2 * mlp_gain, normed_two, scale_two)
    da = dx2.astype(bf16)
    da_pieces = gather_fsdp(da)
    grad_mlp_gain = jnp.sum(dh2 * normed_two, axis=0)
    grad_router = es("te,td->ed", dl, h2)
    early = sum_all(jnp.concatenate([grad_router, grad_mlp_gain[None]], axis=0))
    y_left, y_right = scatter_plane(y_left, y_right)
    output = (resid_two + jnp.concatenate([y_left, y_right], axis=1)).astype(bf16)
    da_all, dq_raw, dkv, q_gain_part = attention_backward(
        da_pieces, zc, w_out, a_b, q_b, k_b, v_b, lse, q_raw, query_gain[None], cosine, signed
    )
    low, high, dqkv, k_gain_part = projection_grads(
        zc, back, dq_raw, dkv, shift(dkv, C, 1), k_raw, key_gain[None], cosine, signed, h1_all
    )

    def halves(v):
        return v[0], v[1], v[2, :2], v[2, 2:], v[3]

    low, high = scatter_plane(halves(low), halves(high))
    keep, send = input_grad(zc, dqkv, w_own)
    dh1 = scatter_fsdp(keep, send)
    grad_input = dx2 + norm_back(dh1 * attn_gain, normed_one, scale_one)
    out_low, out_high = out_grads(back, a_b, da_all)
    out_low, out_high = scatter_plane(halves(out_low), halves(out_high))
    grad_out = place_out(idx, *gather_plane(out_low.astype(bf16), out_high.astype(bf16)))
    parted = jnp.concatenate([low, high]).astype(bf16)
    parted = lax.all_to_all(parted, FSDP, 0, 0, tiled=True)
    grad_query, grad_key, grad_value = place_rows(idx, *gather_plane(parted[:4], parted[4:]))
    grad_attn_gain = jnp.sum(dh1 * normed_one, axis=0)
    late = sum_all(jnp.concatenate([grad_attn_gain, q_gain_part[0], k_gain_part[0] * 0.5]).reshape(18, 128))
    late = late.reshape(-1)
    grad_router = lax.dynamic_slice_in_dim(early[:EXPERTS], 256 * lax.axis_index(FSDP), 256, 1).T
    return (
        output[None],
        grad_input.astype(bf16)[None],
        late[:MODEL_WIDTH],
        late[MODEL_WIDTH : MODEL_WIDTH + HEAD_SIZE],
        late[MODEL_WIDTH + HEAD_SIZE :],
        early[EXPERTS],
        grad_query,
        grad_key,
        grad_value,
        grad_out,
        grad_router,
        *expert_grads,
    )


def solution(mesh):
    torus = Mesh(mesh.devices.reshape(4, 2, 4, 4), ALL)
    tokens, rows, experts = P(EXPERT, FSDP, None), P(FSDP, None), P(EXPERT, FSDP, None)
    return jax.shard_map(
        local,
        mesh=torus,
        in_specs=(tokens,) * 3 + (P(),) * 4 + (rows,) * 5 + (experts,) * 3,
        out_specs=(tokens,) * 2 + (P(),) * 4 + (rows,) * 5 + (experts,) * 3,
        check_vma=False,
    )
```

```python
import functools

import jax
import jax.numpy as jnp
from jax import lax
from jax.experimental import pallas as pl
from jax.experimental.pallas import tpu as pltpu
from jax.sharding import Mesh
from jax.sharding import PartitionSpec as P

MODEL_WIDTH = 2048
QUERY_HEADS = 32
KEY_VALUE_HEADS = 4
HEAD_SIZE = 128
TOPK = 8
EXPERTS = 32
CAP = 40
Z, C, Y, X = "z", "c", "y", "x"
FSDP = (Z, C)
EXPERT = (Y, X)
ALL = (Z, C, Y, X)

bf16 = jnp.bfloat16
f32 = jnp.float32
epsilon = 1e-06
rope_base = 1000000.0


def dot(a, b):
    return jnp.dot(a, b, preferred_element_type=f32)


def es(spec, a, b):
    return jnp.einsum(spec, a, b, preferred_element_type=f32)


def shift(v, axis, by):
    n = 2 if axis == C else 4
    return lax.ppermute(v, axis, [(i, (i + by) % n) for i in range(n)])


def gather_fsdp(p, join=lambda *values: values):
    half = p.shape[0] // 2
    up, down = join(shift(p, Z, -1), shift(p, Z, 1))
    other = shift(p, C, 1)
    far_low, far_high = shift(down[:half], Z, 1), shift(up[half:], Z, -1)
    far = [(up, 1, 0), (down, 3, 0), (far_low, 2, 0), (far_high, 2, half)]
    return (
        [(p, 0, 0, 0), (other, 0, 1, 0)]
        + [(a, dz, 0, r) for a, dz, r in far]
        + [(shift(a, C, 1), dz, 1, r) for a, dz, r in far]
    )


def scatter_fsdp(keep, send, join=lambda *values: values):
    got = shift(send, C, 1)
    half = keep.shape[1] // 2

    def both(d, rows=slice(None)):
        return (keep[d, rows].astype(f32) + got[d, rows].astype(f32)).astype(bf16)

    low, high = slice(None, half), slice(half, None)
    far_low, far_high = both(2, low), both(2, high)
    from_down, from_up = shift(far_low, Z, 1), shift(far_high, Z, -1)
    one, three = both(1), both(3)
    one = jnp.concatenate([(one[low].astype(f32) + from_down.astype(f32)).astype(bf16), one[high]])
    three = jnp.concatenate([three[low], (three[high].astype(f32) + from_up.astype(f32)).astype(bf16)])
    one, three = join(one, three)
    from_down, from_up = shift(one, Z, 1), shift(three, Z, -1)
    own = keep[0].astype(f32) + got[0].astype(f32)
    return own + from_down.astype(f32) + from_up.astype(f32)


def gather_ring(v, axis):
    half = v.shape[0] // 2
    up, down = shift(v, axis, -1), shift(v, axis, 1)
    return v, up, shift(down[:half], axis, 1), shift(up[half:], axis, -1), down


def gather_plane(left, right):
    def stacked(parts):
        a, b, low, high, d = parts
        return jnp.stack([a, b, jnp.concatenate([low, high]), d])

    left, right = gather_ring(left, X), gather_ring(right, Y)
    return gather_ring(stacked(left), Y), gather_ring(stacked(right), X)


def sum_all(v):
    v = v + shift(v, C, 1)
    for axis in (Z, Y, X):
        v = (v + shift(v, axis, 2)) + (shift(v, axis, 1) + shift(v, axis, 3))
    return v


def inv_rms(values):
    return lax.rsqrt(jnp.mean(values * values, axis=-1, keepdims=True) + epsilon)


def norm_back(grad_norm, normed, scale_part):
    return scale_part * (grad_norm - normed * jnp.mean(grad_norm * normed, axis=-1, keepdims=True))


def rope_tables(positions):
    frequency = rope_base ** (-(jnp.arange(HEAD_SIZE // 2).astype(f32) * 2.0 / HEAD_SIZE))
    frequency = jnp.concatenate([frequency, frequency])
    angles = positions[:, None] * frequency[None, :]
    return jnp.cos(angles), jnp.sin(angles)


def mm(a, b, dims=((1,), (0,))):
    return lax.dot_general(a, b, (dims, ((), ())), preferred_element_type=f32)


NT = ((1,), (1,))
TN = ((0,), (0,))
ANY = pl.BlockSpec(memory_space=pl.ANY)
VM = pl.BlockSpec(memory_space=pltpu.VMEM)
SM = pl.BlockSpec(memory_space=pltpu.SMEM)
MIB = 1 << 20


def load_pieces(place, spec, pieces, whole, sems):
    copies = []
    for k, (dz, dc, first, rows) in enumerate(spec):
        at = lax.rem(place[0] + dz, 4) * 256 + lax.rem(place[1] + dc, 2) * 128 + first
        at = pl.multiple_of(at, 64)
        copies.append(pltpu.make_async_copy(pieces[k], whole.at[pl.ds(at, rows)], sems.at[k]))
    for copy in copies:
        copy.start()
    return copies


def load_weights(place, parts, w, sems):
    copies = []
    width = w.shape[3] // 2
    own, from_x, from_y = parts
    for k in range(8):
        source = lax.rem(place[0] + 4 - k % 4, 4) * 2 + lax.rem(place[1] + k // 4, 2)
        for side, (at, other) in enumerate(((place[3], from_x), (place[2], from_y))):
            cols = pl.ds(side * width, width)
            for j, piece in enumerate((own.at[k, :, cols], other.at[k])):
                into = w.at[source, lax.rem(at + j, 2), :, cols]
                copies.append(pltpu.make_async_copy(piece, into, sems.at[4 * k + 2 * side + j]))
    for copy in copies:
        copy.start()
    return copies


def attention_kernel(spec, place, w_out, q_gain, k_gain, cosine, sine, *rest):
    n = len(spec)
    pieces, parts, rest = rest[:n], rest[n : n + 3], rest[n + 3 :]
    w, h1, q_raw, k_raw, v_b, q_b, k_b, a_b, lse, keep, send, sems, w_sems = rest
    z, c = place[0], place[1]
    copies = load_weights(place, parts, w, w_sems)
    for copy in load_pieces(place, spec, pieces, h1, sems) + copies:
        copy.wait()

    @pl.loop(0, 4)
    def _(i):
        rows = pl.ds(pl.multiple_of(i * 256, 256), 256)
        t = mm(h1[rows, :MODEL_WIDTH], w[...].reshape(MODEL_WIDTH, 768))
        q_raw[rows] = t[:, :512]
        k_raw[rows] = t[:, 512:640]
        v_b[rows] = t[:, 640:].astype(bf16)
        co, si = cosine[rows], sine[rows]

        def rotated(u, gain):
            u = u * lax.rsqrt(jnp.mean(u * u, axis=-1, keepdims=True) + epsilon) * gain
            return (u * co + pltpu.roll(u, 64, 1) * si).astype(bf16)

        for h in range(4):
            q_b[h, rows] = rotated(t[:, 128 * h : 128 * h + 128], q_gain[...])
        k_b[rows] = rotated(t[:, 512:640], k_gain[...])

    lane = lax.broadcasted_iota(jnp.int32, (256, 128), 1)
    below = lax.broadcasted_iota(jnp.int32, (256, 256), 0) >= lax.broadcasted_iota(
        jnp.int32, (256, 256), 1
    )
    for i in range(4):
        n_keys = 256 * (i + 1)
        rows = slice(256 * i, n_keys)
        logs = jnp.zeros((256, 128), f32)
        for h in range(4):
            s = mm(q_b[h, rows], k_b[:n_keys], NT) * (HEAD_SIZE**-0.5)
            e = jnp.exp(s)
            tail = jnp.where(below, e[:, n_keys - 256 :], 0.0)
            e = tail if i == 0 else jnp.concatenate([e[:, : n_keys - 256], tail], axis=1)
            total = jnp.sum(e, axis=1, keepdims=True)
            a = mm(e.astype(bf16), v_b[:n_keys]) / total
            a_b[rows, 128 * h : 128 * h + 128] = a.astype(bf16)
            logs = jnp.where(lane == h, jnp.log(total), logs)
        lse[rows] = logs
        part = mm(a_b[rows], w_out[...]).astype(bf16)
        dz = lax.rem(i - z + 4, 4)
        first, second = part[:128], part[128:]
        keep[dz] = jnp.where(c == 0, first, second)
        send[dz] = jnp.where(c == 0, second, first)


def attention_forward(pieces, parts, place, w_out, q_gain, k_gain, cosine, sine):
    spec = [(dz, dc, first, a.shape[0]) for a, dz, dc, first in pieces]
    seq = 1024
    shapes = [
        ((8, 2, 128, 768), bf16),
        ((seq, MODEL_WIDTH + 128), bf16),
        ((seq, 512), f32),
        ((seq, 128), f32),
        ((seq, 128), bf16),
        ((4, seq, 128), bf16),
        ((seq, 128), bf16),
        ((seq, 512), bf16),
        ((seq, 128), f32),
        ((4, 128, MODEL_WIDTH), bf16),
        ((4, 128, MODEL_WIDTH), bf16),
    ]
    return pl.pallas_call(
        functools.partial(attention_kernel, spec),
        out_shape=[jax.ShapeDtypeStruct(*s) for s in shapes],
        in_specs=[SM] + [VM] * 5 + [ANY] * (len(spec) + 3),
        out_specs=[VM] * len(shapes),
        scratch_shapes=[pltpu.SemaphoreType.DMA((len(spec),)), pltpu.SemaphoreType.DMA((32,))],
        compiler_params=pltpu.CompilerParams(vmem_limit_bytes=56 * MIB),
        cost_estimate=pl.CostEstimate(flops=9 << 30, bytes_accessed=28 << 20, transcendentals=3 << 20),
        name="attention_forward",
    )(place, w_out, q_gain, k_gain, cosine, sine, *[p[0] for p in pieces], *parts)


def expert_kernel(e, xs_in, dys_in, w_in, w_down, back, hid, dg, du, xs, dys, wg, wu, wd, sems):
    loads = []
    for k, (source, into) in enumerate(
        (
            (xs_in.at[:, pl.ds(0, MODEL_WIDTH)], xs), (w_in.at[e], wg), (w_in.at[2 + e], wu), (dys_in, dys), (w_down.at[e], wd),
        )
    ):
        loads.append(pltpu.make_async_copy(source, into, sems.at[k]))
        loads[-1].start()
    total = jnp.zeros((640, 1), f32)
    for k in range(3):
        loads[k].wait()
    for i in range(3):
        cols = slice(256 * i, 256 * i + 256)
        g, u = mm(xs[...], wg[:, cols]), mm(xs[...], wu[:, cols])
        if i == 0:
            loads[3].wait()
            loads[4].wait()
        d = mm(dys[...], wd[cols], NT)
        sig = 0.5 + 0.5 * jnp.tanh(0.5 * g)
        act = g * sig
        h = act * u
        total = total + jnp.sum(d * h, axis=1, keepdims=True)
        hid[:, cols] = h.astype(bf16)
        du[:, cols] = (d * act).astype(bf16)
        dg[:, cols] = (d * u * (sig + act * (1.0 - sig))).astype(bf16)
    back[:, :MODEL_WIDTH] = (mm(dg[...], wg[...], NT) + mm(du[...], wu[...], NT)).astype(bf16)
    high = total.astype(bf16).astype(f32)
    lane = lax.broadcasted_iota(jnp.int32, (640, 128), 1)
    back[:, MODEL_WIDTH:] = jnp.where(lane == 0, high, jnp.where(lane == 1, total - high, 0.0)).astype(bf16)


def expert_rows(e, xs, dys, w_in, w_down):
    row, act = (640, MODEL_WIDTH), (640, 768)
    scratch = [row, row, (MODEL_WIDTH, 768), (MODEL_WIDTH, 768), (768, MODEL_WIDTH)]
    return pl.pallas_call(
        functools.partial(expert_kernel, e),
        out_shape=[jax.ShapeDtypeStruct(s, bf16) for s in ((640, MODEL_WIDTH + 128), act, act, act)],
        in_specs=[ANY] * 4,
        out_specs=[VM] * 4,
        scratch_shapes=[pltpu.VMEM(s, bf16) for s in scratch] + [pltpu.SemaphoreType.DMA((5,))],
        compiler_params=pltpu.CompilerParams(vmem_limit_bytes=48 * MIB),
        cost_estimate=pl.CostEstimate(flops=10 << 30, bytes_accessed=20 << 20, transcendentals=1 << 20),
        name="expert_rows",
    )(xs, dys, w_in, w_down)


def weight_grads_kernel(*refs):
    rows, w_down, grads, ys = refs[:12], refs[12], refs[14:17], refs[17:19]
    first = pl.program_id(0) == 0
    for e in range(2):
        xs, dys, hid, dg, du, gate = rows[6 * e : 6 * e + 6]

        @pl.when(first if e == 0 else jnp.logical_not(first))
        def _(xs=xs, dys=dys, hid=hid, dg=dg, du=du, gate=gate, out=ys[e]):
            s = gate[:, 0:1]

            def scaled(v):
                return (v[...].astype(f32) * s).astype(bf16)

            out[...] = mm(hid[...], w_down[0]).astype(bf16)
            grads[0][0] = mm(xs[:, :MODEL_WIDTH], scaled(dg), TN).astype(bf16)
            grads[1][0] = mm(xs[:, :MODEL_WIDTH], scaled(du), TN).astype(bf16)
            grads[2][0] = mm(scaled(hid), dys[...], TN).astype(bf16)


def weight_grads(rows, w_down, event):
    def per_expert(*dims):
        return pl.BlockSpec((1, *dims), lambda e: (e, 0, 0))

    sizes = [(MODEL_WIDTH, 768), (MODEL_WIDTH, 768), (768, MODEL_WIDTH)]
    return pl.pallas_call(
        weight_grads_kernel,
        grid=(2,),
        out_shape=[jax.ShapeDtypeStruct((2, *s), bf16) for s in sizes]
        + [jax.ShapeDtypeStruct((640, MODEL_WIDTH), bf16)] * 2,
        in_specs=[VM] * 12 + [per_expert(768, MODEL_WIDTH), ANY],
        out_specs=[per_expert(*s) for s in sizes] + [VM] * 2,
        compiler_params=pltpu.CompilerParams(vmem_limit_bytes=60 * MIB),
        cost_estimate=pl.CostEstimate(flops=16 << 30, bytes_accessed=48 << 20, transcendentals=0),
        name="weight_grads",
    )(*rows, w_down, event)


def out_back_kernel(spec, place, w_out, a_b, *rest):
    n = len(spec)
    pieces, (dob, shares, da, sems) = rest[:n], rest[n:]
    for copy in load_pieces(place, spec, pieces, da, sems):
        copy.wait()

    @pl.loop(0, 4)
    def _(i):
        rows = pl.ds(pl.multiple_of(i * 256, 256), 256)
        dob[rows] = mm(da[rows], w_out[...], NT).astype(bf16)

    shares[...] = mm(a_b[...], da[...], TN).astype(bf16)


def out_back(pieces, place, w_out, a_b):
    spec = [(dz, dc, first, a.shape[0]) for a, dz, dc, first in pieces]
    shapes = [((1024, 512), bf16), ((512, MODEL_WIDTH), bf16)]
    return pl.pallas_call(
        functools.partial(out_back_kernel, spec),
        out_shape=[jax.ShapeDtypeStruct(*s) for s in shapes],
        in_specs=[SM] + [VM] * 2 + [ANY] * len(spec),
        out_specs=[VM] * 2,
        scratch_shapes=[pltpu.VMEM((1024, MODEL_WIDTH), bf16), pltpu.SemaphoreType.DMA((len(spec),))],
        compiler_params=pltpu.CompilerParams(vmem_limit_bytes=40 * MIB),
        cost_estimate=pl.CostEstimate(flops=5 << 30, bytes_accessed=12 << 20, transcendentals=0),
        name="out_back",
    )(place, w_out, a_b, *[p[0] for p in pieces])


def attention_back_kernel(dob, a_b, q_b, k_b, v_b, lse, q_raw, q_gain, cosine, sine, dq_raw, dkv, gain):
    root = HEAD_SIZE**-0.5
    below = lax.broadcasted_iota(jnp.int32, (256, 256), 0) >= lax.broadcasted_iota(
        jnp.int32, (256, 256), 1
    )
    dkv[...] = jnp.zeros(dkv.shape, f32)
    total = jnp.zeros((1, HEAD_SIZE), f32)
    for i in range(4):
        keys = 256 * (i + 1)
        rows = slice(256 * i, keys)
        co, si = cosine[rows], sine[rows]
        for h in range(4):
            cols = slice(128 * h, 128 * h + 128)
            q, do = q_b[h, rows], dob[rows, cols]
            p = jnp.exp(mm(q, k_b[:keys], NT) * root - lse[rows, h : h + 1])
            tail = jnp.where(below, p[:, keys - 256 :], 0.0)
            p = tail if i == 0 else jnp.concatenate([p[:, : keys - 256], tail], axis=1)
            dp = mm(do, v_b[:keys], NT)
            mean = jnp.sum(do.astype(f32) * a_b[rows, cols].astype(f32), axis=1, keepdims=True)
            ds = (p * (dp - mean)).astype(bf16)
            dkv[:keys, :128] += mm(ds, q, TN) * root
            dkv[:keys, 128:] += mm(p.astype(bf16), do, TN)
            dq = (mm(ds, k_b[:keys]) * root).astype(bf16).astype(f32)
            dq_in = dq * co + pltpu.roll(dq * si, 64, 1)
            raw = q_raw[rows, cols]
            scale = lax.rsqrt(jnp.mean(raw * raw, axis=-1, keepdims=True) + epsilon)
            hat = raw * scale
            total = total + jnp.sum(dq_in * hat, axis=0, keepdims=True)
            t = dq_in * q_gain[...]
            back = scale * (t - hat * jnp.mean(t * hat, axis=-1, keepdims=True))
            dq_raw[rows, cols] = back.astype(bf16)
    gain[...] = total


def attention_backward(dob, a_b, q_b, k_b, v_b, lse, q_raw, q_gain, cosine, sine):
    shapes = [((1024, 512), bf16), ((1024, 256), f32), ((1, HEAD_SIZE), f32)]
    return pl.pallas_call(
        attention_back_kernel,
        out_shape=[jax.ShapeDtypeStruct(*s) for s in shapes],
        in_specs=[VM] * 10,
        out_specs=[VM] * 3,
        compiler_params=pltpu.CompilerParams(vmem_limit_bytes=48 * MIB),
        cost_estimate=pl.CostEstimate(flops=10 << 30, bytes_accessed=12 << 20, transcendentals=3 << 20),
        name="attention_backward",
    )(dob, a_b, q_b, k_b, v_b, lse, q_raw, q_gain, cosine, sine)


def grads_kernel(
    place, dq_raw, own, other, k_raw, q_part, k_gain, cosine, sine, h1, w, aux, _,
    shares, dqkv, along_out, k_part,
):
    c = place[1]
    dqkv[:, :512] = dq_raw[...]
    total = jnp.zeros((1, HEAD_SIZE), f32)
    for i in range(4):
        rows = slice(256 * i, 256 * i + 256)
        both = (own[rows] + other[rows]).astype(bf16)
        dk = both[:, :128].astype(f32)
        dk_in = dk * cosine[rows] + pltpu.roll(dk * sine[rows], 64, 1)
        raw = k_raw[rows]
        scale = lax.rsqrt(jnp.mean(raw * raw, axis=-1, keepdims=True) + epsilon)
        hat = raw * scale
        total = total + jnp.sum(dk_in * hat, axis=0, keepdims=True)
        t = dk_in * k_gain[...]
        grad = scale * (t - hat * jnp.mean(t * hat, axis=-1, keepdims=True))
        dqkv[rows, 512:] = jnp.where(c == 0, grad, both[:, 128:].astype(f32)).astype(bf16)
    k_part[...] = total * 0.5
    for f in range(8):
        shard = slice(256 * f, 256 * f + 256)
        part = mm(h1[:, shard], dqkv[...], TN)
        last = jnp.where(c == 0, w[shard, 512:640], w[shard, 640:])
        along = jnp.sum(part[:, :512] * w[shard, :512].astype(f32), axis=1, keepdims=True)
        along = along + jnp.sum(part[:, 512:] * last.astype(f32), axis=1, keepdims=True)
        along_out[shard] = jnp.broadcast_to(along, (256, 128))
        part = jnp.concatenate([part.astype(bf16), aux[shard].astype(bf16)], axis=1)
        for r in range(16):
            shares[r, 16 * f : 16 * f + 16] = part[16 * r : 16 * r + 16]


def projection_grads(place, dq_raw, own, other, k_raw, q_part, k_gain, cosine, sine, h1, w, aux, event):
    shapes = [((16, 128, 768), bf16), ((1024, 640), bf16), ((MODEL_WIDTH, 128), f32), ((1, HEAD_SIZE), f32)]
    return pl.pallas_call(
        grads_kernel,
        out_shape=[jax.ShapeDtypeStruct(*s) for s in shapes],
        in_specs=[SM] + [VM] * 11 + [ANY],
        out_specs=[VM] * 4,
        compiler_params=pltpu.CompilerParams(vmem_limit_bytes=48 * MIB),
        cost_estimate=pl.CostEstimate(flops=3 << 30, bytes_accessed=16 << 20, transcendentals=0),
        name="projection_grads",
    )(place, dq_raw, own, other, k_raw, q_part, k_gain, cosine, sine, h1, w, aux, event)


def input_grad_kernel(place, dqkv, w, keep, send, w_own):
    z, c = place[0], place[1]
    w_own[:, :512] = w[:, :512]
    w_own[:, 512:] = jnp.where(c == 0, w[:, 512:640], w[:, 640:])

    @pl.loop(0, 4)
    def _(i):
        rows = pl.ds(pl.multiple_of(i * 256, 256), 256)
        part = mm(dqkv[rows], w_own[...], NT).astype(bf16)
        dz = lax.rem(i - z + 4, 4)
        first, second = part[:128], part[128:]
        keep[dz] = jnp.where(c == 0, first, second)
        send[dz] = jnp.where(c == 0, second, first)


def input_grad(place, dqkv, w):
    return pl.pallas_call(
        input_grad_kernel,
        out_shape=[jax.ShapeDtypeStruct((4, 128, MODEL_WIDTH), bf16)] * 2,
        in_specs=[SM, VM, VM],
        out_specs=[VM] * 2,
        scratch_shapes=[pltpu.VMEM((MODEL_WIDTH, 640), bf16)],
        compiler_params=pltpu.CompilerParams(vmem_limit_bytes=40 * MIB),
        cost_estimate=pl.CostEstimate(flops=3 << 30, bytes_accessed=8 << 20, transcendentals=0),
        name="input_grad",
    )(place, dqkv, w)


def part_of(outer, inner):
    return {0: (0, inner), 1: (1, inner), 2: (2 + inner // 2, inner % 2), 3: (4, inner)}[outer]


def place_kernel(idx, *refs):
    left, right, (query, key, value, aux, out) = refs[:5], refs[5:10], refs[-5:]
    for r in range(16):
        dy, dx = divmod(r, 4)
        rows = pl.ds(pl.multiple_of(idx[r] * 16, 16), 16)
        a, ai = part_of(dy, dx)
        b, bi = part_of(dx, dy)
        total = jnp.zeros((16, 128), f32)
        for f in range(8):
            block = (left[a][ai, f] if f < 4 else right[b][bi, f - 4]).astype(f32)
            query[rows, 512 * f : 512 * f + 512] = block[:, :512]
            to = key if f % 2 == 0 else value
            to[rows, 128 * (f // 2) : 128 * (f // 2) + 128] = block[:, 512:640]
            total = total + block[:, 640:768]
            out_rows = pl.ds(pl.multiple_of(idx[r] * 32 + 16 * (f % 2), 16), 16)
            out[out_rows, 512 * (f // 2) : 512 * (f // 2) + 512] = block[:, 768:]
        aux[rows] = total


def place_rows(idx, left, right, *events):
    shapes = [(256, 4096), (256, 512), (256, 512), (256, 128), (512, MODEL_WIDTH)]
    return pl.pallas_call(
        place_kernel,
        out_shape=[jax.ShapeDtypeStruct(s, f32) for s in shapes],
        in_specs=[SM] + [VM] * 10 + [ANY] * len(events),
        out_specs=[VM] * 5,
        compiler_params=pltpu.CompilerParams(vmem_limit_bytes=40 * MIB),
        cost_estimate=pl.CostEstimate(flops=0, bytes_accessed=16 << 20, transcendentals=0),
        name="place_rows",
    )(idx, *left, *right, *events)


def nothing(*refs):
    pass


def after(values, *events):
    n = len(values)
    return pl.pallas_call(
        nothing,
        out_shape=[jax.ShapeDtypeStruct(v.shape, v.dtype) for v in values],
        in_specs=[ANY] * (n + len(events)),
        out_specs=[ANY] * n,
        input_output_aliases={i: i for i in range(n)},
        cost_estimate=pl.CostEstimate(flops=0, bytes_accessed=0, transcendentals=0),
        name="after",
    )(*values, *events)


def local(
    layer_input, routes, cotangent, attn_gain, query_gain, key_gain, mlp_gain,
    w_query, key_weight, value_weight, w_out, w_router, w_gate, w_up, w_down,
):
    core = lax.axis_index(C)
    py, px = lax.axis_index(Y), lax.axis_index(X)
    zc = jnp.stack([lax.axis_index(Z), core, py, px]).astype(jnp.int32)
    ahead = jnp.arange(16, dtype=jnp.int32)
    idx = (py + ahead // 4) % 4 * 4 + (px + ahead % 4) % 4
    residual = layer_input[0].astype(f32)
    dy_low = cotangent[0]
    upstream = dy_low.astype(f32)
    scale_one = inv_rms(residual)
    normed_one = residual * scale_one
    h1 = (normed_one * attn_gain).astype(bf16)
    beside = jnp.pad(w_router.reshape(128, 64), ((0, 0), (0, 64)))
    h1 = jnp.concatenate([h1, beside], axis=1)
    seq = 1024
    cosine, sine = rope_tables(jnp.arange(seq).astype(f32))
    sign = jnp.where(jnp.arange(HEAD_SIZE) < HEAD_SIZE // 2, -1.0, 1.0).astype(f32)
    signed = sine * sign
    ids = jnp.arange(EXPERTS, dtype=jnp.int32)
    chosen = jnp.any(routes[0][:, :, None] == ids, axis=1)
    before = jnp.tril(jnp.ones((128, 128), bf16), -1)
    rank = dot(before, chosen.astype(bf16)).astype(jnp.int32)
    slot = jnp.where(chosen, rank, -1).T.reshape(16, 2, 128).transpose(1, 0, 2)
    picks = (slot[:, :, None, :] == jnp.arange(CAP)[:, None]).reshape(2, 640, 128)

    def sent(e, v):
        packed = dot(picks[e].astype(bf16), v).astype(bf16)
        return packed.reshape(16, CAP, MODEL_WIDTH)

    def exchanged(v):
        return lax.all_to_all(v, EXPERT, 0, 0, tiled=True)

    dy_all = lax.all_gather(dy_low, EXPERT, axis=0, tiled=False)
    tokens = jnp.arange(128, dtype=jnp.int32)
    slot_token = jnp.max(jnp.where(picks, tokens, -1), axis=-1).reshape(2, 16, CAP).transpose(1, 0, 2)
    slot_token = exchanged(slot_token.astype(f32)).astype(jnp.int32)
    taken = (slot_token.transpose(1, 0, 2)[..., None] == tokens).astype(bf16)
    dys = [es("sct,std->scd", taken[e], dy_all).astype(bf16).reshape(640, MODEL_WIDTH) for e in range(2)]
    in_own = jnp.concatenate([w_gate, w_up])
    rows = w_query.shape[0]

    def per_head(w, n):
        return jnp.repeat(w.reshape(rows, 4, 128), 2, axis=1) if n == 2 else w.reshape(rows, 8, 512)

    blocks = jnp.concatenate([per_head(w_query, 1), per_head(key_weight, 2), per_head(value_weight, 2)], axis=2)
    blocks = blocks.reshape(2, 128, 8, 768)
    halved = jnp.concatenate(
        [
            jnp.where(px % 2 == 0, blocks[0, :, :, :384], blocks[1, :, :, :384]),
            jnp.where(py % 2 == 0, blocks[0, :, :, 384:], blocks[1, :, :, 384:]),
        ],
        axis=2,
    ).transpose(1, 0, 2)
    halved = halved.reshape(4, 2, 128, 768)
    halved = jnp.where(core == 0, halved, halved[:, ::-1])
    place_z = lax.axis_index(Z)

    def meant_for(ahead):
        return lax.dynamic_index_in_dim(halved, (place_z + ahead) % 4, 0, keepdims=False)

    arrived = [shift(meant_for(d), Z, d) for d in range(1, 4)]
    h1_pieces = gather_fsdp(h1, lambda up, down: after([up, down], *arrived, slot_token, cosine, signed, in_own))
    arrived = jnp.stack([meant_for(0)] + arrived, axis=1)
    arrived = jnp.concatenate([arrived[0], shift(arrived[1], C, 1)])
    swap = [(0, 1), (1, 0), (2, 3), (3, 2)]
    w_parts = [
        arrived, lax.ppermute(arrived[:, :, :384], X, swap), lax.ppermute(arrived[:, :, 384:], Y, swap)
    ]
    in_own, down_own = after(
        [in_own, w_down], arrived, h1_pieces[4][0], h1_pieces[5][0]
    )
    in_all = lax.all_gather(in_own, FSDP, axis=1, tiled=True)
    down_all = lax.all_gather(down_own, FSDP, axis=1, tiled=True)
    w, h1_all, q_raw, k_raw, v_b, q_b, k_b, a_b, lse, keep, send = attention_forward(
        h1_pieces, w_parts, zc, w_out, query_gain[None], key_gain[None], cosine, signed
    )
    router = h1_all[:, MODEL_WIDTH : MODEL_WIDTH + 64].reshape(MODEL_WIDTH, EXPERTS)
    w = w.reshape(MODEL_WIDTH, 768)
    attn = scatter_fsdp(keep, send)
    resid_two = residual + attn
    scale_two = inv_rms(resid_two)
    normed_two = resid_two * scale_two
    h2 = (normed_two * mlp_gain).astype(bf16)
    xs_first = exchanged(sent(0, h2))
    logits = jnp.where(chosen, dot(h2, router), -1e30)
    powers = jnp.where(chosen, jnp.exp(logits - jnp.max(logits, axis=-1, keepdims=True)), 0.0)
    gates = powers / jnp.sum(powers, axis=-1, keepdims=True)
    gates_slot = gates.T.reshape(16, 2, 128).transpose(1, 0, 2)
    weighted = jnp.where(picks.reshape(2, 16, CAP, 128), gates_slot[:, :, None, :], 0.0)
    slot_gate = jnp.sum(weighted, axis=-1)
    high = slot_gate.astype(bf16)
    low = (slot_gate - high.astype(f32)).astype(bf16)
    beside = jnp.stack([high[0], low[0], high[1], low[1]], axis=-1)
    beside = jnp.pad(beside, ((0, 0), (0, 0), (0, 124)))
    second = jnp.concatenate([sent(1, h2), beside], axis=-1)
    (second,) = after([second], xs_first)
    xs_second = exchanged(second)
    xs = [xs_first.reshape(640, MODEL_WIDTH), xs_second.reshape(640, MODEL_WIDTH + 128)]
    back_first, *kept_first = expert_rows(0, xs[0], dys[0], in_all, down_all)
    wide = (16, CAP, MODEL_WIDTH + 128)
    (back_first,) = after([back_first.reshape(wide)], xs_second)
    from_first = exchanged(back_first)
    back_second, *kept_second = expert_rows(1, xs[1], dys[1], in_all, down_all)
    (back_second,) = after([back_second.reshape(wide)], from_first)
    from_second = exchanged(back_second)
    got = xs[1][:, MODEL_WIDTH : MODEL_WIDTH + 4].astype(f32)
    slot_gate = [jnp.broadcast_to(got[:, 2 * e : 2 * e + 1] + got[:, 2 * e + 1 : 2 * e + 2], (640, 128)) for e in range(2)]
    weighted = weighted.reshape(2, 640, 128).astype(bf16)

    def combined(parts):
        return sum(es("rt,rd->td", weighted[e], parts[e].reshape(640, -1)[:, :MODEL_WIDTH]) for e in range(2))

    kept = [
        (xs[e], dys[e], *kept, slot_gate[e]) for e, kept in enumerate((kept_first, kept_second))
    ]
    grad_gate, grad_up, grad_down, *ys = weight_grads([*kept[0], *kept[1]], down_all, from_first)
    grad_gate, grad_up, grad_down = after([grad_gate, grad_up, grad_down], from_second)
    (from_second,) = after([from_second], ys[0])
    backs = [from_first, from_second]
    dh_sum = combined(backs)
    dgate = [v.reshape(640, -1)[:, MODEL_WIDTH : MODEL_WIDTH + 2].astype(f32).sum(axis=1) for v in backs]
    dgate = jnp.stack(dgate).reshape(2, 16, CAP, 1)
    dgate = jnp.sum(jnp.where(picks.reshape(2, 16, CAP, 128), dgate, 0.0), axis=2)
    dgate = dgate.transpose(2, 1, 0).reshape(128, EXPERTS)
    dl = (gates * (dgate - jnp.sum(gates * dgate, axis=-1, keepdims=True))).astype(bf16)
    dh2 = es("te,de->td", dl, router) + dh_sum
    dx2 = upstream + norm_back(dh2 * mlp_gain, normed_two, scale_two)
    da = dx2.astype(bf16)
    y_first, y_second = (v.reshape(16, CAP, MODEL_WIDTH) for v in ys)
    y_first = exchanged(y_first)
    da_pieces = gather_fsdp(da, lambda up, down: after([up, down], y_first))
    (y_second,) = after([y_second], da_pieces[2][0])
    y_second = exchanged(y_second)
    output = (resid_two + combined([y_first, y_second])).astype(bf16)
    aux = jnp.pad(es("td,te->de", h2, dl), ((0, 0), (0, 128 - EXPERTS)))
    grad_mlp_gain = jnp.sum(dh2 * normed_two, axis=0)
    def scattered(v):
        return lax.psum_scatter(v, FSDP, scatter_dimension=1, tiled=True)

    def summed(v):
        return jnp.sum(exchanged(v).astype(f32), axis=0).astype(bf16)

    grad_gate, grad_up, grad_down = scattered(grad_gate), scattered(grad_up), scattered(grad_down)
    dob, out_shares = out_back(da_pieces, zc, w_out, a_b)
    (out_shares,) = after([out_shares.reshape(16, 32, MODEL_WIDTH)], y_second)
    grad_out = summed(out_shares)
    dq_raw, dkv, q_part = attention_backward(
        dob, a_b, q_b, k_b, v_b, lse, q_raw, query_gain[None], cosine, signed
    )
    shares, dqkv, along, k_part = projection_grads(
        zc, dq_raw, dkv, shift(dkv, C, 1), k_raw, q_part, key_gain[None], cosine, signed, h1_all, w, aux,
        grad_out,
    )
    keep, send = input_grad(zc, dqkv, w)
    dh1 = scatter_fsdp(keep, send)
    gains = jnp.concatenate([along[:, 0], grad_mlp_gain, q_part[0], k_part[0]]).reshape(34, 128)
    gains = sum_all(gains).reshape(-1)
    (shares,) = after([summed(shares).reshape(8, 16, 768)], dh1)
    parted = lax.all_to_all(shares, FSDP, 0, 0, tiled=True)
    grad_out = grad_out.reshape(2, 16, 4, 512).transpose(2, 0, 1, 3).reshape(8, 16, 512)
    parted = jnp.concatenate([parted, grad_out], axis=2)
    grad_input = dx2 + norm_back(dh1 * attn_gain, normed_one, scale_one)
    expert_grads = [v.astype(f32) for v in (grad_gate, grad_up, grad_down)]
    grad_query, grad_key, grad_value, aux, grad_out = place_rows(
        idx, *gather_plane(parted[:4], parted[4:]), gains, *expert_grads
    )
    return (
        output[None],
        grad_input.astype(bf16)[None],
        gains[:MODEL_WIDTH] / attn_gain,
        gains[2 * MODEL_WIDTH : 2 * MODEL_WIDTH + HEAD_SIZE],
        gains[2 * MODEL_WIDTH + HEAD_SIZE :],
        gains[MODEL_WIDTH : 2 * MODEL_WIDTH],
        grad_query,
        grad_key,
        grad_value,
        grad_out,
        aux[:, :EXPERTS],
        *expert_grads,
    )


def solution(mesh):
    torus = Mesh(mesh.devices.reshape(4, 2, 4, 4), ALL)
    tokens, rows, experts = P(EXPERT, FSDP, None), P(FSDP, None), P(EXPERT, FSDP, None)
    return jax.shard_map(
        local,
        mesh=torus,
        in_specs=(tokens,) * 3 + (P(),) * 4 + (rows,) * 5 + (experts,) * 3,
        out_specs=(tokens,) * 2 + (P(),) * 4 + (rows,) * 5 + (experts,) * 3,
        check_vma=False,
    )
```

```python
import functools

import jax
import jax.numpy as jnp
from jax import lax
from jax.experimental import pallas as pl
from jax.experimental.pallas import tpu as pltpu
from jax.sharding import Mesh
from jax.sharding import PartitionSpec as P

MODEL_WIDTH = 2048
QUERY_HEADS = 32
KEY_VALUE_HEADS = 4
HEAD_SIZE = 128
TOPK = 8
EXPERTS = 32
CAP = 40
Z, C, Y, X = "z", "c", "y", "x"
FSDP = (Z, C)
EXPERT = (Y, X)
ALL = (Z, C, Y, X)

bf16 = jnp.bfloat16
f32 = jnp.float32
epsilon = 1e-06
rope_base = 1000000.0


def dot(a, b):
    return jnp.dot(a, b, preferred_element_type=f32)


def es(spec, a, b):
    return jnp.einsum(spec, a, b, preferred_element_type=f32)


def shift(v, axis, by):
    n = 2 if axis == C else 4
    return lax.ppermute(v, axis, [(i, (i + by) % n) for i in range(n)])


def gather_fsdp(p, join=lambda *values: values):
    half = p.shape[0] // 2
    up, down = join(shift(p, Z, -1), shift(p, Z, 1))
    other = shift(p, C, 1)
    far_low, far_high = shift(down[:half], Z, 1), shift(up[half:], Z, -1)
    far = [(up, 1, 0), (down, 3, 0), (far_low, 2, 0), (far_high, 2, half)]
    return (
        [(p, 0, 0, 0), (other, 0, 1, 0)]
        + [(a, dz, 0, r) for a, dz, r in far]
        + [(shift(a, C, 1), dz, 1, r) for a, dz, r in far]
    )


def scatter_fsdp(keep, send, join=lambda *values: values):
    got = shift(send, C, 1)
    half = keep.shape[1] // 2

    def both(d, rows=slice(None)):
        return (keep[d, rows].astype(f32) + got[d, rows].astype(f32)).astype(bf16)

    low, high = slice(None, half), slice(half, None)
    far_low, far_high = both(2, low), both(2, high)
    from_down, from_up = shift(far_low, Z, 1), shift(far_high, Z, -1)
    one, three = both(1), both(3)
    one = jnp.concatenate([(one[low].astype(f32) + from_down.astype(f32)).astype(bf16), one[high]])
    three = jnp.concatenate([three[low], (three[high].astype(f32) + from_up.astype(f32)).astype(bf16)])
    one, three = join(one, three)
    from_down, from_up = shift(one, Z, 1), shift(three, Z, -1)
    own = keep[0].astype(f32) + got[0].astype(f32)
    return own + from_down.astype(f32) + from_up.astype(f32)


def gather_ring(v, axis):
    half = v.shape[0] // 2
    up, down = shift(v, axis, -1), shift(v, axis, 1)
    return v, up, shift(down[:half], axis, 1), shift(up[half:], axis, -1), down


def scatter_ring(parts, axis):
    own, one, low, high, three = parts
    k = low.shape[0]
    down, up = shift(low, axis, 1), shift(high, axis, -1)
    first = down

    def plus(a, b):
        return (a.astype(f32) + b.astype(f32)).astype(bf16)

    one = jnp.concatenate([plus(one[:k], down), one[k:]])
    three = jnp.concatenate([three[:k], plus(three[k:], up)])
    down, up = shift(one, axis, 1), shift(three, axis, -1)
    return own.astype(f32) + down.astype(f32) + up.astype(f32), first


def scatter_plane(left, right):
    def halves(v):
        v = v.astype(bf16)
        k = v.shape[1] // 2
        return v[0], v[1], v[2, :k], v[2, k:], v[3]

    left, first = scatter_ring(left, Y)
    right, _ = scatter_ring(right, X)
    return scatter_ring(halves(left), X)[0], scatter_ring(halves(right), Y)[0], first


def inv_rms(values):
    return lax.rsqrt(jnp.mean(values * values, axis=-1, keepdims=True) + epsilon)


def norm_back(grad_norm, normed, scale_part):
    return scale_part * (grad_norm - normed * jnp.mean(grad_norm * normed, axis=-1, keepdims=True))


def rope_tables(positions):
    frequency = rope_base ** (-(jnp.arange(HEAD_SIZE // 2).astype(f32) * 2.0 / HEAD_SIZE))
    frequency = jnp.concatenate([frequency, frequency])
    angles = positions[:, None] * frequency[None, :]
    return jnp.cos(angles), jnp.sin(angles)


def mm(a, b, dims=((1,), (0,))):
    return lax.dot_general(a, b, (dims, ((), ())), preferred_element_type=f32)


NT = ((1,), (1,))
TN = ((0,), (0,))
ANY = pl.BlockSpec(memory_space=pl.ANY)
VM = pl.BlockSpec(memory_space=pltpu.VMEM)
SM = pl.BlockSpec(memory_space=pltpu.SMEM)
MIB = 1 << 20


def load_pieces(place, spec, pieces, whole, sems):
    copies = []
    for k, (dz, dc, first, rows) in enumerate(spec):
        at = lax.rem(place[0] + dz, 4) * 256 + lax.rem(place[1] + dc, 2) * 128 + first
        at = pl.multiple_of(at, 64)
        copies.append(pltpu.make_async_copy(pieces[k], whole.at[pl.ds(at, rows)], sems.at[k]))
    for copy in copies:
        copy.start()
    return copies


def load_weights(place, parts, w, sems):
    copies = []
    for k in range(8):
        source = lax.rem(place[0] + 4 - k % 4, 4) * 2 + lax.rem(place[1] + k // 4, 2)
        rows = pl.ds(pl.multiple_of(source * 256, 256), 256)
        piece = parts[k].at[0] if k < 4 else parts[4].at[k - 4]
        copies.append(pltpu.make_async_copy(piece, w.at[rows], sems.at[k]))
    for copy in copies:
        copy.start()
    return copies


def attention_kernel(spec, place, w_out, q_gain, k_gain, cosine, sine, *rest):
    n = len(spec)
    pieces, parts, rest = rest[:n], rest[n : n + 5], rest[n + 5 :]
    w, h1, q_raw, k_raw, v_b, q_b, k_b, a_b, lse, keep, send, sems, w_sems = rest
    z, c = place[0], place[1]
    copies = load_weights(place, parts, w, w_sems)
    for copy in load_pieces(place, spec, pieces, h1, sems) + copies:
        copy.wait()

    @pl.loop(0, 4)
    def _(i):
        rows = pl.ds(pl.multiple_of(i * 256, 256), 256)
        t = mm(h1[rows, :MODEL_WIDTH], w[...])
        q_raw[rows] = t[:, :512]
        k_raw[rows] = t[:, 512:640]
        v_b[rows] = t[:, 640:].astype(bf16)
        co, si = cosine[rows], sine[rows]

        def rotated(u, gain):
            u = u * lax.rsqrt(jnp.mean(u * u, axis=-1, keepdims=True) + epsilon) * gain
            return (u * co + pltpu.roll(u, 64, 1) * si).astype(bf16)

        for h in range(4):
            q_b[h, rows] = rotated(t[:, 128 * h : 128 * h + 128], q_gain[...])
        k_b[rows] = rotated(t[:, 512:640], k_gain[...])

    lane = lax.broadcasted_iota(jnp.int32, (256, 128), 1)
    below = lax.broadcasted_iota(jnp.int32, (256, 256), 0) >= lax.broadcasted_iota(
        jnp.int32, (256, 256), 1
    )
    for i in range(4):
        n_keys = 256 * (i + 1)
        rows = slice(256 * i, n_keys)
        logs = jnp.zeros((256, 128), f32)
        for h in range(4):
            s = mm(q_b[h, rows], k_b[:n_keys], NT) * (HEAD_SIZE**-0.5)
            e = jnp.exp(s)
            tail = jnp.where(below, e[:, n_keys - 256 :], 0.0)
            e = tail if i == 0 else jnp.concatenate([e[:, : n_keys - 256], tail], axis=1)
            total = jnp.sum(e, axis=1, keepdims=True)
            a = mm(e.astype(bf16), v_b[:n_keys]) / total
            a_b[rows, 128 * h : 128 * h + 128] = a.astype(bf16)
            logs = jnp.where(lane == h, jnp.log(total), logs)
        lse[rows] = logs
        part = mm(a_b[rows], w_out[...]).astype(bf16)
        dz = lax.rem(i - z + 4, 4)
        first, second = part[:128], part[128:]
        keep[dz] = jnp.where(c == 0, first, second)
        send[dz] = jnp.where(c == 0, second, first)


def attention_forward(pieces, parts, place, w_out, q_gain, k_gain, cosine, sine):
    spec = [(dz, dc, first, a.shape[0]) for a, dz, dc, first in pieces]
    seq = 1024
    shapes = [
        ((MODEL_WIDTH, 768), bf16),
        ((seq, MODEL_WIDTH + 128), bf16),
        ((seq, 512), f32),
        ((seq, 128), f32),
        ((seq, 128), bf16),
        ((4, seq, 128), bf16),
        ((seq, 128), bf16),
        ((seq, 512), bf16),
        ((seq, 128), f32),
        ((4, 128, MODEL_WIDTH), bf16),
        ((4, 128, MODEL_WIDTH), bf16),
    ]
    return pl.pallas_call(
        functools.partial(attention_kernel, spec),
        out_shape=[jax.ShapeDtypeStruct(*s) for s in shapes],
        in_specs=[SM] + [VM] * 5 + [ANY] * (len(spec) + 5),
        out_specs=[VM] * len(shapes),
        scratch_shapes=[pltpu.SemaphoreType.DMA((len(spec),)), pltpu.SemaphoreType.DMA((8,))],
        compiler_params=pltpu.CompilerParams(vmem_limit_bytes=56 * MIB),
        cost_estimate=pl.CostEstimate(flops=9 << 30, bytes_accessed=28 << 20, transcendentals=3 << 20),
        name="attention_forward",
    )(place, w_out, q_gain, k_gain, cosine, sine, *[p[0] for p in pieces], *parts)


def expert_kernel(e, xs_in, dys_in, w_in, w_down, back, hid, dg, du, xs, dys, wg, wu, wd, sems):
    loads = []
    for k, (source, into) in enumerate(
        (
            (xs_in.at[:, pl.ds(0, MODEL_WIDTH)], xs), (w_in.at[e], wg), (w_in.at[2 + e], wu), (dys_in, dys), (w_down.at[e], wd),
        )
    ):
        loads.append(pltpu.make_async_copy(source, into, sems.at[k]))
        loads[-1].start()
    total = jnp.zeros((640, 1), f32)
    for k in range(3):
        loads[k].wait()
    for i in range(3):
        cols = slice(256 * i, 256 * i + 256)
        g, u = mm(xs[...], wg[:, cols]), mm(xs[...], wu[:, cols])
        if i == 0:
            loads[3].wait()
            loads[4].wait()
        d = mm(dys[...], wd[cols], NT)
        sig = 0.5 + 0.5 * jnp.tanh(0.5 * g)
        act = g * sig
        h = act * u
        total = total + jnp.sum(d * h, axis=1, keepdims=True)
        hid[:, cols] = h.astype(bf16)
        du[:, cols] = (d * act).astype(bf16)
        dg[:, cols] = (d * u * (sig + act * (1.0 - sig))).astype(bf16)
    back[:, :MODEL_WIDTH] = (mm(dg[...], wg[...], NT) + mm(du[...], wu[...], NT)).astype(bf16)
    high = total.astype(bf16).astype(f32)
    lane = lax.broadcasted_iota(jnp.int32, (640, 128), 1)
    back[:, MODEL_WIDTH:] = jnp.where(lane == 0, high, jnp.where(lane == 1, total - high, 0.0)).astype(bf16)


def expert_rows(e, xs, dys, w_in, w_down):
    row, act = (640, MODEL_WIDTH), (640, 768)
    scratch = [row, row, (MODEL_WIDTH, 768), (MODEL_WIDTH, 768), (768, MODEL_WIDTH)]
    return pl.pallas_call(
        functools.partial(expert_kernel, e),
        out_shape=[jax.ShapeDtypeStruct(s, bf16) for s in ((640, MODEL_WIDTH + 128), act, act, act)],
        in_specs=[ANY] * 4,
        out_specs=[VM] * 4,
        scratch_shapes=[pltpu.VMEM(s, bf16) for s in scratch] + [pltpu.SemaphoreType.DMA((5,))],
        compiler_params=pltpu.CompilerParams(vmem_limit_bytes=48 * MIB),
        cost_estimate=pl.CostEstimate(flops=10 << 30, bytes_accessed=20 << 20, transcendentals=1 << 20),
        name="expert_rows",
    )(xs, dys, w_in, w_down)


def weight_grads_kernel(*refs):
    rows, w_down, grads, ys = refs[:12], refs[12], refs[14:17], refs[17]
    first = pl.program_id(0) == 0
    for e in range(2):
        xs, dys, hid, dg, du, gate = rows[6 * e : 6 * e + 6]

        @pl.when(first if e == 0 else jnp.logical_not(first))
        def _(e=e, xs=xs, dys=dys, hid=hid, dg=dg, du=du, gate=gate):
            s = gate[:, 0:1]

            def scaled(v):
                return (v[...].astype(f32) * s).astype(bf16)

            y = mm(hid[...], w_down[0])
            for o in range(16):
                ys[o, CAP * e : CAP * e + CAP] = y[CAP * o : CAP * o + CAP].astype(bf16)
            grads[0][0] = mm(xs[:, :MODEL_WIDTH], scaled(dg), TN).astype(bf16)
            grads[1][0] = mm(xs[:, :MODEL_WIDTH], scaled(du), TN).astype(bf16)
            grads[2][0] = mm(scaled(hid), dys[...], TN).astype(bf16)


def weight_grads(rows, w_down, event):
    def per_expert(*dims):
        return pl.BlockSpec((1, *dims), lambda e: (e, 0, 0))

    sizes = [(MODEL_WIDTH, 768), (MODEL_WIDTH, 768), (768, MODEL_WIDTH)]
    return pl.pallas_call(
        weight_grads_kernel,
        grid=(2,),
        out_shape=[jax.ShapeDtypeStruct((2, *s), bf16) for s in sizes]
        + [jax.ShapeDtypeStruct((16, 2 * CAP, MODEL_WIDTH), bf16)],
        in_specs=[VM] * 12 + [per_expert(768, MODEL_WIDTH), ANY],
        out_specs=[per_expert(*s) for s in sizes] + [VM],
        compiler_params=pltpu.CompilerParams(vmem_limit_bytes=60 * MIB),
        cost_estimate=pl.CostEstimate(flops=16 << 30, bytes_accessed=48 << 20, transcendentals=0),
        name="weight_grads",
    )(*rows, w_down, event)


def out_back_kernel(spec, place, w_out, a_b, *rest):
    n = len(spec)
    pieces, (dob, shares, da, sems) = rest[:n], rest[n:]
    for copy in load_pieces(place, spec, pieces, da, sems):
        copy.wait()

    @pl.loop(0, 4)
    def _(i):
        rows = pl.ds(pl.multiple_of(i * 256, 256), 256)
        dob[rows] = mm(da[rows], w_out[...], NT).astype(bf16)

    for h in range(4):
        grads = mm(a_b[:, 128 * h : 128 * h + 128], da[...], TN).astype(bf16)
        for r in range(4):
            for k in range(4):
                block = grads[32 * r : 32 * r + 32, 512 * k : 512 * k + 512]
                shares[4 * h + r, 32 * k : 32 * k + 32] = block


def out_back(pieces, place, w_out, a_b):
    spec = [(dz, dc, first, a.shape[0]) for a, dz, dc, first in pieces]
    shapes = [((1024, 512), bf16), ((16, 128, 512), bf16)]
    return pl.pallas_call(
        functools.partial(out_back_kernel, spec),
        out_shape=[jax.ShapeDtypeStruct(*s) for s in shapes],
        in_specs=[SM] + [VM] * 2 + [ANY] * len(spec),
        out_specs=[VM] * 2,
        scratch_shapes=[pltpu.VMEM((1024, MODEL_WIDTH), bf16), pltpu.SemaphoreType.DMA((len(spec),))],
        compiler_params=pltpu.CompilerParams(vmem_limit_bytes=40 * MIB),
        cost_estimate=pl.CostEstimate(flops=5 << 30, bytes_accessed=12 << 20, transcendentals=0),
        name="out_back",
    )(place, w_out, a_b, *[p[0] for p in pieces])


def attention_back_kernel(dob, a_b, q_b, k_b, v_b, lse, q_raw, q_gain, cosine, sine, dq_raw, dkv, gain):
    root = HEAD_SIZE**-0.5
    below = lax.broadcasted_iota(jnp.int32, (256, 256), 0) >= lax.broadcasted_iota(
        jnp.int32, (256, 256), 1
    )
    dkv[...] = jnp.zeros(dkv.shape, f32)
    total = jnp.zeros((1, HEAD_SIZE), f32)
    for i in range(4):
        keys = 256 * (i + 1)
        rows = slice(256 * i, keys)
        co, si = cosine[rows], sine[rows]
        for h in range(4):
            cols = slice(128 * h, 128 * h + 128)
            q, do = q_b[h, rows], dob[rows, cols]
            p = jnp.exp(mm(q, k_b[:keys], NT) * root - lse[rows, h : h + 1])
            tail = jnp.where(below, p[:, keys - 256 :], 0.0)
            p = tail if i == 0 else jnp.concatenate([p[:, : keys - 256], tail], axis=1)
            dp = mm(do, v_b[:keys], NT)
            mean = jnp.sum(do.astype(f32) * a_b[rows, cols].astype(f32), axis=1, keepdims=True)
            ds = (p * (dp - mean)).astype(bf16)
            dkv[:keys, :128] += mm(ds, q, TN) * root
            dkv[:keys, 128:] += mm(p.astype(bf16), do, TN)
            dq = (mm(ds, k_b[:keys]) * root).astype(bf16).astype(f32)
            dq_in = dq * co + pltpu.roll(dq * si, 64, 1)
            raw = q_raw[rows, cols]
            scale = lax.rsqrt(jnp.mean(raw * raw, axis=-1, keepdims=True) + epsilon)
            hat = raw * scale
            total = total + jnp.sum(dq_in * hat, axis=0, keepdims=True)
            t = dq_in * q_gain[...]
            back = scale * (t - hat * jnp.mean(t * hat, axis=-1, keepdims=True))
            dq_raw[rows, cols] = back.astype(bf16)
    gain[...] = total


def attention_backward(dob, a_b, q_b, k_b, v_b, lse, q_raw, q_gain, cosine, sine):
    shapes = [((1024, 512), bf16), ((1024, 256), f32), ((1, HEAD_SIZE), f32)]
    return pl.pallas_call(
        attention_back_kernel,
        out_shape=[jax.ShapeDtypeStruct(*s) for s in shapes],
        in_specs=[VM] * 10,
        out_specs=[VM] * 3,
        compiler_params=pltpu.CompilerParams(vmem_limit_bytes=48 * MIB),
        cost_estimate=pl.CostEstimate(flops=10 << 30, bytes_accessed=12 << 20, transcendentals=0),
        name="attention_backward",
    )(dob, a_b, q_b, k_b, v_b, lse, q_raw, q_gain, cosine, sine)


def grads_kernel(
    place, idx, dq_raw, own, other, k_raw, q_part, k_gain, cosine, sine, h1, w, aux, out_shares, _, *outs
):
    left, right, (dqkv, along_out, k_part, shares) = outs[:5], outs[5:10], outs[10:]
    c = place[1]
    dqkv[:, :512] = dq_raw[...]
    total = jnp.zeros((1, HEAD_SIZE), f32)
    for i in range(4):
        rows = slice(256 * i, 256 * i + 256)
        both = (own[rows] + other[rows]).astype(bf16)
        dk = both[:, :128].astype(f32)
        dk_in = dk * cosine[rows] + pltpu.roll(dk * sine[rows], 64, 1)
        raw = k_raw[rows]
        scale = lax.rsqrt(jnp.mean(raw * raw, axis=-1, keepdims=True) + epsilon)
        hat = raw * scale
        total = total + jnp.sum(dk_in * hat, axis=0, keepdims=True)
        t = dk_in * k_gain[...]
        grad = scale * (t - hat * jnp.mean(t * hat, axis=-1, keepdims=True))
        dqkv[rows, 512:] = jnp.where(c == 0, grad, both[:, 128:].astype(f32)).astype(bf16)
    k_part[...] = total * 0.5
    for f in range(8):
        shard = slice(256 * f, 256 * f + 256)
        part = mm(h1[:, shard], dqkv[...], TN)
        last = jnp.where(c == 0, w[shard, 512:640], w[shard, 640:])
        along = jnp.sum(part[:, :512] * w[shard, :512].astype(f32), axis=1, keepdims=True)
        along = along + jnp.sum(part[:, 512:] * last.astype(f32), axis=1, keepdims=True)
        along_out[shard] = jnp.broadcast_to(along, (256, 128))
        shares[f, :, :640] = part.astype(bf16)
        shares[f, :, 640:] = aux[shard].astype(bf16)
    for r in range(16):
        dy, dx = divmod(r, 4)
        rows = pl.ds(pl.multiple_of(idx[r] * 16, 16), 16)
        a, ai = part_of(dy, dx)
        b, bi = part_of(dx, dy)
        for f in range(4):
            left[a][ai, 16 * f : 16 * f + 16, :768] = shares[f, rows]
            right[b][bi, 16 * f : 16 * f + 16, :768] = shares[f + 4, rows]
        left[a][ai, :, 768:] = out_shares[idx[r], :64]
        right[b][bi, :, 768:] = out_shares[idx[r], 64:]


def projection_grads(place, idx, dq_raw, own, other, k_raw, q_part, k_gain, cosine, sine, h1, w, aux, out_shares, event):
    shapes = [((n, 64, 1280), bf16) for n in [4, 4, 2, 2, 4] * 2]
    shapes += [((1024, 640), bf16), ((MODEL_WIDTH, 128), f32), ((1, HEAD_SIZE), f32)]
    outs = pl.pallas_call(
        grads_kernel,
        out_shape=[jax.ShapeDtypeStruct(*s) for s in shapes],
        in_specs=[SM, SM] + [VM] * 12 + [ANY],
        out_specs=[VM] * len(shapes),
        scratch_shapes=[pltpu.VMEM((8, 256, 768), bf16)],
        compiler_params=pltpu.CompilerParams(vmem_limit_bytes=52 * MIB),
        cost_estimate=pl.CostEstimate(flops=3 << 30, bytes_accessed=16 << 20, transcendentals=0),
        name="projection_grads",
    )(place, idx, dq_raw, own, other, k_raw, q_part, k_gain, cosine, sine, h1, w, aux, out_shares, event)
    return outs[:5], outs[5:10], *outs[10:]


def input_grad_kernel(place, dqkv, w, _, keep, send, w_own):
    z, c = place[0], place[1]
    w_own[:, :512] = w[:, :512]
    w_own[:, 512:] = jnp.where(c == 0, w[:, 512:640], w[:, 640:])

    @pl.loop(0, 4)
    def _(i):
        rows = pl.ds(pl.multiple_of(i * 256, 256), 256)
        part = mm(dqkv[rows], w_own[...], NT).astype(bf16)
        dz = lax.rem(i - z + 4, 4)
        first, second = part[:128], part[128:]
        keep[dz] = jnp.where(c == 0, first, second)
        send[dz] = jnp.where(c == 0, second, first)


def input_grad(place, dqkv, w, event):
    return pl.pallas_call(
        input_grad_kernel,
        out_shape=[jax.ShapeDtypeStruct((4, 128, MODEL_WIDTH), bf16)] * 2,
        in_specs=[SM, VM, VM, ANY],
        out_specs=[VM] * 2,
        scratch_shapes=[pltpu.VMEM((MODEL_WIDTH, 640), bf16)],
        compiler_params=pltpu.CompilerParams(vmem_limit_bytes=40 * MIB),
        cost_estimate=pl.CostEstimate(flops=3 << 30, bytes_accessed=8 << 20, transcendentals=0),
        name="input_grad",
    )(place, dqkv, w, event)


def part_of(outer, inner):
    return {0: (0, inner), 1: (1, inner), 2: (2 + inner // 2, inner % 2), 3: (4, inner)}[outer]


def place_kernel(parts, *refs):
    query, key, value, aux, gains, out = refs[-6:]
    for r in range(16):
        rows = slice(16 * r, 16 * r + 16)
        total = jnp.zeros((16, 128), f32)
        for f in range(8):
            block = parts[r, f].astype(f32)
            query[rows, 512 * f : 512 * f + 512] = block[:, :512]
            to = key if f % 2 == 0 else value
            to[rows, 128 * (f // 2) : 128 * (f // 2) + 128] = block[:, 512:640]
            total = total + block[:, 640:768]
            gains[f] = block[:, 640:768] if r == 0 else gains[f] + block[:, 640:768]
            first = 32 * r + 16 * (f % 2)
            out[first : first + 16, 512 * (f // 2) : 512 * (f // 2) + 512] = block[:, 768:]
        aux[rows] = total


def place_rows(parts, *events):
    shapes = [(256, 4096), (256, 512), (256, 512), (256, 128), (8, 16, 128), (512, MODEL_WIDTH)]
    return pl.pallas_call(
        place_kernel,
        out_shape=[jax.ShapeDtypeStruct(s, f32) for s in shapes],
        in_specs=[VM] + [ANY] * len(events),
        out_specs=[VM] * 6,
        compiler_params=pltpu.CompilerParams(vmem_limit_bytes=40 * MIB),
        cost_estimate=pl.CostEstimate(flops=0, bytes_accessed=16 << 20, transcendentals=0),
        name="place_rows",
    )(parts, *events)


def nothing(*refs):
    pass


def after(values, *events):
    n = len(values)
    return pl.pallas_call(
        nothing,
        out_shape=[jax.ShapeDtypeStruct(v.shape, v.dtype) for v in values],
        in_specs=[ANY] * (n + len(events)),
        out_specs=[ANY] * n,
        input_output_aliases={i: i for i in range(n)},
        cost_estimate=pl.CostEstimate(flops=0, bytes_accessed=0, transcendentals=0),
        name="after",
    )(*values, *events)


def local(
    layer_input, routes, cotangent, attn_gain, query_gain, key_gain, mlp_gain,
    w_query, key_weight, value_weight, w_out, w_router, w_gate, w_up, w_down,
):
    core = lax.axis_index(C)
    py, px = lax.axis_index(Y), lax.axis_index(X)
    zc = jnp.stack([lax.axis_index(Z), core, py, px]).astype(jnp.int32)
    ahead = jnp.arange(16, dtype=jnp.int32)
    idx = (py + ahead // 4) % 4 * 4 + (px + ahead % 4) % 4
    residual = layer_input[0].astype(f32)
    dy_low = cotangent[0]
    upstream = dy_low.astype(f32)
    scale_one = inv_rms(residual)
    normed_one = residual * scale_one
    h1 = (normed_one * attn_gain).astype(bf16)
    beside = jnp.pad(w_router.reshape(128, 64), ((0, 0), (0, 64)))
    h1 = jnp.concatenate([h1, beside], axis=1)
    seq = 1024
    cosine, sine = rope_tables(jnp.arange(seq).astype(f32))
    sign = jnp.where(jnp.arange(HEAD_SIZE) < HEAD_SIZE // 2, -1.0, 1.0).astype(f32)
    signed = sine * sign
    ids = jnp.arange(EXPERTS, dtype=jnp.int32)
    chosen = jnp.any(routes[0][:, :, None] == ids, axis=1)
    before = jnp.tril(jnp.ones((128, 128), bf16), -1)
    rank = dot(before, chosen.astype(bf16)).astype(jnp.int32)
    slot = jnp.where(chosen, rank, -1).T.reshape(16, 2, 128).transpose(1, 0, 2)
    picks = (slot[:, :, None, :] == jnp.arange(CAP)[:, None]).reshape(2, 640, 128)

    def sent(e, v):
        packed = dot(picks[e].astype(bf16), v).astype(bf16)
        return packed.reshape(16, CAP, MODEL_WIDTH)

    def exchanged(v):
        return lax.all_to_all(v, EXPERT, 0, 0, tiled=True)

    dy_all = lax.all_gather(dy_low, EXPERT, axis=0, tiled=False)
    tokens = jnp.arange(128, dtype=jnp.int32)
    slot_token = jnp.max(jnp.where(picks, tokens, -1), axis=-1).reshape(2, 16, CAP)
    in_own = jnp.concatenate([w_gate, w_up])
    rows = w_query.shape[0]

    def per_head(w, n):
        return jnp.repeat(w.reshape(rows, 4, 128), 2, axis=1) if n == 2 else w.reshape(rows, 8, 512)

    blocks = jnp.concatenate([per_head(w_query, 1), per_head(key_weight, 2), per_head(value_weight, 2)], axis=2)
    blocks = blocks.transpose(1, 0, 2).reshape(4, 2, rows, 768)
    blocks = jnp.where(core == 0, blocks, blocks[:, ::-1])
    place_z = lax.axis_index(Z)

    def meant_for(ahead):
        return lax.dynamic_index_in_dim(blocks, (place_z + ahead) % 4, 0, keepdims=False)

    w_parts = [meant_for(0)] + [shift(meant_for(d), Z, d) for d in range(1, 4)]
    h1_pieces = gather_fsdp(h1, lambda up, down: after([up, down], cosine, signed, in_own, *w_parts[1:]))
    from_other = shift(jnp.stack([v[1] for v in w_parts]), C, 1)
    in_own, down_own = after(
        [in_own, w_down], *w_parts[1:], h1_pieces[4][0], h1_pieces[5][0]
    )
    in_all = lax.all_gather(in_own, FSDP, axis=1, tiled=True)
    down_all = lax.all_gather(down_own, FSDP, axis=1, tiled=True)
    w, h1_all, q_raw, k_raw, v_b, q_b, k_b, a_b, lse, keep, send = attention_forward(
        h1_pieces, [*w_parts, from_other], zc, w_out, query_gain[None], key_gain[None], cosine, signed
    )
    router = h1_all[:, MODEL_WIDTH : MODEL_WIDTH + 64].reshape(MODEL_WIDTH, EXPERTS)
    attn = scatter_fsdp(keep, send)
    resid_two = residual + attn
    scale_two = inv_rms(resid_two)
    normed_two = resid_two * scale_two
    h2 = (normed_two * mlp_gain).astype(bf16)
    beside = jnp.pad(jnp.stack([slot_token[0], slot_token[1]], axis=-1).astype(bf16), ((0, 0), (0, 0), (0, 126)))
    xs_first = exchanged(jnp.concatenate([sent(0, h2), beside], axis=-1))
    slot_token = xs_first[:, :, MODEL_WIDTH : MODEL_WIDTH + 2].astype(jnp.int32)
    taken = (slot_token[..., None] == tokens).astype(bf16)
    dys = [es("sct,std->scd", taken[:, :, e], dy_all).astype(bf16).reshape(640, MODEL_WIDTH) for e in range(2)]
    logits = jnp.where(chosen, dot(h2, router), -1e30)
    powers = jnp.where(chosen, jnp.exp(logits - jnp.max(logits, axis=-1, keepdims=True)), 0.0)
    gates = powers / jnp.sum(powers, axis=-1, keepdims=True)
    gates_slot = gates.T.reshape(16, 2, 128).transpose(1, 0, 2)
    weighted = jnp.where(picks.reshape(2, 16, CAP, 128), gates_slot[:, :, None, :], 0.0)
    slot_gate = jnp.sum(weighted, axis=-1)
    high = slot_gate.astype(bf16)
    low = (slot_gate - high.astype(f32)).astype(bf16)
    beside = jnp.stack([high[0], low[0], high[1], low[1]], axis=-1)
    beside = jnp.pad(beside, ((0, 0), (0, 0), (0, 124)))
    second = jnp.concatenate([sent(1, h2), beside], axis=-1)
    (second,) = after([second], xs_first)
    xs_second = exchanged(second)
    xs = [v.reshape(640, MODEL_WIDTH + 128) for v in (xs_first, xs_second)]
    back_first, *kept_first = expert_rows(0, xs[0], dys[0], in_all, down_all)
    wide = (16, CAP, MODEL_WIDTH + 128)
    (back_first,) = after([back_first.reshape(wide)], xs_second)
    from_first = exchanged(back_first)
    back_second, *kept_second = expert_rows(1, xs[1], dys[1], in_all, down_all)
    (back_second,) = after([back_second.reshape(wide)], from_first)
    from_second = exchanged(back_second)
    got = xs[1][:, MODEL_WIDTH : MODEL_WIDTH + 4].astype(f32)
    slot_gate = [jnp.broadcast_to(got[:, 2 * e : 2 * e + 1] + got[:, 2 * e + 1 : 2 * e + 2], (640, 128)) for e in range(2)]
    weighted = weighted.reshape(2, 640, 128).astype(bf16)

    def combined(parts):
        return sum(es("rt,rd->td", weighted[e], parts[e].reshape(640, -1)[:, :MODEL_WIDTH]) for e in range(2))

    kept = [
        (xs[e], dys[e], *kept, slot_gate[e]) for e, kept in enumerate((kept_first, kept_second))
    ]
    grad_gate, grad_up, grad_down, ys = weight_grads([*kept[0], *kept[1]], down_all, from_first)
    (from_second,) = after([from_second], ys)
    backs = [from_first, from_second]
    dh_sum = combined(backs)
    dgate = [v.reshape(640, -1)[:, MODEL_WIDTH : MODEL_WIDTH + 2].astype(f32).sum(axis=1) for v in backs]
    dgate = jnp.stack(dgate).reshape(2, 16, CAP, 1)
    dgate = jnp.sum(jnp.where(picks.reshape(2, 16, CAP, 128), dgate, 0.0), axis=2)
    dgate = dgate.transpose(2, 1, 0).reshape(128, EXPERTS)
    expert_grads = after([grad_gate, grad_up, grad_down], from_second)
    dl = (gates * (dgate - jnp.sum(gates * dgate, axis=-1, keepdims=True))).astype(bf16)
    dh2 = es("te,de->td", dl, router) + dh_sum
    dx2 = upstream + norm_back(dh2 * mlp_gain, normed_two, scale_two)
    da = dx2.astype(bf16)
    da_pieces = gather_fsdp(da)
    (ys,) = after([ys], from_second)
    ys = exchanged(ys).reshape(1280, MODEL_WIDTH)
    by_owner = weighted.reshape(2, 16, CAP, 128).transpose(1, 0, 2, 3).reshape(1280, 128)
    output = (resid_two + es("rt,rd->td", by_owner, ys)).astype(bf16)
    aux = jnp.pad(es("td,te->de", h2, dl), ((0, 0), (0, 128 - EXPERTS)))
    grad_mlp_gain = jnp.sum(dh2 * normed_two, axis=0)
    def scattered(v):
        return lax.psum_scatter(v, FSDP, scatter_dimension=1, tiled=True)

    grad_gate, grad_up, grad_down = (scattered(v) for v in expert_grads)
    dob, out_shares = out_back(da_pieces, zc, w_out, a_b)
    dq_raw, dkv, q_part = attention_backward(
        dob, a_b, q_b, k_b, v_b, lse, q_raw, query_gain[None], cosine, signed
    )
    left, right, dqkv, along, k_part = projection_grads(
        zc, idx, dq_raw, dkv, shift(dkv, C, 1), k_raw, q_part, key_gain[None], cosine, signed, h1_all, w, aux,
        out_shares, ys,
    )
    left, right, first = scatter_plane(left, right)
    keep, send = input_grad(zc, dqkv, w, first)
    dh1 = scatter_fsdp(keep, send)
    gains = jnp.concatenate([along[:, 0], grad_mlp_gain, q_part[0], k_part[0]]).reshape(34, 128)
    (gains,) = after([gains], first)
    gains = gains + shift(gains, C, 1)
    gains = (gains + shift(gains, Z, 2)) + (shift(gains, Z, 1) + shift(gains, Z, 3))
    high = gains.astype(bf16)
    gains = jnp.stack([high, (gains - high.astype(f32)).astype(bf16)]).reshape(8, 16, 68)
    gains = jnp.pad(gains, ((0, 0), (0, 0), (0, 28)))
    shares = jnp.concatenate([left, right]).astype(bf16)
    parted = lax.all_to_all(shares[:, :768].reshape(8, 16, 768), FSDP, 0, 0, tiled=True)
    expert_grads = [v.astype(f32) for v in (grad_gate, grad_up, grad_down)]
    parted = jnp.concatenate([parted[:, :, : 640 + EXPERTS], gains, shares[:, 768:].reshape(8, 16, 512)], axis=2)
    grad_input = dx2 + norm_back(dh1 * attn_gain, normed_one, scale_one)
    grad_input = grad_input.astype(bf16)
    parted = lax.all_gather(parted, EXPERT, axis=0, tiled=False)
    grad_query, grad_key, grad_value, aux, gains, grad_out = place_rows(parted, grad_input, *expert_grads)
    gains = (gains[:4] + gains[4:])[:, :, EXPERTS : EXPERTS + 68].reshape(-1)
    return (
        output[None],
        grad_input[None],
        gains[:MODEL_WIDTH] / attn_gain,
        gains[2 * MODEL_WIDTH : 2 * MODEL_WIDTH + HEAD_SIZE],
        gains[2 * MODEL_WIDTH + HEAD_SIZE :],
        gains[MODEL_WIDTH : 2 * MODEL_WIDTH],
        grad_query,
        grad_key,
        grad_value,
        grad_out,
        aux[:, :EXPERTS],
        *expert_grads,
    )


def solution(mesh):
    torus = Mesh(mesh.devices.reshape(4, 2, 4, 4), ALL)
    tokens, rows, experts = P(EXPERT, FSDP, None), P(FSDP, None), P(EXPERT, FSDP, None)
    return jax.shard_map(
        local,
        mesh=torus,
        in_specs=(tokens,) * 3 + (P(),) * 4 + (rows,) * 5 + (experts,) * 3,
        out_specs=(tokens,) * 2 + (P(),) * 4 + (rows,) * 5 + (experts,) * 3,
        check_vma=False,
    )
```

```python
import functools

import jax
import jax.numpy as jnp
from jax import lax
from jax.experimental import pallas as pl
from jax.experimental.pallas import tpu as pltpu
from jax.sharding import Mesh
from jax.sharding import PartitionSpec as P

MODEL_WIDTH = 2048
QUERY_HEADS = 32
KEY_VALUE_HEADS = 4
HEAD_SIZE = 128
TOPK = 8
EXPERTS = 32
CAP = 40
Z, C, Y, X = "z", "c", "y", "x"
FSDP = (Z, C)
EXPERT = (Y, X)
ALL = (Z, C, Y, X)

bf16 = jnp.bfloat16
f32 = jnp.float32
epsilon = 1e-06
rope_base = 1000000.0


def dot(a, b):
    return jnp.dot(a, b, preferred_element_type=f32)


def es(spec, a, b):
    return jnp.einsum(spec, a, b, preferred_element_type=f32)


def shift(v, axis, by):
    n = 2 if axis == C else 4
    return lax.ppermute(v, axis, [(i, (i + by) % n) for i in range(n)])


def gather_fsdp(p, join=lambda *values: values):
    half = p.shape[0] // 2
    up, down = join(shift(p, Z, -1), shift(p, Z, 1))
    other = shift(p, C, 1)
    far_low, far_high = shift(down[:half], Z, 1), shift(up[half:], Z, -1)
    far = [(up, 1, 0), (down, 3, 0), (far_low, 2, 0), (far_high, 2, half)]
    return (
        [(p, 0, 0, 0), (other, 0, 1, 0)]
        + [(a, dz, 0, r) for a, dz, r in far]
        + [(shift(a, C, 1), dz, 1, r) for a, dz, r in far]
    )


def scatter_fsdp(keep, send, join=lambda *values: values):
    got = shift(send, C, 1)
    half = keep.shape[1] // 2

    def both(d, rows=slice(None)):
        return (keep[d, rows].astype(f32) + got[d, rows].astype(f32)).astype(bf16)

    low, high = slice(None, half), slice(half, None)
    far_low, far_high = both(2, low), both(2, high)
    from_down, from_up = shift(far_low, Z, 1), shift(far_high, Z, -1)
    one, three = both(1), both(3)
    one = jnp.concatenate([(one[low].astype(f32) + from_down.astype(f32)).astype(bf16), one[high]])
    three = jnp.concatenate([three[low], (three[high].astype(f32) + from_up.astype(f32)).astype(bf16)])
    one, three = join(one, three)
    from_down, from_up = shift(one, Z, 1), shift(three, Z, -1)
    own = keep[0].astype(f32) + got[0].astype(f32)
    return own + from_down.astype(f32) + from_up.astype(f32)


def gather_ring(v, axis):
    half = v.shape[0] // 2
    up, down = shift(v, axis, -1), shift(v, axis, 1)
    return v, up, shift(down[:half], axis, 1), shift(up[half:], axis, -1), down


def scatter_ring(parts, axis):
    own, one, low, high, three = parts
    k = low.shape[0]
    down, up = shift(low, axis, 1), shift(high, axis, -1)
    first = down

    def plus(a, b):
        return (a.astype(f32) + b.astype(f32)).astype(bf16)

    one = jnp.concatenate([plus(one[:k], down), one[k:]])
    three = jnp.concatenate([three[:k], plus(three[k:], up)])
    down, up = shift(one, axis, 1), shift(three, axis, -1)
    return own.astype(f32) + down.astype(f32) + up.astype(f32), first


def scatter_plane(left, right):
    def halves(v):
        v = v.astype(bf16)
        k = v.shape[1] // 2
        return v[0], v[1], v[2, :k], v[2, k:], v[3]

    left, first = scatter_ring(left, Y)
    right, _ = scatter_ring(right, X)
    return scatter_ring(halves(left), X)[0], scatter_ring(halves(right), Y)[0], first


def inv_rms(values):
    return lax.rsqrt(jnp.mean(values * values, axis=-1, keepdims=True) + epsilon)


def norm_back(grad_norm, normed, scale_part):
    return scale_part * (grad_norm - normed * jnp.mean(grad_norm * normed, axis=-1, keepdims=True))


def rope_tables(positions):
    frequency = rope_base ** (-(jnp.arange(HEAD_SIZE // 2).astype(f32) * 2.0 / HEAD_SIZE))
    frequency = jnp.concatenate([frequency, frequency])
    angles = positions[:, None] * frequency[None, :]
    return jnp.cos(angles), jnp.sin(angles)


def mm(a, b, dims=((1,), (0,))):
    return lax.dot_general(a, b, (dims, ((), ())), preferred_element_type=f32)


NT = ((1,), (1,))
TN = ((0,), (0,))
ANY = pl.BlockSpec(memory_space=pl.ANY)
VM = pl.BlockSpec(memory_space=pltpu.VMEM)
SM = pl.BlockSpec(memory_space=pltpu.SMEM)
MIB = 1 << 20


def load_pieces(place, spec, pieces, whole, sems):
    copies = []
    for k, (dz, dc, first, rows) in enumerate(spec):
        at = lax.rem(place[0] + dz, 4) * 256 + lax.rem(place[1] + dc, 2) * 128 + first
        at = pl.multiple_of(at, 64)
        copies.append(pltpu.make_async_copy(pieces[k], whole.at[pl.ds(at, rows)], sems.at[k]))
    for copy in copies:
        copy.start()
    return copies


def load_weights(place, parts, w, sems):
    copies = []
    for k in range(8):
        source = lax.rem(place[0] + 4 - k % 4, 4) * 2 + lax.rem(place[1] + k // 4, 2)
        rows = pl.ds(pl.multiple_of(source * 256, 256), 256)
        piece = parts[k].at[0] if k < 4 else parts[4].at[k - 4]
        copies.append(pltpu.make_async_copy(piece, w.at[rows], sems.at[k]))
    for copy in copies:
        copy.start()
    return copies


def attention_kernel(spec, place, w_out, q_gain, k_gain, cosine, sine, *rest):
    n = len(spec)
    pieces, parts, rest = rest[:n], rest[n : n + 5], rest[n + 5 :]
    w, h1, q_raw, k_raw, v_b, q_b, k_b, a_b, lse, keep, send, sems, w_sems = rest
    z, c = place[0], place[1]
    copies = load_weights(place, parts, w, w_sems)
    for copy in load_pieces(place, spec, pieces, h1, sems) + copies:
        copy.wait()

    @pl.loop(0, 4)
    def _(i):
        rows = pl.ds(pl.multiple_of(i * 256, 256), 256)
        t = mm(h1[rows, :MODEL_WIDTH], w[...])
        q_raw[rows] = t[:, :512]
        k_raw[rows] = t[:, 512:640]
        v_b[rows] = t[:, 640:].astype(bf16)
        co, si = cosine[rows], sine[rows]

        def rotated(u, gain):
            u = u * lax.rsqrt(jnp.mean(u * u, axis=-1, keepdims=True) + epsilon) * gain
            return (u * co + pltpu.roll(u, 64, 1) * si).astype(bf16)

        for h in range(4):
            q_b[h, rows] = rotated(t[:, 128 * h : 128 * h + 128], q_gain[...])
        k_b[rows] = rotated(t[:, 512:640], k_gain[...])

    lane = lax.broadcasted_iota(jnp.int32, (256, 128), 1)
    below = lax.broadcasted_iota(jnp.int32, (256, 256), 0) >= lax.broadcasted_iota(
        jnp.int32, (256, 256), 1
    )
    for i in range(4):
        n_keys = 256 * (i + 1)
        rows = slice(256 * i, n_keys)
        logs = jnp.zeros((256, 128), f32)
        for h in range(4):
            s = mm(q_b[h, rows], k_b[:n_keys], NT) * (HEAD_SIZE**-0.5)
            e = jnp.exp(s)
            tail = jnp.where(below, e[:, n_keys - 256 :], 0.0)
            e = tail if i == 0 else jnp.concatenate([e[:, : n_keys - 256], tail], axis=1)
            total = jnp.sum(e, axis=1, keepdims=True)
            a = mm(e.astype(bf16), v_b[:n_keys]) / total
            a_b[rows, 128 * h : 128 * h + 128] = a.astype(bf16)
            logs = jnp.where(lane == h, jnp.log(total), logs)
        lse[rows] = logs
        part = mm(a_b[rows], w_out[...]).astype(bf16)
        dz = lax.rem(i - z + 4, 4)
        first, second = part[:128], part[128:]
        keep[dz] = jnp.where(c == 0, first, second)
        send[dz] = jnp.where(c == 0, second, first)


def attention_forward(pieces, parts, place, w_out, q_gain, k_gain, cosine, sine):
    spec = [(dz, dc, first, a.shape[0]) for a, dz, dc, first in pieces]
    seq = 1024
    shapes = [
        ((MODEL_WIDTH, 768), bf16),
        ((seq, MODEL_WIDTH + 128), bf16),
        ((seq, 512), f32),
        ((seq, 128), f32),
        ((seq, 128), bf16),
        ((4, seq, 128), bf16),
        ((seq, 128), bf16),
        ((seq, 512), bf16),
        ((seq, 128), f32),
        ((4, 128, MODEL_WIDTH), bf16),
        ((4, 128, MODEL_WIDTH), bf16),
    ]
    return pl.pallas_call(
        functools.partial(attention_kernel, spec),
        out_shape=[jax.ShapeDtypeStruct(*s) for s in shapes],
        in_specs=[SM] + [VM] * 5 + [ANY] * (len(spec) + 5),
        out_specs=[VM] * len(shapes),
        scratch_shapes=[pltpu.SemaphoreType.DMA((len(spec),)), pltpu.SemaphoreType.DMA((8,))],
        compiler_params=pltpu.CompilerParams(vmem_limit_bytes=56 * MIB),
        cost_estimate=pl.CostEstimate(flops=9 << 30, bytes_accessed=28 << 20, transcendentals=3 << 20),
        name="attention_forward",
    )(place, w_out, q_gain, k_gain, cosine, sine, *[p[0] for p in pieces], *parts)


def expert_kernel(e, xs_in, dys_in, w_in, w_down, back, hid, dg, du, xs, dys, wg, wu, wd, sems):
    loads = []
    for k, (source, into) in enumerate(
        (
            (xs_in.at[:, pl.ds(0, MODEL_WIDTH)], xs), (w_in.at[e], wg), (w_in.at[2 + e], wu), (dys_in, dys), (w_down.at[e], wd),
        )
    ):
        loads.append(pltpu.make_async_copy(source, into, sems.at[k]))
        loads[-1].start()
    total = jnp.zeros((640, 1), f32)
    for k in range(3):
        loads[k].wait()
    for i in range(3):
        cols = slice(256 * i, 256 * i + 256)
        g, u = mm(xs[...], wg[:, cols]), mm(xs[...], wu[:, cols])
        if i == 0:
            loads[3].wait()
            loads[4].wait()
        d = mm(dys[...], wd[cols], NT)
        sig = 0.5 + 0.5 * jnp.tanh(0.5 * g)
        act = g * sig
        h = act * u
        total = total + jnp.sum(d * h, axis=1, keepdims=True)
        hid[:, cols] = h.astype(bf16)
        du[:, cols] = (d * act).astype(bf16)
        dg[:, cols] = (d * u * (sig + act * (1.0 - sig))).astype(bf16)
    back[:, :MODEL_WIDTH] = (mm(dg[...], wg[...], NT) + mm(du[...], wu[...], NT)).astype(bf16)
    high = total.astype(bf16).astype(f32)
    lane = lax.broadcasted_iota(jnp.int32, (640, 128), 1)
    back[:, MODEL_WIDTH:] = jnp.where(lane == 0, high, jnp.where(lane == 1, total - high, 0.0)).astype(bf16)


def expert_rows(e, xs, dys, w_in, w_down):
    row, act = (640, MODEL_WIDTH), (640, 768)
    scratch = [row, row, (MODEL_WIDTH, 768), (MODEL_WIDTH, 768), (768, MODEL_WIDTH)]
    return pl.pallas_call(
        functools.partial(expert_kernel, e),
        out_shape=[jax.ShapeDtypeStruct(s, bf16) for s in ((640, MODEL_WIDTH + 128), act, act, act)],
        in_specs=[ANY] * 4,
        out_specs=[VM] * 4,
        scratch_shapes=[pltpu.VMEM(s, bf16) for s in scratch] + [pltpu.SemaphoreType.DMA((5,))],
        compiler_params=pltpu.CompilerParams(vmem_limit_bytes=48 * MIB),
        cost_estimate=pl.CostEstimate(flops=10 << 30, bytes_accessed=20 << 20, transcendentals=1 << 20),
        name="expert_rows",
    )(xs, dys, w_in, w_down)


def weight_grads_kernel(*refs):
    rows, w_down, grads, ys = refs[:12], refs[12], refs[14:17], refs[17]
    first = pl.program_id(0) == 0
    for e in range(2):
        xs, dys, hid, dg, du, gate = rows[6 * e : 6 * e + 6]

        @pl.when(first if e == 0 else jnp.logical_not(first))
        def _(e=e, xs=xs, dys=dys, hid=hid, dg=dg, du=du, gate=gate):
            s = gate[:, 0:1]

            def scaled(v):
                return (v[...].astype(f32) * s).astype(bf16)

            y = mm(hid[...], w_down[0])
            for o in range(16):
                ys[o, CAP * e : CAP * e + CAP] = y[CAP * o : CAP * o + CAP].astype(bf16)
            grads[0][0] = mm(xs[:, :MODEL_WIDTH], scaled(dg), TN).astype(bf16)
            grads[1][0] = mm(xs[:, :MODEL_WIDTH], scaled(du), TN).astype(bf16)
            grads[2][0] = mm(scaled(hid), dys[...], TN).astype(bf16)


def weight_grads(rows, w_down, event):
    def per_expert(*dims):
        return pl.BlockSpec((1, *dims), lambda e: (e, 0, 0))

    sizes = [(MODEL_WIDTH, 768), (MODEL_WIDTH, 768), (768, MODEL_WIDTH)]
    return pl.pallas_call(
        weight_grads_kernel,
        grid=(2,),
        out_shape=[jax.ShapeDtypeStruct((2, *s), bf16) for s in sizes]
        + [jax.ShapeDtypeStruct((16, 2 * CAP, MODEL_WIDTH), bf16)],
        in_specs=[VM] * 12 + [per_expert(768, MODEL_WIDTH), ANY],
        out_specs=[per_expert(*s) for s in sizes] + [VM],
        compiler_params=pltpu.CompilerParams(vmem_limit_bytes=60 * MIB),
        cost_estimate=pl.CostEstimate(flops=16 << 30, bytes_accessed=48 << 20, transcendentals=0),
        name="weight_grads",
    )(*rows, w_down, event)


def out_back_kernel(spec, place, w_out, a_b, *rest):
    n = len(spec)
    pieces, (dob, shares, da, sems) = rest[:n], rest[n:]
    for copy in load_pieces(place, spec, pieces, da, sems):
        copy.wait()

    @pl.loop(0, 4)
    def _(i):
        rows = pl.ds(pl.multiple_of(i * 256, 256), 256)
        dob[rows] = mm(da[rows], w_out[...], NT).astype(bf16)

    for h in range(4):
        grads = mm(a_b[:, 128 * h : 128 * h + 128], da[...], TN).astype(bf16)
        for r in range(4):
            for k in range(4):
                block = grads[32 * r : 32 * r + 32, 512 * k : 512 * k + 512]
                shares[4 * h + r, 32 * k : 32 * k + 32] = block


def out_back(pieces, place, w_out, a_b):
    spec = [(dz, dc, first, a.shape[0]) for a, dz, dc, first in pieces]
    shapes = [((1024, 512), bf16), ((16, 128, 512), bf16)]
    return pl.pallas_call(
        functools.partial(out_back_kernel, spec),
        out_shape=[jax.ShapeDtypeStruct(*s) for s in shapes],
        in_specs=[SM] + [VM] * 2 + [ANY] * len(spec),
        out_specs=[VM] * 2,
        scratch_shapes=[pltpu.VMEM((1024, MODEL_WIDTH), bf16), pltpu.SemaphoreType.DMA((len(spec),))],
        compiler_params=pltpu.CompilerParams(vmem_limit_bytes=40 * MIB),
        cost_estimate=pl.CostEstimate(flops=5 << 30, bytes_accessed=12 << 20, transcendentals=0),
        name="out_back",
    )(place, w_out, a_b, *[p[0] for p in pieces])


def attention_back_kernel(dob, a_b, q_b, k_b, v_b, lse, q_raw, q_gain, cosine, sine, dq_raw, dkv, gain):
    root = HEAD_SIZE**-0.5
    below = lax.broadcasted_iota(jnp.int32, (256, 256), 0) >= lax.broadcasted_iota(
        jnp.int32, (256, 256), 1
    )
    dkv[...] = jnp.zeros(dkv.shape, f32)
    total = jnp.zeros((1, HEAD_SIZE), f32)
    for i in range(4):
        keys = 256 * (i + 1)
        rows = slice(256 * i, keys)
        co, si = cosine[rows], sine[rows]
        for h in range(4):
            cols = slice(128 * h, 128 * h + 128)
            q, do = q_b[h, rows], dob[rows, cols]
            p = jnp.exp(mm(q, k_b[:keys], NT) * root - lse[rows, h : h + 1])
            tail = jnp.where(below, p[:, keys - 256 :], 0.0)
            p = tail if i == 0 else jnp.concatenate([p[:, : keys - 256], tail], axis=1)
            dp = mm(do, v_b[:keys], NT)
            mean = jnp.sum(do.astype(f32) * a_b[rows, cols].astype(f32), axis=1, keepdims=True)
            ds = (p * (dp - mean)).astype(bf16)
            dkv[:keys, :128] += mm(ds, q, TN) * root
            dkv[:keys, 128:] += mm(p.astype(bf16), do, TN)
            dq = (mm(ds, k_b[:keys]) * root).astype(bf16).astype(f32)
            dq_in = dq * co + pltpu.roll(dq * si, 64, 1)
            raw = q_raw[rows, cols]
            scale = lax.rsqrt(jnp.mean(raw * raw, axis=-1, keepdims=True) + epsilon)
            hat = raw * scale
            total = total + jnp.sum(dq_in * hat, axis=0, keepdims=True)
            t = dq_in * q_gain[...]
            back = scale * (t - hat * jnp.mean(t * hat, axis=-1, keepdims=True))
            dq_raw[rows, cols] = back.astype(bf16)
    gain[...] = total


def attention_backward(dob, a_b, q_b, k_b, v_b, lse, q_raw, q_gain, cosine, sine):
    shapes = [((1024, 512), bf16), ((1024, 256), f32), ((1, HEAD_SIZE), f32)]
    return pl.pallas_call(
        attention_back_kernel,
        out_shape=[jax.ShapeDtypeStruct(*s) for s in shapes],
        in_specs=[VM] * 10,
        out_specs=[VM] * 3,
        compiler_params=pltpu.CompilerParams(vmem_limit_bytes=48 * MIB),
        cost_estimate=pl.CostEstimate(flops=10 << 30, bytes_accessed=12 << 20, transcendentals=0),
        name="attention_backward",
    )(dob, a_b, q_b, k_b, v_b, lse, q_raw, q_gain, cosine, sine)


def grads_kernel(
    place, idx, dq_raw, own, other, k_raw, q_part, k_gain, cosine, sine, h1, w, aux, out_shares, _, *outs
):
    left, right, (dqkv, along_out, k_part, shares) = outs[:5], outs[5:10], outs[10:]
    c = place[1]
    dqkv[:, :512] = dq_raw[...]
    total = jnp.zeros((1, HEAD_SIZE), f32)
    for i in range(4):
        rows = slice(256 * i, 256 * i + 256)
        both = (own[rows] + other[rows]).astype(bf16)
        dk = both[:, :128].astype(f32)
        dk_in = dk * cosine[rows] + pltpu.roll(dk * sine[rows], 64, 1)
        raw = k_raw[rows]
        scale = lax.rsqrt(jnp.mean(raw * raw, axis=-1, keepdims=True) + epsilon)
        hat = raw * scale
        total = total + jnp.sum(dk_in * hat, axis=0, keepdims=True)
        t = dk_in * k_gain[...]
        grad = scale * (t - hat * jnp.mean(t * hat, axis=-1, keepdims=True))
        dqkv[rows, 512:] = jnp.where(c == 0, grad, both[:, 128:].astype(f32)).astype(bf16)
    k_part[...] = total * 0.5
    for f in range(8):
        shard = slice(256 * f, 256 * f + 256)
        part = mm(h1[:, shard], dqkv[...], TN)
        last = jnp.where(c == 0, w[shard, 512:640], w[shard, 640:])
        along = jnp.sum(part[:, :512] * w[shard, :512].astype(f32), axis=1, keepdims=True)
        along = along + jnp.sum(part[:, 512:] * last.astype(f32), axis=1, keepdims=True)
        along_out[shard] = jnp.broadcast_to(along, (256, 128))
        shares[f, :, :640] = part.astype(bf16)
        shares[f, :, 640:] = aux[shard].astype(bf16)
    for r in range(16):
        dy, dx = divmod(r, 4)
        rows = pl.ds(pl.multiple_of(idx[r] * 16, 16), 16)
        a, ai = part_of(dy, dx)
        b, bi = part_of(dx, dy)
        for f in range(4):
            left[a][ai, 16 * f : 16 * f + 16, :768] = shares[f, rows]
            right[b][bi, 16 * f : 16 * f + 16, :768] = shares[f + 4, rows]
        left[a][ai, :, 768:] = out_shares[idx[r], :64]
        right[b][bi, :, 768:] = out_shares[idx[r], 64:]


def projection_grads(place, idx, dq_raw, own, other, k_raw, q_part, k_gain, cosine, sine, h1, w, aux, out_shares, event):
    shapes = [((n, 64, 1280), bf16) for n in [4, 4, 2, 2, 4] * 2]
    shapes += [((1024, 640), bf16), ((MODEL_WIDTH, 128), f32), ((1, HEAD_SIZE), f32)]
    outs = pl.pallas_call(
        grads_kernel,
        out_shape=[jax.ShapeDtypeStruct(*s) for s in shapes],
        in_specs=[SM, SM] + [VM] * 12 + [ANY],
        out_specs=[VM] * len(shapes),
        scratch_shapes=[pltpu.VMEM((8, 256, 768), bf16)],
        compiler_params=pltpu.CompilerParams(vmem_limit_bytes=52 * MIB),
        cost_estimate=pl.CostEstimate(flops=3 << 30, bytes_accessed=16 << 20, transcendentals=0),
        name="projection_grads",
    )(place, idx, dq_raw, own, other, k_raw, q_part, k_gain, cosine, sine, h1, w, aux, out_shares, event)
    return outs[:5], outs[5:10], *outs[10:]


def input_grad_kernel(place, dqkv, w, _, keep, send, w_own):
    z, c = place[0], place[1]
    w_own[:, :512] = w[:, :512]
    w_own[:, 512:] = jnp.where(c == 0, w[:, 512:640], w[:, 640:])

    @pl.loop(0, 4)
    def _(i):
        rows = pl.ds(pl.multiple_of(i * 256, 256), 256)
        part = mm(dqkv[rows], w_own[...], NT).astype(bf16)
        dz = lax.rem(i - z + 4, 4)
        first, second = part[:128], part[128:]
        keep[dz] = jnp.where(c == 0, first, second)
        send[dz] = jnp.where(c == 0, second, first)


def input_grad(place, dqkv, w, event):
    return pl.pallas_call(
        input_grad_kernel,
        out_shape=[jax.ShapeDtypeStruct((4, 128, MODEL_WIDTH), bf16)] * 2,
        in_specs=[SM, VM, VM, ANY],
        out_specs=[VM] * 2,
        scratch_shapes=[pltpu.VMEM((MODEL_WIDTH, 640), bf16)],
        compiler_params=pltpu.CompilerParams(vmem_limit_bytes=40 * MIB),
        cost_estimate=pl.CostEstimate(flops=3 << 30, bytes_accessed=8 << 20, transcendentals=0),
        name="input_grad",
    )(place, dqkv, w, event)


def part_of(outer, inner):
    return {0: (0, inner), 1: (1, inner), 2: (2 + inner // 2, inner % 2), 3: (4, inner)}[outer]


def place_kernel(source, *refs):
    query, key, value, aux, gains, out, parts, sems = refs[-8:]
    copies = [pltpu.make_async_copy(source.at[r], parts.at[r], sems.at[r]) for r in range(16)]
    for copy in copies:
        copy.start()
    for r in range(16):
        copies[r].wait()
        rows = slice(16 * r, 16 * r + 16)
        total = jnp.zeros((16, 128), f32)
        for f in range(8):
            block = parts[r, f].astype(f32)
            query[rows, 512 * f : 512 * f + 512] = block[:, :512]
            to = key if f % 2 == 0 else value
            to[rows, 128 * (f // 2) : 128 * (f // 2) + 128] = block[:, 512:640]
            total = total + block[:, 640:768]
            gains[f] = block[:, 640:768] if r == 0 else gains[f] + block[:, 640:768]
            first = 32 * r + 16 * (f % 2)
            out[first : first + 16, 512 * (f // 2) : 512 * (f // 2) + 512] = block[:, 768:]
        aux[rows] = total


def place_rows(parts, *events):
    shapes = [(256, 4096), (256, 512), (256, 512), (256, 128), (8, 16, 128), (512, MODEL_WIDTH)]
    return pl.pallas_call(
        place_kernel,
        out_shape=[jax.ShapeDtypeStruct(s, f32) for s in shapes],
        in_specs=[ANY] * (1 + len(events)),
        out_specs=[VM] * 6,
        scratch_shapes=[pltpu.VMEM((16, 8, 16, 1280), bf16), pltpu.SemaphoreType.DMA((16,))],
        compiler_params=pltpu.CompilerParams(vmem_limit_bytes=60 * MIB),
        cost_estimate=pl.CostEstimate(flops=0, bytes_accessed=16 << 20, transcendentals=0),
        name="place_rows",
    )(parts, *events)


def nothing(*refs):
    pass


def after(values, *events):
    n = len(values)
    return pl.pallas_call(
        nothing,
        out_shape=[jax.ShapeDtypeStruct(v.shape, v.dtype) for v in values],
        in_specs=[ANY] * (n + len(events)),
        out_specs=[ANY] * n,
        input_output_aliases={i: i for i in range(n)},
        cost_estimate=pl.CostEstimate(flops=0, bytes_accessed=0, transcendentals=0),
        name="after",
    )(*values, *events)


def local(
    layer_input, routes, cotangent, attn_gain, query_gain, key_gain, mlp_gain,
    w_query, key_weight, value_weight, w_out, w_router, w_gate, w_up, w_down,
):
    core = lax.axis_index(C)
    py, px = lax.axis_index(Y), lax.axis_index(X)
    zc = jnp.stack([lax.axis_index(Z), core, py, px]).astype(jnp.int32)
    ahead = jnp.arange(16, dtype=jnp.int32)
    idx = (py + ahead // 4) % 4 * 4 + (px + ahead % 4) % 4
    residual = layer_input[0].astype(f32)
    dy_low = cotangent[0]
    upstream = dy_low.astype(f32)
    scale_one = inv_rms(residual)
    normed_one = residual * scale_one
    h1 = (normed_one * attn_gain).astype(bf16)
    beside = jnp.pad(w_router.reshape(128, 64), ((0, 0), (0, 64)))
    h1 = jnp.concatenate([h1, beside], axis=1)
    seq = 1024
    cosine, sine = rope_tables(jnp.arange(seq).astype(f32))
    sign = jnp.where(jnp.arange(HEAD_SIZE) < HEAD_SIZE // 2, -1.0, 1.0).astype(f32)
    signed = sine * sign
    ids = jnp.arange(EXPERTS, dtype=jnp.int32)
    chosen = jnp.any(routes[0][:, :, None] == ids, axis=1)
    before = jnp.tril(jnp.ones((128, 128), bf16), -1)
    rank = dot(before, chosen.astype(bf16)).astype(jnp.int32)
    slot = jnp.where(chosen, rank, -1).T.reshape(16, 2, 128).transpose(1, 0, 2)
    picks = (slot[:, :, None, :] == jnp.arange(CAP)[:, None]).reshape(2, 640, 128)

    def sent(e, v):
        packed = dot(picks[e].astype(bf16), v).astype(bf16)
        return packed.reshape(16, CAP, MODEL_WIDTH)

    def exchanged(v):
        return lax.all_to_all(v, EXPERT, 0, 0, tiled=True)

    dy_all = lax.all_gather(dy_low, EXPERT, axis=0, tiled=False)
    tokens = jnp.arange(128, dtype=jnp.int32)
    slot_token = jnp.max(jnp.where(picks, tokens, -1), axis=-1).reshape(2, 16, CAP)
    in_own = jnp.concatenate([w_gate, w_up])
    rows = w_query.shape[0]

    def per_head(w, n):
        return jnp.repeat(w.reshape(rows, 4, 128), 2, axis=1) if n == 2 else w.reshape(rows, 8, 512)

    blocks = jnp.concatenate([per_head(w_query, 1), per_head(key_weight, 2), per_head(value_weight, 2)], axis=2)
    blocks = blocks.transpose(1, 0, 2).reshape(4, 2, rows, 768)
    blocks = jnp.where(core == 0, blocks, blocks[:, ::-1])
    place_z = lax.axis_index(Z)

    def meant_for(ahead):
        return lax.dynamic_index_in_dim(blocks, (place_z + ahead) % 4, 0, keepdims=False)

    w_parts = [meant_for(0)] + [shift(meant_for(d), Z, d) for d in range(1, 4)]
    h1_pieces = gather_fsdp(h1, lambda up, down: after([up, down], cosine, signed, in_own))
    w_parts[1:] = after(w_parts[1:], *[h1_pieces[k][0] for k in (1, 4, 5)])
    from_other = shift(jnp.stack([v[1] for v in w_parts]), C, 1)
    in_own, down_own = after(
        [in_own, w_down], *w_parts[1:], h1_pieces[4][0], h1_pieces[5][0]
    )
    in_all = lax.all_gather(in_own, FSDP, axis=1, tiled=True)
    down_all = lax.all_gather(down_own, FSDP, axis=1, tiled=True)
    w, h1_all, q_raw, k_raw, v_b, q_b, k_b, a_b, lse, keep, send = attention_forward(
        h1_pieces, [*w_parts, from_other], zc, w_out, query_gain[None], key_gain[None], cosine, signed
    )
    router = h1_all[:, MODEL_WIDTH : MODEL_WIDTH + 64].reshape(MODEL_WIDTH, EXPERTS)
    attn = scatter_fsdp(keep, send)
    resid_two = residual + attn
    scale_two = inv_rms(resid_two)
    normed_two = resid_two * scale_two
    h2 = (normed_two * mlp_gain).astype(bf16)
    beside = jnp.pad(jnp.stack([slot_token[0], slot_token[1]], axis=-1).astype(bf16), ((0, 0), (0, 0), (0, 126)))
    xs_first = exchanged(jnp.concatenate([sent(0, h2), beside], axis=-1))
    slot_token = xs_first[:, :, MODEL_WIDTH : MODEL_WIDTH + 2].astype(jnp.int32)
    taken = (slot_token[..., None] == tokens).astype(bf16)
    dys = [es("sct,std->scd", taken[:, :, e], dy_all).astype(bf16).reshape(640, MODEL_WIDTH) for e in range(2)]
    logits = jnp.where(chosen, dot(h2, router), -1e30)
    powers = jnp.where(chosen, jnp.exp(logits - jnp.max(logits, axis=-1, keepdims=True)), 0.0)
    gates = powers / jnp.sum(powers, axis=-1, keepdims=True)
    gates_slot = gates.T.reshape(16, 2, 128).transpose(1, 0, 2)
    weighted = jnp.where(picks.reshape(2, 16, CAP, 128), gates_slot[:, :, None, :], 0.0)
    slot_gate = jnp.sum(weighted, axis=-1)
    high = slot_gate.astype(bf16)
    low = (slot_gate - high.astype(f32)).astype(bf16)
    beside = jnp.stack([high[0], low[0], high[1], low[1]], axis=-1)
    beside = jnp.pad(beside, ((0, 0), (0, 0), (0, 124)))
    second = jnp.concatenate([sent(1, h2), beside], axis=-1)
    (second,) = after([second], xs_first)
    xs_second = exchanged(second)
    xs = [v.reshape(640, MODEL_WIDTH + 128) for v in (xs_first, xs_second)]
    back_first, *kept_first = expert_rows(0, xs[0], dys[0], in_all, down_all)
    wide = (16, CAP, MODEL_WIDTH + 128)
    (back_first,) = after([back_first.reshape(wide)], xs_second)
    from_first = exchanged(back_first)
    back_second, *kept_second = expert_rows(1, xs[1], dys[1], in_all, down_all)
    (back_second,) = after([back_second.reshape(wide)], from_first)
    from_second = exchanged(back_second)
    got = xs[1][:, MODEL_WIDTH : MODEL_WIDTH + 4].astype(f32)
    slot_gate = [jnp.broadcast_to(got[:, 2 * e : 2 * e + 1] + got[:, 2 * e + 1 : 2 * e + 2], (640, 128)) for e in range(2)]
    weighted = weighted.reshape(2, 640, 128).astype(bf16)

    def combined(parts):
        return sum(es("rt,rd->td", weighted[e], parts[e].reshape(640, -1)[:, :MODEL_WIDTH]) for e in range(2))

    kept = [
        (xs[e], dys[e], *kept, slot_gate[e]) for e, kept in enumerate((kept_first, kept_second))
    ]
    grad_gate, grad_up, grad_down, ys = weight_grads([*kept[0], *kept[1]], down_all, from_first)
    (from_second,) = after([from_second], ys)
    backs = [from_first, from_second]
    dh_sum = combined(backs)
    dgate = [v.reshape(640, -1)[:, MODEL_WIDTH : MODEL_WIDTH + 2].astype(f32).sum(axis=1) for v in backs]
    dgate = jnp.stack(dgate).reshape(2, 16, CAP, 1)
    dgate = jnp.sum(jnp.where(picks.reshape(2, 16, CAP, 128), dgate, 0.0), axis=2)
    dgate = dgate.transpose(2, 1, 0).reshape(128, EXPERTS)
    expert_grads = after([grad_gate, grad_up, grad_down], from_second)
    dl = (gates * (dgate - jnp.sum(gates * dgate, axis=-1, keepdims=True))).astype(bf16)
    dh2 = es("te,de->td", dl, router) + dh_sum
    dx2 = upstream + norm_back(dh2 * mlp_gain, normed_two, scale_two)
    da = dx2.astype(bf16)
    da_pieces = gather_fsdp(da)
    (ys,) = after([ys], from_second)
    ys = exchanged(ys).reshape(1280, MODEL_WIDTH)
    by_owner = weighted.reshape(2, 16, CAP, 128).transpose(1, 0, 2, 3).reshape(1280, 128)
    output = (resid_two + es("rt,rd->td", by_owner, ys)).astype(bf16)
    aux = jnp.pad(es("td,te->de", h2, dl), ((0, 0), (0, 128 - EXPERTS)))
    grad_mlp_gain = jnp.sum(dh2 * normed_two, axis=0)
    def scattered(v):
        return lax.psum_scatter(v, FSDP, scatter_dimension=1, tiled=True)

    grad_gate, grad_up, grad_down = (scattered(v) for v in expert_grads)
    dob, out_shares = out_back(da_pieces, zc, w_out, a_b)
    dq_raw, dkv, q_part = attention_backward(
        dob, a_b, q_b, k_b, v_b, lse, q_raw, query_gain[None], cosine, signed
    )
    left, right, dqkv, along, k_part = projection_grads(
        zc, idx, dq_raw, dkv, shift(dkv, C, 1), k_raw, q_part, key_gain[None], cosine, signed, h1_all, w, aux,
        out_shares, ys,
    )
    left, right, first = scatter_plane(left, right)
    keep, send = input_grad(zc, dqkv, w, first)
    dh1 = scatter_fsdp(keep, send)
    gains = jnp.concatenate([along[:, 0], grad_mlp_gain, q_part[0], k_part[0]]).reshape(34, 128)
    (gains,) = after([gains], first)
    gains = gains + shift(gains, C, 1)
    gains = (gains + shift(gains, Z, 2)) + (shift(gains, Z, 1) + shift(gains, Z, 3))
    high = gains.astype(bf16)
    gains = jnp.stack([high, (gains - high.astype(f32)).astype(bf16)]).reshape(8, 16, 68)
    gains = jnp.pad(gains, ((0, 0), (0, 0), (0, 28)))
    shares = jnp.concatenate([left, right]).astype(bf16)
    parted = lax.all_to_all(shares[:, :768].reshape(8, 16, 768), FSDP, 0, 0, tiled=True)
    expert_grads = [v.astype(f32) for v in (grad_gate, grad_up, grad_down)]
    parted = jnp.concatenate([parted[:, :, : 640 + EXPERTS], gains, shares[:, 768:].reshape(8, 16, 512)], axis=2)
    grad_input = dx2 + norm_back(dh1 * attn_gain, normed_one, scale_one)
    grad_input = grad_input.astype(bf16)
    parted = lax.all_gather(parted, EXPERT, axis=0, tiled=False)
    grad_query, grad_key, grad_value, aux, gains, grad_out = place_rows(parted, grad_input, *expert_grads)
    gains = (gains[:4] + gains[4:])[:, :, EXPERTS : EXPERTS + 68].reshape(-1)
    return (
        output[None],
        grad_input[None],
        gains[:MODEL_WIDTH] / attn_gain,
        gains[2 * MODEL_WIDTH : 2 * MODEL_WIDTH + HEAD_SIZE],
        gains[2 * MODEL_WIDTH + HEAD_SIZE :],
        gains[MODEL_WIDTH : 2 * MODEL_WIDTH],
        grad_query,
        grad_key,
        grad_value,
        grad_out,
        aux[:, :EXPERTS],
        *expert_grads,
    )


def solution(mesh):
    torus = Mesh(mesh.devices.reshape(4, 2, 4, 4), ALL)
    tokens, rows, experts = P(EXPERT, FSDP, None), P(FSDP, None), P(EXPERT, FSDP, None)
    return jax.shard_map(
        local,
        mesh=torus,
        in_specs=(tokens,) * 3 + (P(),) * 4 + (rows,) * 5 + (experts,) * 3,
        out_specs=(tokens,) * 2 + (P(),) * 4 + (rows,) * 5 + (experts,) * 3,
        check_vma=False,
    )
```

```python
import functools

import jax
import jax.numpy as jnp
from jax import lax
from jax.experimental import pallas as pl
from jax.experimental.pallas import tpu as pltpu
from jax.sharding import Mesh
from jax.sharding import PartitionSpec as P

MODEL_WIDTH = 2048
QUERY_HEADS = 32
KEY_VALUE_HEADS = 4
HEAD_SIZE = 128
TOPK = 8
EXPERTS = 32
CAP = 40
Z, C, Y, X = "z", "c", "y", "x"
FSDP = (Z, C)
EXPERT = (Y, X)
ALL = (Z, C, Y, X)

bf16 = jnp.bfloat16
f32 = jnp.float32
epsilon = 1e-06
rope_base = 1000000.0


def dot(a, b):
    return jnp.dot(a, b, preferred_element_type=f32)


def es(spec, a, b):
    return jnp.einsum(spec, a, b, preferred_element_type=f32)


def shift(v, axis, by):
    n = 2 if axis == C else 4
    return lax.ppermute(v, axis, [(i, (i + by) % n) for i in range(n)])


def gather_fsdp(p, join=lambda *values: values):
    half = p.shape[0] // 2
    up, down = join(shift(p, Z, -1), shift(p, Z, 1))
    other = shift(p, C, 1)
    far_low, far_high = shift(down[:half], Z, 1), shift(up[half:], Z, -1)
    far = [(up, 1, 0), (down, 3, 0), (far_low, 2, 0), (far_high, 2, half)]
    return (
        [(p, 0, 0, 0), (other, 0, 1, 0)]
        + [(a, dz, 0, r) for a, dz, r in far]
        + [(shift(a, C, 1), dz, 1, r) for a, dz, r in far]
    )


def scatter_fsdp(keep, send, join=lambda *values: values):
    got = shift(send, C, 1)
    half = keep.shape[1] // 2

    def both(d, rows=slice(None)):
        return (keep[d, rows].astype(f32) + got[d, rows].astype(f32)).astype(bf16)

    low, high = slice(None, half), slice(half, None)
    far_low, far_high = both(2, low), both(2, high)
    from_down, from_up = shift(far_low, Z, 1), shift(far_high, Z, -1)
    one, three = both(1), both(3)
    one = jnp.concatenate([(one[low].astype(f32) + from_down.astype(f32)).astype(bf16), one[high]])
    three = jnp.concatenate([three[low], (three[high].astype(f32) + from_up.astype(f32)).astype(bf16)])
    one, three = join(one, three)
    from_down, from_up = shift(one, Z, 1), shift(three, Z, -1)
    own = keep[0].astype(f32) + got[0].astype(f32)
    return own + from_down.astype(f32) + from_up.astype(f32)


def gather_ring(v, axis):
    half = v.shape[0] // 2
    up, down = shift(v, axis, -1), shift(v, axis, 1)
    return v, up, shift(down[:half], axis, 1), shift(up[half:], axis, -1), down


def scatter_ring(parts, axis):
    own, one, low, high, three = parts
    k = low.shape[0]
    down, up = shift(low, axis, 1), shift(high, axis, -1)
    first = down

    def plus(a, b):
        return (a.astype(f32) + b.astype(f32)).astype(bf16)

    one = jnp.concatenate([plus(one[:k], down), one[k:]])
    three = jnp.concatenate([three[:k], plus(three[k:], up)])
    down, up = shift(one, axis, 1), shift(three, axis, -1)
    return own.astype(f32) + down.astype(f32) + up.astype(f32), first


def scatter_plane(left, right):
    def halves(v):
        v = v.astype(bf16)
        k = v.shape[1] // 2
        return v[0], v[1], v[2, :k], v[2, k:], v[3]

    left, first = scatter_ring(left, Y)
    right, _ = scatter_ring(right, X)
    return scatter_ring(halves(left), X)[0], scatter_ring(halves(right), Y)[0], first


def inv_rms(values):
    return lax.rsqrt(jnp.mean(values * values, axis=-1, keepdims=True) + epsilon)


def norm_back(grad_norm, normed, scale_part):
    return scale_part * (grad_norm - normed * jnp.mean(grad_norm * normed, axis=-1, keepdims=True))


def rope_tables(positions):
    frequency = rope_base ** (-(jnp.arange(HEAD_SIZE // 2).astype(f32) * 2.0 / HEAD_SIZE))
    frequency = jnp.concatenate([frequency, frequency])
    angles = positions[:, None] * frequency[None, :]
    return jnp.cos(angles), jnp.sin(angles)


def mm(a, b, dims=((1,), (0,))):
    return lax.dot_general(a, b, (dims, ((), ())), preferred_element_type=f32)


NT = ((1,), (1,))
TN = ((0,), (0,))
ANY = pl.BlockSpec(memory_space=pl.ANY)
VM = pl.BlockSpec(memory_space=pltpu.VMEM)
SM = pl.BlockSpec(memory_space=pltpu.SMEM)
MIB = 1 << 20


def load_pieces(place, spec, pieces, whole, sems):
    copies = []
    for k, (dz, dc, first, rows) in enumerate(spec):
        at = lax.rem(place[0] + dz, 4) * 256 + lax.rem(place[1] + dc, 2) * 128 + first
        at = pl.multiple_of(at, 64)
        copies.append(pltpu.make_async_copy(pieces[k], whole.at[pl.ds(at, rows)], sems.at[k]))
    for copy in copies:
        copy.start()
    return copies


def load_weights(place, parts, w, sems):
    copies = []
    for k in range(8):
        source = lax.rem(place[0] + 4 - k % 4, 4) * 2 + lax.rem(place[1] + k // 4, 2)
        rows = pl.ds(pl.multiple_of(source * 256, 256), 256)
        piece = parts[k].at[0] if k < 4 else parts[4].at[k - 4]
        copies.append(pltpu.make_async_copy(piece, w.at[rows], sems.at[k]))
    for copy in copies:
        copy.start()
    return copies


def attention_kernel(spec, place, w_out, q_gain, k_gain, cosine, sine, *rest):
    n = len(spec)
    pieces, parts, rest = rest[:n], rest[n : n + 5], rest[n + 5 :]
    w, h1, q_raw, k_raw, v_b, q_b, k_b, a_b, lse, keep, send, sems, w_sems = rest
    z, c = place[0], place[1]
    copies = load_weights(place, parts, w, w_sems)
    for copy in load_pieces(place, spec, pieces, h1, sems) + copies:
        copy.wait()

    @pl.loop(0, 4)
    def _(i):
        rows = pl.ds(pl.multiple_of(i * 256, 256), 256)
        t = mm(h1[rows, :MODEL_WIDTH], w[...])
        q_raw[rows] = t[:, :512]
        k_raw[rows] = t[:, 512:640]
        v_b[rows] = t[:, 640:].astype(bf16)
        co, si = cosine[rows], sine[rows]

        def rotated(u, gain):
            u = u * lax.rsqrt(jnp.mean(u * u, axis=-1, keepdims=True) + epsilon) * gain
            return (u * co + pltpu.roll(u, 64, 1) * si).astype(bf16)

        for h in range(4):
            q_b[h, rows] = rotated(t[:, 128 * h : 128 * h + 128], q_gain[...])
        k_b[rows] = rotated(t[:, 512:640], k_gain[...])

    lane = lax.broadcasted_iota(jnp.int32, (256, 128), 1)
    below = lax.broadcasted_iota(jnp.int32, (256, 256), 0) >= lax.broadcasted_iota(
        jnp.int32, (256, 256), 1
    )
    for i in range(4):
        n_keys = 256 * (i + 1)
        rows = slice(256 * i, n_keys)
        logs = jnp.zeros((256, 128), f32)
        for h in range(4):
            s = mm(q_b[h, rows], k_b[:n_keys], NT) * (HEAD_SIZE**-0.5)
            e = jnp.exp(s)
            tail = jnp.where(below, e[:, n_keys - 256 :], 0.0)
            e = tail if i == 0 else jnp.concatenate([e[:, : n_keys - 256], tail], axis=1)
            total = jnp.sum(e, axis=1, keepdims=True)
            a = mm(e.astype(bf16), v_b[:n_keys]) / total
            a_b[rows, 128 * h : 128 * h + 128] = a.astype(bf16)
            logs = jnp.where(lane == h, jnp.log(total), logs)
        lse[rows] = logs
        part = mm(a_b[rows], w_out[...]).astype(bf16)
        dz = lax.rem(i - z + 4, 4)
        first, second = part[:128], part[128:]
        keep[dz] = jnp.where(c == 0, first, second)
        send[dz] = jnp.where(c == 0, second, first)


def attention_forward(pieces, parts, place, w_out, q_gain, k_gain, cosine, sine):
    spec = [(dz, dc, first, a.shape[0]) for a, dz, dc, first in pieces]
    seq = 1024
    shapes = [
        ((MODEL_WIDTH, 768), bf16),
        ((seq, MODEL_WIDTH + 128), bf16),
        ((seq, 512), f32),
        ((seq, 128), f32),
        ((seq, 128), bf16),
        ((4, seq, 128), bf16),
        ((seq, 128), bf16),
        ((seq, 512), bf16),
        ((seq, 128), f32),
        ((4, 128, MODEL_WIDTH), bf16),
        ((4, 128, MODEL_WIDTH), bf16),
    ]
    return pl.pallas_call(
        functools.partial(attention_kernel, spec),
        out_shape=[jax.ShapeDtypeStruct(*s) for s in shapes],
        in_specs=[SM] + [VM] * 5 + [ANY] * (len(spec) + 5),
        out_specs=[VM] * len(shapes),
        scratch_shapes=[pltpu.SemaphoreType.DMA((len(spec),)), pltpu.SemaphoreType.DMA((8,))],
        compiler_params=pltpu.CompilerParams(vmem_limit_bytes=56 * MIB),
        cost_estimate=pl.CostEstimate(flops=9 << 30, bytes_accessed=28 << 20, transcendentals=3 << 20),
        name="attention_forward",
    )(place, w_out, q_gain, k_gain, cosine, sine, *[p[0] for p in pieces], *parts)


def expert_kernel(e, xs_in, dys_in, w_in, w_down, back, hid, dg, du, xs, dys, wg, wu, wd, sems):
    loads = []
    for k, (source, into) in enumerate(
        (
            (xs_in.at[:, pl.ds(0, MODEL_WIDTH)], xs), (w_in.at[e], wg), (w_in.at[2 + e], wu), (dys_in, dys), (w_down.at[e], wd),
        )
    ):
        loads.append(pltpu.make_async_copy(source, into, sems.at[k]))
        loads[-1].start()
    total = jnp.zeros((640, 1), f32)
    for k in range(3):
        loads[k].wait()
    for i in range(3):
        cols = slice(256 * i, 256 * i + 256)
        g, u = mm(xs[...], wg[:, cols]), mm(xs[...], wu[:, cols])
        if i == 0:
            loads[3].wait()
            loads[4].wait()
        d = mm(dys[...], wd[cols], NT)
        sig = 0.5 + 0.5 * jnp.tanh(0.5 * g)
        act = g * sig
        h = act * u
        total = total + jnp.sum(d * h, axis=1, keepdims=True)
        hid[:, cols] = h.astype(bf16)
        du[:, cols] = (d * act).astype(bf16)
        dg[:, cols] = (d * u * (sig + act * (1.0 - sig))).astype(bf16)
    back[:, :MODEL_WIDTH] = (mm(dg[...], wg[...], NT) + mm(du[...], wu[...], NT)).astype(bf16)
    high = total.astype(bf16).astype(f32)
    lane = lax.broadcasted_iota(jnp.int32, (640, 128), 1)
    back[:, MODEL_WIDTH:] = jnp.where(lane == 0, high, jnp.where(lane == 1, total - high, 0.0)).astype(bf16)


def expert_rows(e, xs, dys, w_in, w_down):
    row, act = (640, MODEL_WIDTH), (640, 768)
    scratch = [row, row, (MODEL_WIDTH, 768), (MODEL_WIDTH, 768), (768, MODEL_WIDTH)]
    return pl.pallas_call(
        functools.partial(expert_kernel, e),
        out_shape=[jax.ShapeDtypeStruct(s, bf16) for s in ((640, MODEL_WIDTH + 128), act, act, act)],
        in_specs=[ANY] * 4,
        out_specs=[VM] * 4,
        scratch_shapes=[pltpu.VMEM(s, bf16) for s in scratch] + [pltpu.SemaphoreType.DMA((5,))],
        compiler_params=pltpu.CompilerParams(vmem_limit_bytes=48 * MIB),
        cost_estimate=pl.CostEstimate(flops=10 << 30, bytes_accessed=20 << 20, transcendentals=1 << 20),
        name="expert_rows",
    )(xs, dys, w_in, w_down)


def weight_grads_kernel(*refs):
    rows, w_down, grads, ys = refs[:12], refs[12], refs[14:17], refs[17:19]
    first = pl.program_id(0) == 0
    for e in range(2):
        xs, dys, hid, dg, du, gate = rows[6 * e : 6 * e + 6]

        @pl.when(first if e == 0 else jnp.logical_not(first))
        def _(xs=xs, dys=dys, hid=hid, dg=dg, du=du, gate=gate, out=ys[e]):
            s = gate[:, 0:1]

            def scaled(v):
                return (v[...].astype(f32) * s).astype(bf16)

            out[...] = mm(hid[...], w_down[0]).astype(bf16)
            grads[0][0] = mm(xs[:, :MODEL_WIDTH], scaled(dg), TN).astype(bf16)
            grads[1][0] = mm(xs[:, :MODEL_WIDTH], scaled(du), TN).astype(bf16)
            grads[2][0] = mm(scaled(hid), dys[...], TN).astype(bf16)


def weight_grads(rows, w_down, event):
    def per_expert(*dims):
        return pl.BlockSpec((1, *dims), lambda e: (e, 0, 0))

    sizes = [(MODEL_WIDTH, 768), (MODEL_WIDTH, 768), (768, MODEL_WIDTH)]
    return pl.pallas_call(
        weight_grads_kernel,
        grid=(2,),
        out_shape=[jax.ShapeDtypeStruct((2, *s), bf16) for s in sizes]
        + [jax.ShapeDtypeStruct((640, MODEL_WIDTH), bf16)] * 2,
        in_specs=[VM] * 12 + [per_expert(768, MODEL_WIDTH), ANY],
        out_specs=[per_expert(*s) for s in sizes] + [VM] * 2,
        compiler_params=pltpu.CompilerParams(vmem_limit_bytes=60 * MIB),
        cost_estimate=pl.CostEstimate(flops=16 << 30, bytes_accessed=48 << 20, transcendentals=0),
        name="weight_grads",
    )(*rows, w_down, event)


def out_back_kernel(spec, place, w_out, a_b, *rest):
    n = len(spec)
    pieces, (dob, shares, da, sems) = rest[:n], rest[n:]
    for copy in load_pieces(place, spec, pieces, da, sems):
        copy.wait()

    @pl.loop(0, 4)
    def _(i):
        rows = pl.ds(pl.multiple_of(i * 256, 256), 256)
        dob[rows] = mm(da[rows], w_out[...], NT).astype(bf16)

    for h in range(4):
        grads = mm(a_b[:, 128 * h : 128 * h + 128], da[...], TN).astype(bf16)
        for r in range(4):
            for k in range(4):
                block = grads[32 * r : 32 * r + 32, 512 * k : 512 * k + 512]
                shares[4 * h + r, 32 * k : 32 * k + 32] = block


def out_back(pieces, place, w_out, a_b):
    spec = [(dz, dc, first, a.shape[0]) for a, dz, dc, first in pieces]
    shapes = [((1024, 512), bf16), ((16, 128, 512), bf16)]
    return pl.pallas_call(
        functools.partial(out_back_kernel, spec),
        out_shape=[jax.ShapeDtypeStruct(*s) for s in shapes],
        in_specs=[SM] + [VM] * 2 + [ANY] * len(spec),
        out_specs=[VM] * 2,
        scratch_shapes=[pltpu.VMEM((1024, MODEL_WIDTH), bf16), pltpu.SemaphoreType.DMA((len(spec),))],
        compiler_params=pltpu.CompilerParams(vmem_limit_bytes=40 * MIB),
        cost_estimate=pl.CostEstimate(flops=5 << 30, bytes_accessed=12 << 20, transcendentals=0),
        name="out_back",
    )(place, w_out, a_b, *[p[0] for p in pieces])


def attention_back_kernel(dob, a_b, q_b, k_b, v_b, lse, q_raw, q_gain, cosine, sine, dq_raw, dkv, gain):
    root = HEAD_SIZE**-0.5
    below = lax.broadcasted_iota(jnp.int32, (256, 256), 0) >= lax.broadcasted_iota(
        jnp.int32, (256, 256), 1
    )
    dkv[...] = jnp.zeros(dkv.shape, f32)
    total = jnp.zeros((1, HEAD_SIZE), f32)
    for i in range(4):
        keys = 256 * (i + 1)
        rows = slice(256 * i, keys)
        co, si = cosine[rows], sine[rows]
        for h in range(4):
            cols = slice(128 * h, 128 * h + 128)
            q, do = q_b[h, rows], dob[rows, cols]
            p = jnp.exp(mm(q, k_b[:keys], NT) * root - lse[rows, h : h + 1])
            tail = jnp.where(below, p[:, keys - 256 :], 0.0)
            p = tail if i == 0 else jnp.concatenate([p[:, : keys - 256], tail], axis=1)
            dp = mm(do, v_b[:keys], NT)
            mean = jnp.sum(do.astype(f32) * a_b[rows, cols].astype(f32), axis=1, keepdims=True)
            ds = (p * (dp - mean)).astype(bf16)
            dkv[:keys, :128] += mm(ds, q, TN) * root
            dkv[:keys, 128:] += mm(p.astype(bf16), do, TN)
            dq = (mm(ds, k_b[:keys]) * root).astype(bf16).astype(f32)
            dq_in = dq * co + pltpu.roll(dq * si, 64, 1)
            raw = q_raw[rows, cols]
            scale = lax.rsqrt(jnp.mean(raw * raw, axis=-1, keepdims=True) + epsilon)
            hat = raw * scale
            total = total + jnp.sum(dq_in * hat, axis=0, keepdims=True)
            t = dq_in * q_gain[...]
            back = scale * (t - hat * jnp.mean(t * hat, axis=-1, keepdims=True))
            dq_raw[rows, cols] = back.astype(bf16)
    gain[...] = total


def attention_backward(dob, a_b, q_b, k_b, v_b, lse, q_raw, q_gain, cosine, sine):
    shapes = [((1024, 512), bf16), ((1024, 256), f32), ((1, HEAD_SIZE), f32)]
    return pl.pallas_call(
        attention_back_kernel,
        out_shape=[jax.ShapeDtypeStruct(*s) for s in shapes],
        in_specs=[VM] * 10,
        out_specs=[VM] * 3,
        compiler_params=pltpu.CompilerParams(vmem_limit_bytes=48 * MIB),
        cost_estimate=pl.CostEstimate(flops=10 << 30, bytes_accessed=12 << 20, transcendentals=0),
        name="attention_backward",
    )(dob, a_b, q_b, k_b, v_b, lse, q_raw, q_gain, cosine, sine)


def grads_kernel(
    place, idx, dq_raw, own, other, k_raw, q_part, k_gain, cosine, sine, h1, w, aux, out_shares, _, *outs
):
    left, right, (dqkv, along_out, k_part, shares) = outs[:5], outs[5:10], outs[10:]
    c = place[1]
    dqkv[:, :512] = dq_raw[...]
    total = jnp.zeros((1, HEAD_SIZE), f32)
    for i in range(4):
        rows = slice(256 * i, 256 * i + 256)
        both = (own[rows] + other[rows]).astype(bf16)
        dk = both[:, :128].astype(f32)
        dk_in = dk * cosine[rows] + pltpu.roll(dk * sine[rows], 64, 1)
        raw = k_raw[rows]
        scale = lax.rsqrt(jnp.mean(raw * raw, axis=-1, keepdims=True) + epsilon)
        hat = raw * scale
        total = total + jnp.sum(dk_in * hat, axis=0, keepdims=True)
        t = dk_in * k_gain[...]
        grad = scale * (t - hat * jnp.mean(t * hat, axis=-1, keepdims=True))
        dqkv[rows, 512:] = jnp.where(c == 0, grad, both[:, 128:].astype(f32)).astype(bf16)
    k_part[...] = total * 0.5
    for f in range(8):
        shard = slice(256 * f, 256 * f + 256)
        part = mm(h1[:, shard], dqkv[...], TN)
        last = jnp.where(c == 0, w[shard, 512:640], w[shard, 640:])
        along = jnp.sum(part[:, :512] * w[shard, :512].astype(f32), axis=1, keepdims=True)
        along = along + jnp.sum(part[:, 512:] * last.astype(f32), axis=1, keepdims=True)
        along_out[shard] = jnp.broadcast_to(along, (256, 128))
        shares[f, :, :640] = part.astype(bf16)
        shares[f, :, 640:] = aux[shard].astype(bf16)
    for r in range(16):
        dy, dx = divmod(r, 4)
        rows = pl.ds(pl.multiple_of(idx[r] * 16, 16), 16)
        a, ai = part_of(dy, dx)
        b, bi = part_of(dx, dy)
        for f in range(4):
            left[a][ai, 16 * f : 16 * f + 16, :768] = shares[f, rows]
            right[b][bi, 16 * f : 16 * f + 16, :768] = shares[f + 4, rows]
        left[a][ai, :, 768:] = out_shares[idx[r], :64]
        right[b][bi, :, 768:] = out_shares[idx[r], 64:]


def projection_grads(place, idx, dq_raw, own, other, k_raw, q_part, k_gain, cosine, sine, h1, w, aux, out_shares, event):
    shapes = [((n, 64, 1280), bf16) for n in [4, 4, 2, 2, 4] * 2]
    shapes += [((1024, 640), bf16), ((MODEL_WIDTH, 128), f32), ((1, HEAD_SIZE), f32)]
    outs = pl.pallas_call(
        grads_kernel,
        out_shape=[jax.ShapeDtypeStruct(*s) for s in shapes],
        in_specs=[SM, SM] + [VM] * 12 + [ANY],
        out_specs=[VM] * len(shapes),
        scratch_shapes=[pltpu.VMEM((8, 256, 768), bf16)],
        compiler_params=pltpu.CompilerParams(vmem_limit_bytes=52 * MIB),
        cost_estimate=pl.CostEstimate(flops=3 << 30, bytes_accessed=16 << 20, transcendentals=0),
        name="projection_grads",
    )(place, idx, dq_raw, own, other, k_raw, q_part, k_gain, cosine, sine, h1, w, aux, out_shares, event)
    return outs[:5], outs[5:10], *outs[10:]


def input_grad_kernel(place, dqkv, w, _, keep, send, w_own):
    z, c = place[0], place[1]
    w_own[:, :512] = w[:, :512]
    w_own[:, 512:] = jnp.where(c == 0, w[:, 512:640], w[:, 640:])

    @pl.loop(0, 4)
    def _(i):
        rows = pl.ds(pl.multiple_of(i * 256, 256), 256)
        part = mm(dqkv[rows], w_own[...], NT).astype(bf16)
        dz = lax.rem(i - z + 4, 4)
        first, second = part[:128], part[128:]
        keep[dz] = jnp.where(c == 0, first, second)
        send[dz] = jnp.where(c == 0, second, first)


def input_grad(place, dqkv, w, event):
    return pl.pallas_call(
        input_grad_kernel,
        out_shape=[jax.ShapeDtypeStruct((4, 128, MODEL_WIDTH), bf16)] * 2,
        in_specs=[SM, VM, VM, ANY],
        out_specs=[VM] * 2,
        scratch_shapes=[pltpu.VMEM((MODEL_WIDTH, 640), bf16)],
        compiler_params=pltpu.CompilerParams(vmem_limit_bytes=40 * MIB),
        cost_estimate=pl.CostEstimate(flops=3 << 30, bytes_accessed=8 << 20, transcendentals=0),
        name="input_grad",
    )(place, dqkv, w, event)


def part_of(outer, inner):
    return {0: (0, inner), 1: (1, inner), 2: (2 + inner // 2, inner % 2), 3: (4, inner)}[outer]


def place_kernel(source, *refs):
    query, key, value, aux, gains, out, parts, sems = refs[-8:]
    copies = [pltpu.make_async_copy(source.at[r], parts.at[r], sems.at[r]) for r in range(16)]
    for copy in copies:
        copy.start()
    for r in range(16):
        copies[r].wait()
        rows = slice(16 * r, 16 * r + 16)
        total = jnp.zeros((16, 128), f32)
        for f in range(8):
            block = parts[r, f].astype(f32)
            query[rows, 512 * f : 512 * f + 512] = block[:, :512]
            to = key if f % 2 == 0 else value
            to[rows, 128 * (f // 2) : 128 * (f // 2) + 128] = block[:, 512:640]
            total = total + block[:, 640:768]
            gains[f] = block[:, 640:768] if r == 0 else gains[f] + block[:, 640:768]
            first = 32 * r + 16 * (f % 2)
            out[first : first + 16, 512 * (f // 2) : 512 * (f // 2) + 512] = block[:, 768:]
        aux[rows] = total


def place_rows(parts, *events):
    shapes = [(256, 4096), (256, 512), (256, 512), (256, 128), (8, 16, 128), (512, MODEL_WIDTH)]
    return pl.pallas_call(
        place_kernel,
        out_shape=[jax.ShapeDtypeStruct(s, f32) for s in shapes],
        in_specs=[ANY] * (1 + len(events)),
        out_specs=[VM] * 6,
        scratch_shapes=[pltpu.VMEM((16, 8, 16, 1280), bf16), pltpu.SemaphoreType.DMA((16,))],
        compiler_params=pltpu.CompilerParams(vmem_limit_bytes=60 * MIB),
        cost_estimate=pl.CostEstimate(flops=0, bytes_accessed=16 << 20, transcendentals=0),
        name="place_rows",
    )(parts, *events)


def nothing(*refs):
    pass


def after(values, *events):
    n = len(values)
    return pl.pallas_call(
        nothing,
        out_shape=[jax.ShapeDtypeStruct(v.shape, v.dtype) for v in values],
        in_specs=[ANY] * (n + len(events)),
        out_specs=[ANY] * n,
        input_output_aliases={i: i for i in range(n)},
        cost_estimate=pl.CostEstimate(flops=0, bytes_accessed=0, transcendentals=0),
        name="after",
    )(*values, *events)


def local(
    layer_input, routes, cotangent, attn_gain, query_gain, key_gain, mlp_gain,
    w_query, key_weight, value_weight, w_out, w_router, w_gate, w_up, w_down,
):
    core = lax.axis_index(C)
    py, px = lax.axis_index(Y), lax.axis_index(X)
    zc = jnp.stack([lax.axis_index(Z), core, py, px]).astype(jnp.int32)
    ahead = jnp.arange(16, dtype=jnp.int32)
    idx = (py + ahead // 4) % 4 * 4 + (px + ahead % 4) % 4
    residual = layer_input[0].astype(f32)
    dy_low = cotangent[0]
    upstream = dy_low.astype(f32)
    scale_one = inv_rms(residual)
    normed_one = residual * scale_one
    h1 = (normed_one * attn_gain).astype(bf16)
    beside = jnp.pad(w_router.reshape(128, 64), ((0, 0), (0, 64)))
    h1 = jnp.concatenate([h1, beside], axis=1)
    seq = 1024
    cosine, sine = rope_tables(jnp.arange(seq).astype(f32))
    sign = jnp.where(jnp.arange(HEAD_SIZE) < HEAD_SIZE // 2, -1.0, 1.0).astype(f32)
    signed = sine * sign
    ids = jnp.arange(EXPERTS, dtype=jnp.int32)
    chosen = jnp.any(routes[0][:, :, None] == ids, axis=1)
    before = jnp.tril(jnp.ones((128, 128), bf16), -1)
    rank = dot(before, chosen.astype(bf16)).astype(jnp.int32)
    slot = jnp.where(chosen, rank, -1).T.reshape(16, 2, 128).transpose(1, 0, 2)
    picks = (slot[:, :, None, :] == jnp.arange(CAP)[:, None]).reshape(2, 640, 128)

    def sent(e, v):
        packed = dot(picks[e].astype(bf16), v).astype(bf16)
        return packed.reshape(16, CAP, MODEL_WIDTH)

    def exchanged(v):
        return lax.all_to_all(v, EXPERT, 0, 0, tiled=True)

    dy_all = lax.all_gather(dy_low, EXPERT, axis=0, tiled=False)
    tokens = jnp.arange(128, dtype=jnp.int32)
    slot_token = jnp.max(jnp.where(picks, tokens, -1), axis=-1).reshape(2, 16, CAP)
    in_own = jnp.concatenate([w_gate, w_up])
    rows = w_query.shape[0]

    def per_head(w, n):
        return jnp.repeat(w.reshape(rows, 4, 128), 2, axis=1) if n == 2 else w.reshape(rows, 8, 512)

    blocks = jnp.concatenate([per_head(w_query, 1), per_head(key_weight, 2), per_head(value_weight, 2)], axis=2)
    blocks = blocks.transpose(1, 0, 2).reshape(4, 2, rows, 768)
    blocks = jnp.where(core == 0, blocks, blocks[:, ::-1])
    place_z = lax.axis_index(Z)

    def meant_for(ahead):
        return lax.dynamic_index_in_dim(blocks, (place_z + ahead) % 4, 0, keepdims=False)

    w_parts = [meant_for(0)] + [shift(meant_for(d), Z, d) for d in range(1, 4)]
    h1_pieces = gather_fsdp(h1, lambda up, down: after([up, down], cosine, signed, in_own))
    w_parts[1:] = after(w_parts[1:], *[h1_pieces[k][0] for k in (1, 4, 5)])
    from_other = shift(jnp.stack([v[1] for v in w_parts]), C, 1)
    in_own, down_own = after(
        [in_own, w_down], *w_parts[1:], h1_pieces[4][0], h1_pieces[5][0]
    )
    in_all = lax.all_gather(in_own, FSDP, axis=1, tiled=True)
    down_all = lax.all_gather(down_own, FSDP, axis=1, tiled=True)
    w, h1_all, q_raw, k_raw, v_b, q_b, k_b, a_b, lse, keep, send = attention_forward(
        h1_pieces, [*w_parts, from_other], zc, w_out, query_gain[None], key_gain[None], cosine, signed
    )
    router = h1_all[:, MODEL_WIDTH : MODEL_WIDTH + 64].reshape(MODEL_WIDTH, EXPERTS)
    attn = scatter_fsdp(keep, send)
    resid_two = residual + attn
    scale_two = inv_rms(resid_two)
    normed_two = resid_two * scale_two
    h2 = (normed_two * mlp_gain).astype(bf16)
    beside = jnp.pad(jnp.stack([slot_token[0], slot_token[1]], axis=-1).astype(bf16), ((0, 0), (0, 0), (0, 126)))
    xs_first = exchanged(jnp.concatenate([sent(0, h2), beside], axis=-1))
    slot_token = xs_first[:, :, MODEL_WIDTH : MODEL_WIDTH + 2].astype(jnp.int32)
    taken = (slot_token[..., None] == tokens).astype(bf16)
    dys = [es("sct,std->scd", taken[:, :, e], dy_all).astype(bf16).reshape(640, MODEL_WIDTH) for e in range(2)]
    logits = jnp.where(chosen, dot(h2, router), -1e30)
    powers = jnp.where(chosen, jnp.exp(logits - jnp.max(logits, axis=-1, keepdims=True)), 0.0)
    gates = powers / jnp.sum(powers, axis=-1, keepdims=True)
    gates_slot = gates.T.reshape(16, 2, 128).transpose(1, 0, 2)
    weighted = jnp.where(picks.reshape(2, 16, CAP, 128), gates_slot[:, :, None, :], 0.0)
    slot_gate = jnp.sum(weighted, axis=-1)
    high = slot_gate.astype(bf16)
    low = (slot_gate - high.astype(f32)).astype(bf16)
    beside = jnp.stack([high[0], low[0], high[1], low[1]], axis=-1)
    beside = jnp.pad(beside, ((0, 0), (0, 0), (0, 124)))
    second = jnp.concatenate([sent(1, h2), beside], axis=-1)
    (second,) = after([second], xs_first)
    xs_second = exchanged(second)
    xs = [v.reshape(640, MODEL_WIDTH + 128) for v in (xs_first, xs_second)]
    back_first, *kept_first = expert_rows(0, xs[0], dys[0], in_all, down_all)
    wide = (16, CAP, MODEL_WIDTH + 128)
    (back_first,) = after([back_first.reshape(wide)], xs_second)
    from_first = exchanged(back_first)
    back_second, *kept_second = expert_rows(1, xs[1], dys[1], in_all, down_all)
    (back_second,) = after([back_second.reshape(wide)], from_first)
    from_second = exchanged(back_second)
    got = xs[1][:, MODEL_WIDTH : MODEL_WIDTH + 4].astype(f32)
    slot_gate = [jnp.broadcast_to(got[:, 2 * e : 2 * e + 1] + got[:, 2 * e + 1 : 2 * e + 2], (640, 128)) for e in range(2)]
    weighted = weighted.reshape(2, 640, 128).astype(bf16)

    def combined(parts):
        return sum(es("rt,rd->td", weighted[e], parts[e].reshape(640, -1)[:, :MODEL_WIDTH]) for e in range(2))

    kept = [
        (xs[e], dys[e], *kept, slot_gate[e]) for e, kept in enumerate((kept_first, kept_second))
    ]
    grad_gate, grad_up, grad_down, *ys = weight_grads([*kept[0], *kept[1]], down_all, from_first)
    ys = jnp.concatenate([v.reshape(16, CAP, MODEL_WIDTH) for v in ys], axis=1)
    (from_second,) = after([from_second], ys)
    backs = [from_first, from_second]
    dh_sum = combined(backs)
    dgate = [v.reshape(640, -1)[:, MODEL_WIDTH : MODEL_WIDTH + 2].astype(f32).sum(axis=1) for v in backs]
    dgate = jnp.stack(dgate).reshape(2, 16, CAP, 1)
    dgate = jnp.sum(jnp.where(picks.reshape(2, 16, CAP, 128), dgate, 0.0), axis=2)
    dgate = dgate.transpose(2, 1, 0).reshape(128, EXPERTS)
    expert_grads = after([grad_gate, grad_up, grad_down], from_second)
    dl = (gates * (dgate - jnp.sum(gates * dgate, axis=-1, keepdims=True))).astype(bf16)
    dh2 = es("te,de->td", dl, router) + dh_sum
    dx2 = upstream + norm_back(dh2 * mlp_gain, normed_two, scale_two)
    da = dx2.astype(bf16)
    da_pieces = gather_fsdp(da)
    (ys,) = after([ys], from_second)
    ys = exchanged(ys).reshape(1280, MODEL_WIDTH)
    by_owner = weighted.reshape(2, 16, CAP, 128).transpose(1, 0, 2, 3).reshape(1280, 128)
    output = (resid_two + es("rt,rd->td", by_owner, ys)).astype(bf16)
    aux = jnp.pad(es("td,te->de", h2, dl), ((0, 0), (0, 128 - EXPERTS)))
    grad_mlp_gain = jnp.sum(dh2 * normed_two, axis=0)
    def scattered(v):
        return lax.psum_scatter(v, FSDP, scatter_dimension=1, tiled=True)

    grad_gate, grad_up, grad_down = (scattered(v) for v in expert_grads)
    dob, out_shares = out_back(da_pieces, zc, w_out, a_b)
    dq_raw, dkv, q_part = attention_backward(
        dob, a_b, q_b, k_b, v_b, lse, q_raw, query_gain[None], cosine, signed
    )
    left, right, dqkv, along, k_part = projection_grads(
        zc, idx, dq_raw, dkv, shift(dkv, C, 1), k_raw, q_part, key_gain[None], cosine, signed, h1_all, w, aux,
        out_shares, ys,
    )
    left, right, first = scatter_plane(left, right)
    keep, send = input_grad(zc, dqkv, w, first)
    dh1 = scatter_fsdp(keep, send)
    gains = jnp.concatenate([along[:, 0], grad_mlp_gain, q_part[0], k_part[0]]).reshape(34, 128)
    (gains,) = after([gains], first)
    gains = gains + shift(gains, C, 1)
    gains = (gains + shift(gains, Z, 2)) + (shift(gains, Z, 1) + shift(gains, Z, 3))
    high = gains.astype(bf16)
    gains = jnp.stack([high, (gains - high.astype(f32)).astype(bf16)]).reshape(8, 16, 68)
    gains = jnp.pad(gains, ((0, 0), (0, 0), (0, 28)))
    shares = jnp.concatenate([left, right]).astype(bf16)
    parted = lax.all_to_all(shares[:, :768].reshape(8, 16, 768), FSDP, 0, 0, tiled=True)
    expert_grads = [v.astype(f32) for v in (grad_gate, grad_up, grad_down)]
    parted = jnp.concatenate([parted[:, :, : 640 + EXPERTS], gains, shares[:, 768:].reshape(8, 16, 512)], axis=2)
    grad_input = dx2 + norm_back(dh1 * attn_gain, normed_one, scale_one)
    grad_input = grad_input.astype(bf16)
    parted = lax.all_gather(parted, EXPERT, axis=0, tiled=False)
    grad_query, grad_key, grad_value, aux, gains, grad_out = place_rows(parted, grad_input, *expert_grads)
    gains = (gains[:4] + gains[4:])[:, :, EXPERTS : EXPERTS + 68].reshape(-1)
    return (
        output[None],
        grad_input[None],
        gains[:MODEL_WIDTH] / attn_gain,
        gains[2 * MODEL_WIDTH : 2 * MODEL_WIDTH + HEAD_SIZE],
        gains[2 * MODEL_WIDTH + HEAD_SIZE :],
        gains[MODEL_WIDTH : 2 * MODEL_WIDTH],
        grad_query,
        grad_key,
        grad_value,
        grad_out,
        aux[:, :EXPERTS],
        *expert_grads,
    )


def solution(mesh):
    torus = Mesh(mesh.devices.reshape(4, 2, 4, 4), ALL)
    tokens, rows, experts = P(EXPERT, FSDP, None), P(FSDP, None), P(EXPERT, FSDP, None)
    return jax.shard_map(
        local,
        mesh=torus,
        in_specs=(tokens,) * 3 + (P(),) * 4 + (rows,) * 5 + (experts,) * 3,
        out_specs=(tokens,) * 2 + (P(),) * 4 + (rows,) * 5 + (experts,) * 3,
        check_vma=False,
    )
```
